512 devices in a mesh: leaf: 128 (over y, z, core), gy: 4 (over x).
Axes of the slice: x: 4, y: 8, z: 8, core: 2. Of those that a mesh axis runs over, the one named last changes fastest.
Arguments:
- field_old: float32 [8, 64, 40960], P('gy', None, 'leaf'), may hold values from -1.2 to 1.2
- coef_old: float32 [64, 40960], P(None, 'leaf'), may hold values from 0.5 to 4
- owner: int32 [40960], P('leaf'), may hold values from 0 to 127, as said below
- counts: int32 [128], P('leaf'), may hold values from 192 to 320, as said below
- pattern: int32 [6, 32768], P(None, 'leaf'), may hold values from -1 to 543, as said below
Outputs:
- extension: float32 [8, 64, 32768], P('gy', None, 'leaf')
The draws below stay inside these ranges and needn't reach their ends.
Inputs may be any that keep to these rules, and one draw needn't show every extreme that they name: `owner`: only live slots matter. The live slots of device d name, in slot order, first device d - 1, then d, then d + 1; at most 32 name d - 1 and at most 32 name d + 1, some device hands exactly 32 each way, and every device receives exactly 256 live bricks. Live slots are the first counts[d] slots of device d. `pattern`: -1 means no neighbour across that face; otherwise the index into the bricks of devices d - 1, d and d + 1 after the rebalance, laid end to end. A neighbour on device d - 1 is one of its last 32 bricks, one on device d + 1 one of its first 32 bricks.
All inputs are finite; a program needn't handle non-finite values.
Results may differ from the reference program's by a relative error of at most 0.00002.
Values sent between devices are 32-bit elements; how exact they have to be, the bound alone decides.
No kernel may reach another device: no remote copies, remote signals or barrier semaphores. Data moves between devices by JAX's collectives and lax.ppermute only.
A program may use at most 64 MiB of HBM per device.

```python
import math
import jax
import jax.numpy as jnp
from jax import lax

BRICKS_DEV = 256
SPILL = 32
Y = 8
SWEEPS = 2
OLD_SLOTS = 320
SLOTS = 40960
BAND = 32
N_LEAF = 128


def flow_table(key):
    key_size, key_sign = jax.random.split(key)
    half_spill = SPILL // 2
    magnitude = half_spill + jax.random.randint(key_size, (N_LEAF + 1,), 0, half_spill + 1)
    sign_flip = jax.random.randint(key_sign, (N_LEAF + 1,), 0, 2) * 2 - 1
    raw_drift = magnitude * sign_flip
    positions = jnp.arange(N_LEAF + 1)
    drift_now = jnp.where(positions == 2, -SPILL, raw_drift)
    drift_now = jnp.where(positions == 3, SPILL, drift_now)
    drift_now = jnp.where((positions == 0) | (positions == N_LEAF), 0, drift_now)
    forward = jnp.maximum(drift_now, 0)
    backward = jnp.maximum(-drift_now, 0)
    forward = jnp.where(positions == 1, SPILL, forward)
    backward = jnp.where(positions == 1, SPILL, backward)
    return (forward.astype(jnp.int32), backward.astype(jnp.int32))


def draw_counts(key, part):
    forward, backward = flow_table(key)
    return (BRICKS_DEV - forward[:-1] - backward[1:] + backward[:-1] + forward[1:]).astype(jnp.int32)


def draw_owner(key, part):
    forward, backward = flow_table(key)
    key = jax.random.fold_in(key, 2)
    old_slots = BRICKS_DEV + 2 * SPILL
    slot_ids = jnp.arange(N_LEAF * old_slots, dtype=jnp.int32)
    device_ids = slot_ids // old_slots
    local_ids = slot_ids % old_slots
    live_count = BRICKS_DEV - forward[device_ids] - backward[device_ids + 1] + backward[device_ids] + forward[device_ids + 1]
    live_owner = jnp.where(local_ids < backward[device_ids], device_ids - 1, jnp.where(local_ids < live_count - forward[device_ids + 1], device_ids, device_ids + 1))
    lowest = jnp.maximum(device_ids - 1, 0)
    highest = jnp.minimum(device_ids + 1, N_LEAF - 1)
    spare_owner = lowest + jax.random.randint(key, slot_ids.shape, 0, 3) % (highest - lowest + 1)
    return jnp.where(local_ids < live_count, live_owner, spare_owner).astype(jnp.int32)


def draw_pattern(key, part):
    key = jax.random.fold_in(key, 3)
    key_kind, key_own, key_band = jax.random.split(key, 3)
    shape = (6, N_LEAF * BRICKS_DEV)
    kind = jax.random.randint(key_kind, shape, 0, 8)
    own_pick = jax.random.randint(key_own, shape, BRICKS_DEV, 2 * BRICKS_DEV)
    band_pick = jax.random.randint(key_band, shape, 0, BAND)
    result = jnp.where(kind == 0, -1, own_pick)
    result = jnp.where(kind == 1, BRICKS_DEV - BAND + band_pick, result)
    result = jnp.where(kind == 2, 2 * BRICKS_DEV + band_pick, result)
    starts = jnp.arange(N_LEAF, dtype=jnp.int32) * BRICKS_DEV
    result = result.at[0, starts].set(BRICKS_DEV - 1)
    result = result.at[1, starts + 1].set(2 * BRICKS_DEV + BAND - 1)
    result = result.at[2, starts].set(-1)
    return result.astype(jnp.int32)


def block_levels(rng, dims, pieces, least, largest):
    loudness = 1.0
    for dim, parts in pieces:
        draws = jax.random.uniform(jax.random.fold_in(jax.random.fold_in(rng, 6), dim), (parts,), jnp.float32, least / len(pieces), largest / len(pieces))
        loudness = loudness * jnp.repeat(jnp.exp(draws), dims[dim] // parts).reshape((-1,) + (1,) * (len(dims) - 1 - dim))
    return loudness


def setup_inputs(seed: int = 0) -> dict:
    arg_keys = jax.random.split(jax.random.key(seed), 6)
    return {
        "field_old": jnp.clip(jax.random.uniform(arg_keys[0], (Y, 64, SLOTS), jnp.float32, -1.2, 1.2) * block_levels(arg_keys[0], (Y, 64, SLOTS), ((0, 4), (2, 128)), -0.4, 0.0), -1.2, 1.2),
        "coef_old": jnp.clip(jnp.exp(math.log(4.0) - 2.0794415 * jax.random.uniform(arg_keys[1], (64, SLOTS), jnp.float32) ** block_levels(arg_keys[1], (64, SLOTS), ((1, 128),), -0.2, 0.2)), 0.5, 4.0),
        "owner": draw_owner(jax.random.fold_in(arg_keys[5], 71), 0),
        "counts": draw_counts(jax.random.fold_in(arg_keys[5], 71), 0),
        "pattern": draw_pattern(jax.random.fold_in(arg_keys[5], 71), 0),
    }


EXPONENT = 0.5
HEIGHT = 8.0
OMEGA = 0.8


def layer_weights(levels):
    y_here = HEIGHT * (levels / float(Y)) ** 2
    y_next = HEIGHT * ((levels + 1.0) / float(Y)) ** 2
    y_prev = HEIGHT * ((levels - 1.0) / float(Y)) ** 2
    step_up = y_next - y_here
    step_down = y_here - y_prev
    up_weight = ((y_here + y_next) * 0.5) ** EXPONENT
    down_weight = ((y_here + y_prev) * 0.5) ** EXPONENT
    has_lower = (levels > 0.5).astype(levels.dtype)
    up_link = up_weight / step_up
    down_link = has_lower * down_weight / step_down
    planar = 0.5 * (up_weight * step_up + has_lower * down_weight * step_down)
    surface = (levels < 0.5).astype(levels.dtype)
    return (planar.reshape(-1, 1, 1), down_link.reshape(-1, 1, 1), up_link.reshape(-1, 1, 1), surface.reshape(-1, 1, 1))


def far_faces(source, pattern_rows, valid_rows):
    picked = []
    for direction in range(6):
        axis_no = 1 + direction // 2
        layer_no = 3 if direction % 2 == 0 else 0
        face_cells = lax.index_in_dim(source, layer_no, axis_no, keepdims=False)
        gathered = jnp.take(face_cells, pattern_rows[direction], axis=3) * valid_rows[direction]
        picked.append(gathered)
    return picked


def shifted_sum(cube_now, face_list):
    running_sum = jnp.concatenate([face_list[0][:, None], cube_now[:, :3]], axis=1)
    running_sum = running_sum + jnp.concatenate([cube_now[:, 1:], face_list[1][:, None]], axis=1)
    running_sum = running_sum + jnp.concatenate([face_list[2][:, :, None], cube_now[:, :, :3]], axis=2)
    running_sum = running_sum + jnp.concatenate([cube_now[:, :, 1:], face_list[3][:, :, None]], axis=2)
    running_sum = running_sum + jnp.concatenate([face_list[4][:, :, :, None], cube_now[:, :, :, :3]], axis=3)
    running_sum = running_sum + jnp.concatenate([cube_now[:, :, :, 1:], face_list[5][:, :, :, None]], axis=3)
    return running_sum


def relax(current, beneath, overhead, neighbour_sum, coef_cells, source_term, weights):
    planar, down_link, up_link, surface = weights
    applied = planar * coef_cells * (6.0 * current - neighbour_sum) + (down_link + up_link + surface) * current - down_link * beneath - up_link * overhead
    diagonal = 6.0 * planar * coef_cells + down_link + up_link + surface
    return current + OMEGA * (source_term - applied) / diagonal


def reference(field_old, coef_old, owner, counts, pattern):
    slots_all = owner.shape[0]
    total_new = N_LEAF * BRICKS_DEV
    slot_ids = jnp.arange(slots_all, dtype=jnp.int32)
    is_live = (slot_ids % OLD_SLOTS) < jnp.repeat(counts, OLD_SLOTS, total_repeat_length=slots_all)
    onehot = ((owner[:, None] == jnp.arange(N_LEAF, dtype=jnp.int32)[None, :]) & is_live[:, None]).astype(jnp.int32)
    running = jnp.cumsum(onehot, axis=0) - onehot
    position = jnp.sum(running * onehot, axis=1).astype(jnp.int32)
    target = jnp.where(is_live & (position < BRICKS_DEV), owner * BRICKS_DEV + position, total_new).astype(jnp.int32)
    field_new = jnp.zeros((Y, 64, total_new), jnp.float32).at[:, :, target].set(field_old, mode="drop")
    coef_new = jnp.zeros((64, total_new), jnp.float32).at[:, target].set(coef_old, mode="drop")
    levels = jnp.arange(Y).astype(jnp.float32)
    weights = layer_weights(levels)
    brick_ids = jnp.arange(total_new, dtype=jnp.int32)
    window_base = ((brick_ids // BRICKS_DEV - 1) * BRICKS_DEV).astype(jnp.int32)
    global_rows = window_base[None, :] + pattern
    is_valid = (pattern >= 0) & (global_rows >= 0) & (global_rows < total_new)
    clipped = jnp.clip(global_rows, 0, total_new - 1).astype(jnp.int32)
    valid_rows = is_valid.astype(jnp.float32)
    phase_field = field_new[0:1]
    source_term = weights[3] * (2.0 * phase_field - phase_field * phase_field * phase_field)
    current = field_new
    zero_layer = jnp.zeros((1, 64, total_new), jnp.float32)
    for sweep_no in range(SWEEPS):
        cube_now = current.reshape(Y, 4, 4, 4, total_new)
        face_list = far_faces(cube_now, clipped, valid_rows)
        neighbour_sum = shifted_sum(cube_now, face_list).reshape(Y, 64, total_new)
        beneath = jnp.concatenate([zero_layer, current[:-1]], axis=0)
        overhead = jnp.concatenate([current[1:], zero_layer], axis=0)
        current = relax(current, beneath, overhead, neighbour_sum, coef_new, source_term, weights)
    return current
```

```python
import functools

import jax
import jax.numpy as jnp
import numpy as np
from jax import lax
from jax.experimental import pallas as pl
from jax.experimental.pallas import tpu as pltpu
from jax.sharding import PartitionSpec as P

BRICKS_DEV = 256
SPILL = 32
Y = 8
OLD_SLOTS = 320
EXPONENT = 0.5
HEIGHT = 8.0
OMEGA = 0.8

F32 = jnp.float32
LANES = 128
TILES = 8
GATHER = lax.GatherDimensionNumbers(
    offset_dims=(),
    collapsed_slice_dims=(1,),
    start_index_map=(1,),
    operand_batching_dims=(0,),
    start_indices_batching_dims=(0,),
)


def weight_table(layers):
    rows = []
    for level in range(-1, Y + 1):
        if not 0 <= level < Y:
            rows.append((0.0, 0.0, 0.0, 0.0, 1.0))
            continue
        y_here = HEIGHT * (level / Y) ** 2
        y_next = HEIGHT * ((level + 1) / Y) ** 2
        y_prev = HEIGHT * ((level - 1) / Y) ** 2
        step_up, step_down = y_next - y_here, y_here - y_prev
        up_weight = ((y_here + y_next) * 0.5) ** EXPONENT
        down_weight = ((y_here + y_prev) * 0.5) ** EXPONENT
        has_lower = float(level > 0)
        up_link = up_weight / step_up
        down_link = has_lower * down_weight / step_down
        planar = 0.5 * (up_weight * step_up + has_lower * down_weight * step_down)
        surface = float(level == 0)
        rows.append((planar, down_link, up_link, surface, down_link + up_link + surface))
    return np.asarray(rows, np.float32)


def weights_at(table, group, layers, offset):
    groups = Y // layers
    out = []
    for column in range(5):
        value = F32(table[offset + 1, column])
        for g in range(1, groups):
            value = jnp.where(group == g, F32(table[g * layers + offset + 1, column]), value)
        out.append(value)
    return out


def lanes():
    return lax.broadcasted_iota(jnp.int32, (8, LANES), 1)


def rows():
    return lax.broadcasted_iota(jnp.int32, (8, LANES), 0)


def spin(tile, shift):
    if isinstance(shift, int):
        return pltpu.roll(tile, shift % LANES, 1) if shift % LANES else tile
    return pltpu.roll(tile, jnp.bitwise_and(shift, LANES - 1), 1)


def pick(tile, index):
    return lax.gather(
        tile,
        index[:, :, None],
        GATHER,
        (1, 1),
        mode=lax.GatherScatterMode.PROMISE_IN_BOUNDS,
    )


def spill_counts(owner_ref, live_count, device):
    to_prev = jnp.int32(0)
    to_next = jnp.int32(0)
    for step in (32, 16, 8, 4, 2, 1):
        near = jnp.minimum(to_prev + step, SPILL)
        hit = (to_prev + step <= SPILL) & (owner_ref[near - 1] < device)
        to_prev = jnp.where(hit, to_prev + step, to_prev)
        near = jnp.minimum(to_next + step, SPILL)
        hit = (to_next + step <= SPILL) & (owner_ref[live_count - near] > device)
        to_next = jnp.where(hit, to_next + step, to_next)
    return to_prev, to_next


def old_tile(ref, lead, t, c):
    at = (lead, pl.ds(8 * t, 8)) if lead is not None else (pl.ds(8 * t, 8),)
    if c < 2:
        return ref[at + (pl.ds(LANES * c, LANES),)]
    half = ref[at + (pl.ds(2 * LANES, OLD_SLOTS - 2 * LANES),)]
    return jnp.concatenate([half, jnp.zeros((8, 3 * LANES - OLD_SLOTS), F32)], axis=1)


def face_indices(pattern_rows):
    sub = rows()
    kinds = (
        pattern_rows[0],
        pattern_rows[1],
        jnp.where(sub < 4, pattern_rows[3], pattern_rows[2]),
        jnp.where((sub & 3) == 3, pattern_rows[4], pattern_rows[5]),
    )
    out = []
    for w in kinds:
        source = w >> 7
        own = (source == 2) | (source == 3)
        beside = jnp.where(w >= 2 * BRICKS_DEV, w - (2 * BRICKS_DEV - SPILL), w - (BRICKS_DEV - SPILL))
        lane = jnp.where(own, w & (LANES - 1), jnp.where(w >= BRICKS_DEV - SPILL, beside, LANES - 1))
        out.append((lane, source == 2, source == 3))
    return out


def face(kind, tiles):
    lane, first, second = kind
    return jnp.where(first, pick(tiles[0], lane), jnp.where(second, pick(tiles[1], lane), pick(tiles[2], lane)))


class Sources:
    def __init__(self, read):
        sub = rows()
        self.tile = [[read(c, t) for t in range(TILES)] for c in range(3)]
        self.turned = [[pltpu.roll(v, 4, 0) for v in column] for column in self.tile]
        self.y_edge = [
            [jnp.where(sub < 4, column[2 * i], column[2 * i + 1]) for i in range(4)]
            for column in self.tile
        ]


def neighbour_sum(src, here, turned, kinds):
    sub = rows()
    low, k = sub < 4, sub & 3
    x_low, x_high, y_both, z_both = kinds
    total = []
    for t in range(TILES):
        if t < 2:
            below = face(x_low, [src.tile[c][6 + t] for c in range(3)])
        else:
            below = here[t - 2]
        if t >= 6:
            above = face(x_high, [src.tile[c][t - 6] for c in range(3)])
        else:
            above = here[t + 2]
        total.append(below + above)
    for i in range(4):
        edge = pltpu.roll(face(y_both, [src.y_edge[c][i] for c in range(3)]), 4, 0)
        first, second = turned[2 * i], turned[2 * i + 1]
        middle = jnp.where(low, first, second)
        total[2 * i] += jnp.where(low, edge, first) + middle
        total[2 * i + 1] += jnp.where(low, second, edge) + middle
    for t in range(TILES):
        edge = face(z_both, [src.turned[c][t] for c in range(3)])
        total[t] += pltpu.roll(jnp.where(k == 3, edge, here[t]), 1, 0)
        total[t] += pltpu.roll(jnp.where(k == 0, edge, here[t]), 7, 0)
    return total


def is_even(axis):
    return (lax.axis_index(axis) & 1) == 0


def send_kernel(
    field_hbm, coef_hbm, owner_hbm, counts_ref,
    near_ref, far_ref, field_ref, coef_ref,
    owner_ref, sems,
):
    pairs = ((owner_hbm, owner_ref), (field_hbm, field_ref), (coef_hbm, coef_ref))
    copies = [pltpu.make_async_copy(a, b, sems.at[i]) for i, (a, b) in enumerate(pairs)]
    for copy in copies:
        copy.start()
    lane, sub = lanes(), rows()
    even = is_even("leaf")
    copies[0].wait()
    live = counts_ref[0]
    to_prev, to_next = spill_counts(owner_ref, live, lax.axis_index("leaf"))
    kept = jnp.where(sub == 1, live, jnp.where(sub == 2, to_prev, to_next)).astype(F32)
    prev_count = jnp.where(sub == 0, to_prev.astype(F32), kept)
    next_count = jnp.where(sub == 0, to_next.astype(F32), kept)
    near_ref[pl.ds(96, 8), :] = jnp.where(even, next_count, prev_count)
    far_ref[pl.ds(96, 8), :] = jnp.where(even, prev_count, next_count)
    for a in range(3):
        ref, lead = (field_ref, a) if a < 2 else (coef_ref, None)
        if a == 0:
            copies[1].wait()
        if a == 2:
            copies[2].wait()
        for r in range(4):
            at = pl.ds(32 * a + 8 * r, 8)
            front = old_tile(ref, lead, r, 0)
            back = old_tile(ref, lead, r + 4, 0)
            prev = jnp.where(lane < 64, front, pltpu.roll(back, 64, 1))
            early = lane >= live - 192
            front = jnp.where(early, old_tile(ref, lead, r, 1), old_tile(ref, lead, r, 2))
            back = jnp.where(early, old_tile(ref, lead, r + 4, 1), old_tile(ref, lead, r + 4, 2))
            next = jnp.where(lane < 64, spin(front, 64 - live), spin(back, 128 - live))
            near_ref[at, :] = jnp.where(even, next, prev)
            far_ref[at, :] = jnp.where(even, prev, next)


def place_kernel(
    field_ref, coef_ref, pattern_ref, kept_ref, near_ref, far_ref,
    pack_ref, coef_out, band_out, sum_near, sum_far,
):
    lane = lanes()
    even = is_even("leaf")
    live, to_prev, to_next = (kept_ref[96 + i, 0].astype(jnp.int32) for i in (1, 2, 3))
    from_near, from_far = near_ref[96, 0], far_ref[96, 0]
    from_prev = jnp.where(even, from_far, from_near).astype(jnp.int32)
    from_next = jnp.where(even, from_near, from_far).astype(jnp.int32)
    stay = live - to_prev - to_next
    drift = to_prev - from_prev
    tail = from_prev + stay - LANES
    for a in range(3):
        ref, lead = (field_ref, a) if a < 2 else (coef_ref, None)
        for t in range(TILES):
            h = 64 * (t // 4)
            at = pl.ds(32 * a + 8 * (t % 4), 8)
            near, far = near_ref[at, :], far_ref[at, :]
            before, after = jnp.where(even, far, near), jnp.where(even, near, far)
            x0, x1, x2 = (old_tile(ref, lead, t, c) for c in range(3))
            r0, r1, r2 = spin(x0, -drift), spin(x1, -drift), spin(x2, -drift)
            own0 = jnp.where(lane < LANES - drift, r0, r1)
            own1 = jnp.where(lane < -drift, r0, jnp.where(lane < LANES - drift, r1, r2))
            own0 = jnp.where(lane < from_prev, spin(before, from_prev - 64 - h), own0)
            own1 = jnp.where(lane >= tail, spin(after, tail - h), own1)
            low = jnp.where(
                lane < SPILL - to_prev,
                spin(before, from_prev - to_prev - SPILL - h),
                spin(x0, SPILL - to_prev),
            )
            end = jnp.where(lane >= live - to_next - LANES, x1, x2)
            high = jnp.where(
                lane < SPILL + to_next,
                spin(end, SPILL + to_next - live),
                spin(after, SPILL + to_next - from_next - h),
            )
            band = jnp.where(lane < SPILL, low, jnp.where(lane < 2 * SPILL, high, 0.0))
            if a < 2:
                pack_ref[pl.ds(128 * a + 8 * t, 8), :] = own0
                pack_ref[pl.ds(128 * a + 64 + 8 * t, 8), :] = own1
            else:
                coef_out[pl.ds(8 * t, 8), :] = own0
                coef_out[pl.ds(64 + 8 * t, 8), :] = own1
            band_out[pl.ds(64 * a + 8 * t, 8), :] = band
    edge_rows = []
    for direction in range(6):
        first = jnp.broadcast_to(pattern_ref[pl.ds(direction, 1), pl.ds(0, LANES)], (8, LANES))
        second = jnp.broadcast_to(pattern_ref[pl.ds(direction, 1), pl.ds(LANES, LANES)], (8, LANES))
        edge_rows.append(jnp.where(lane < 64, first, second))
    kinds = face_indices(edge_rows)
    for a in range(2):

        def read(c, t):
            if c < 2:
                return pack_ref[pl.ds(128 * a + 64 * c + 8 * t, 8), :]
            return band_out[pl.ds(64 * a + 8 * t, 8), :]

        src = Sources(read)
        for r in range(4):
            pack_ref[pl.ds(256 + 32 * a + 8 * r, 8), :] = jnp.where(
                lane < 64, src.tile[2][r], pltpu.roll(src.tile[2][r + 4], 64, 1)
            )
        here = [jnp.where(lane < 64, src.tile[0][t], src.tile[1][t]) for t in range(TILES)]
        turned = [jnp.where(lane < 64, src.turned[0][t], src.turned[1][t]) for t in range(TILES)]
        total = neighbour_sum(src, here, turned, kinds)
        for half in range(2):
            at = pl.ds(16 * a + 8 * half, 8)
            first = [spin(total[2 * q + half], 32 * q) for q in range(4)]
            last = [spin(total[2 * q + half], 32 * q + 32) for q in range(4)]
            first, last = (
                jnp.where(
                    lane < 64,
                    jnp.where(lane < 32, values[0], values[1]),
                    jnp.where(lane < 96, values[2], values[3]),
                )
                for values in (first, last)
            )
            sum_near[at, :] = jnp.where(even, last, first)
            sum_far[at, :] = jnp.where(even, first, last)


def own(ref, a, c, t):
    return ref[pl.ds(128 * a + 64 * c + 8 * t, 8), :]


def own_kinds(pattern_ref):
    return [
        face_indices(
            [
                jnp.broadcast_to(pattern_ref[pl.ds(d, 1), pl.ds(LANES * c, LANES)], (8, LANES))
                for d in range(6)
            ]
        )
        for c in range(2)
    ]


def gains(weights, coef):
    spread = weights[0] * coef
    return spread, OMEGA / (6.0 * spread + weights[4])


def bulge(weights, phase):
    return weights[3] * (2.0 * phase - phase * phase * phase)


def own_kernel(layers, table, pattern_ref, pack_ref, coef_ref, band_ref, half_ref):
    group = lax.axis_index("gy")
    kinds = own_kinds(pattern_ref)
    weights = [weights_at(table, group, layers, a) for a in range(2)]
    for a in range(2):
        src = Sources(
            lambda c, t: own(pack_ref, a, c, t) if c < 2 else band_ref[pl.ds(64 * a + 8 * t, 8), :]
        )
        for c in range(2):
            total = neighbour_sum(src, src.tile[c], src.turned[c], kinds[c])
            for t in range(TILES):
                now = src.tile[c][t]
                spread, gain = gains(weights[a], coef_ref[pl.ds(64 * c + 8 * t, 8), :])
                push = spread * total[t] + weights[a][2 - a] * own(pack_ref, 1 - a, c, t)
                if a == 0:
                    push = push + bulge(weights[0], now)
                half_ref[pl.ds(128 * a + 64 * c + 8 * t, 8), :] = (1.0 - OMEGA) * now + gain * push


def relax_kernel(
    layers, table,
    pattern_ref, pack_ref, coef_ref, band_ref, half_ref, side_near, side_far, sum_near, sum_far,
    out_ref, next_own, next_band, next_side,
):
    lane = lanes()
    group = lax.axis_index("gy")
    even = is_even("leaf")
    even_group = is_even("gy")
    kinds = own_kinds(pattern_ref)
    w_lower, w_first, w_second, w_upper = (weights_at(table, group, layers, o) for o in (-1, 0, 1, 2))

    def step(weights, now, total, below, above, coef, phase):
        spread, gain = gains(weights, coef)
        push = spread * total + weights[1] * below + weights[2] * above
        if phase is not None:
            push = push + bulge(weights, phase)
        return (1.0 - OMEGA) * now + gain * push

    def beside(upper, at):
        near, far = side_near[at, :], side_far[at, :]
        return jnp.where(even_group, near, far) if upper else jnp.where(even_group, far, near)

    def side(upper, a, c, t):
        return beside(upper, pl.ds(128 * a + 64 * c + 8 * t, 8))

    def side_band(upper, a, t):
        tile = beside(upper, pl.ds(256 + 32 * a + 8 * (t % 4), 8))
        tile = pltpu.roll(tile, 64, 1) if t >= 4 else tile
        return jnp.where(lane < 64, tile, 0.0)

    for a in range(2):
        weights = w_second if a else w_first
        for c in range(2):
            for t in range(TILES):
                _, gain = gains(weights, coef_ref[pl.ds(64 * c + 8 * t, 8), :])
                missing = weights[1 + a] * side(a, 1 - a, c, t)
                next_own[pl.ds(128 * a + 64 * c + 8 * t, 8), :] = own(half_ref, a, c, t) + gain * missing
        for t in range(TILES):
            now = band_ref[pl.ds(64 * a + 8 * t, 8), :]
            coef = band_ref[pl.ds(128 + 8 * t, 8), :]
            at = pl.ds(16 * a + 8 * (t % 2), 8)
            q = t // 2
            near, far = sum_near[at, :], sum_far[at, :]
            low, high = jnp.where(even, far, near), jnp.where(even, near, far)
            low, high = spin(low, -32 * q), spin(high, 32 - 32 * q)
            total_t = jnp.where(lane < 32, low, jnp.where(lane < 64, high, 0.0))
            if a == 0:
                below, above = side_band(0, 1, t), band_ref[pl.ds(64 + 8 * t, 8), :]
                new = step(w_first, now, total_t, below, above, coef, now)
            else:
                below, above = band_ref[pl.ds(8 * t, 8), :], side_band(1, 0, t)
                new = step(w_second, now, total_t, below, above, coef, None)
            next_band[pl.ds(64 * a + 8 * t, 8), :] = new

    for upper in range(2):
        a = 1 - upper
        src = Sources(lambda c, t: side(upper, a, c, t) if c < 2 else side_band(upper, a, t))
        for c in range(2):
            total = neighbour_sum(src, src.tile[c], src.turned[c], kinds[c])
            for t in range(TILES):
                coef = coef_ref[pl.ds(64 * c + 8 * t, 8), :]
                if upper:
                    below, above = own(pack_ref, 1, c, t), side(1, 1, c, t)
                    new = step(w_upper, src.tile[c][t], total[t], below, above, coef, None)
                else:
                    below, above = side(0, 0, c, t), own(pack_ref, 0, c, t)
                    new = step(w_lower, src.tile[c][t], total[t], below, above, coef, None)
                next_side[pl.ds(128 * upper + 64 * c + 8 * t, 8), :] = new

    for a in range(2):
        src = Sources(
            lambda c, t: own(next_own, a, c, t) if c < 2 else next_band[pl.ds(64 * a + 8 * t, 8), :]
        )
        for c in range(2):
            total = neighbour_sum(src, src.tile[c], src.turned[c], kinds[c])
            for t in range(TILES):
                coef = coef_ref[pl.ds(64 * c + 8 * t, 8), :]
                now = src.tile[c][t]
                if a == 0:
                    below, above = own(next_side, 0, c, t), own(next_own, 1, c, t)
                    new = step(w_first, now, total[t], below, above, coef, own(pack_ref, 0, c, t))
                else:
                    below, above = own(next_own, 0, c, t), own(next_side, 1, c, t)
                    new = step(w_second, now, total[t], below, above, coef, None)
                out_ref[a, pl.ds(8 * t, 8), pl.ds(LANES * c, LANES)] = new


def swap(block, axis, first):
    route = []
    for i in range(first, lax.axis_size(axis) - 1, 2):
        route += [(i, i + 1), (i + 1, i)]
    return lax.ppermute(block, axis, route)


def call(kernel, shapes, spaces, *operands, scratch=(), flops=0):
    vmem = pltpu.VMEM
    space = {"h": pltpu.HBM, "v": vmem, "s": pltpu.SMEM}
    moved = sum(4 * int(np.prod(o.shape)) for o in operands)
    return pl.pallas_call(
        kernel,
        out_shape=[jax.ShapeDtypeStruct(s, F32) for s in shapes],
        in_specs=[pl.BlockSpec(memory_space=space[s]) for s in spaces],
        out_specs=[pl.BlockSpec(memory_space=vmem) for _ in shapes],
        scratch_shapes=list(scratch),
        compiler_params=pltpu.CompilerParams(vmem_limit_bytes=16 * 2**20),
        cost_estimate=pl.CostEstimate(flops=flops, bytes_accessed=moved, transcendentals=0),
    )(*operands)


def local(table, field_old, coef_old, owner, counts, pattern):
    layers = field_old.shape[0]
    stored = [pltpu.with_memory_space_constraint(x, pltpu.HBM) for x in (field_old, coef_old, owner)]
    to_near, to_far, field, coef = call(
        send_kernel,
        [(104, LANES), (104, LANES), field_old.shape, coef_old.shape],
        "hhhs",
        *stored, counts,
        scratch=[
            pltpu.SMEM((OLD_SLOTS,), jnp.int32),
            pltpu.SemaphoreType.DMA((3,)),
        ],
    )
    from_far = swap(to_far, "leaf", 1)
    from_near = swap(to_near, "leaf", 0)
    pack, coef, band, sum_near, sum_far = call(
        place_kernel,
        [(320, LANES), (128, LANES), (192, LANES), (32, LANES), (32, LANES)],
        "vvvvvv",
        field, coef, pattern, to_near, from_near, from_far,
    )
    sum_near = swap(sum_near, "leaf", 0)
    sum_far = swap(sum_far, "leaf", 1)
    side_near = swap(pack, "gy", 0)
    side_far = swap(pack, "gy", 1)
    (half,) = call(
        functools.partial(own_kernel, layers, table),
        [(256, LANES)],
        "vvvv",
        pattern, pack, coef, band,
    )
    (out,) = call(
        functools.partial(relax_kernel, layers, table),
        [(layers, 64, BRICKS_DEV)],
        "vvvvvvvvv",
        pattern, pack, coef, band, half, side_near, side_far, sum_near, sum_far,
        scratch=[pltpu.VMEM((rows, LANES), F32) for rows in (256, 128, 256)],
    )
    return out


def solution(mesh):
    layers = Y // mesh.shape["gy"]
    return jax.shard_map(
        functools.partial(local, weight_table(layers)),
        mesh=mesh,
        in_specs=(P("gy", None, "leaf"), P(None, "leaf"), P("leaf"), P("leaf"), P(None, "leaf")),
        out_specs=P("gy", None, "leaf"),
        check_vma=False,
    )
```

```python
import functools

import jax
import jax.numpy as jnp
import numpy as np
from jax import lax
from jax.experimental import pallas as pl
from jax.experimental.pallas import tpu as pltpu
from jax.sharding import PartitionSpec as P

BRICKS_DEV = 256
SPILL = 32
Y = 8
OLD_SLOTS = 320
EXPONENT = 0.5
HEIGHT = 8.0
OMEGA = 0.8

F32 = jnp.float32
LANES = 128
TILES = 8
GATHER = lax.GatherDimensionNumbers(
    offset_dims=(),
    collapsed_slice_dims=(1,),
    start_index_map=(1,),
    operand_batching_dims=(0,),
    start_indices_batching_dims=(0,),
)


def weight_table(layers):
    rows = []
    for level in range(-1, Y + 1):
        if not 0 <= level < Y:
            rows.append((0.0, 0.0, 0.0, 0.0, 1.0))
            continue
        y_here = HEIGHT * (level / Y) ** 2
        y_next = HEIGHT * ((level + 1) / Y) ** 2
        y_prev = HEIGHT * ((level - 1) / Y) ** 2
        step_up, step_down = y_next - y_here, y_here - y_prev
        up_weight = ((y_here + y_next) * 0.5) ** EXPONENT
        down_weight = ((y_here + y_prev) * 0.5) ** EXPONENT
        has_lower = float(level > 0)
        up_link = up_weight / step_up
        down_link = has_lower * down_weight / step_down
        planar = 0.5 * (up_weight * step_up + has_lower * down_weight * step_down)
        surface = float(level == 0)
        rows.append((planar, down_link, up_link, surface, down_link + up_link + surface))
    return np.asarray(rows, np.float32)


def weights_at(table, group, layers, offset):
    groups = Y // layers
    out = []
    for column in range(5):
        value = F32(table[offset + 1, column])
        for g in range(1, groups):
            value = jnp.where(group == g, F32(table[g * layers + offset + 1, column]), value)
        out.append(value)
    return out


def lanes():
    return lax.broadcasted_iota(jnp.int32, (8, LANES), 1)


def rows():
    return lax.broadcasted_iota(jnp.int32, (8, LANES), 0)


def spin(tile, shift):
    if isinstance(shift, int):
        return pltpu.roll(tile, shift % LANES, 1) if shift % LANES else tile
    return pltpu.roll(tile, jnp.bitwise_and(shift, LANES - 1), 1)


def pick(tile, index):
    return lax.gather(
        tile,
        index[:, :, None],
        GATHER,
        (1, 1),
        mode=lax.GatherScatterMode.PROMISE_IN_BOUNDS,
    )


def spill_counts(owner_ref, live_count, device):
    to_prev = jnp.int32(0)
    to_next = jnp.int32(0)
    for step in (32, 16, 8, 4, 2, 1):
        near = jnp.minimum(to_prev + step, SPILL)
        hit = (to_prev + step <= SPILL) & (owner_ref[near - 1] < device)
        to_prev = jnp.where(hit, to_prev + step, to_prev)
        near = jnp.minimum(to_next + step, SPILL)
        hit = (to_next + step <= SPILL) & (owner_ref[live_count - near] > device)
        to_next = jnp.where(hit, to_next + step, to_next)
    return to_prev, to_next


def old_tile(ref, lead, t, c):
    at = (lead, pl.ds(8 * t, 8)) if lead is not None else (pl.ds(8 * t, 8),)
    if c < 2:
        return ref[at + (pl.ds(LANES * c, LANES),)]
    half = ref[at + (pl.ds(2 * LANES, OLD_SLOTS - 2 * LANES),)]
    return jnp.concatenate([half, jnp.zeros((8, 3 * LANES - OLD_SLOTS), F32)], axis=1)


def face_indices(pattern_rows):
    sub = rows()
    kinds = (
        pattern_rows[0],
        pattern_rows[1],
        jnp.where(sub < 4, pattern_rows[3], pattern_rows[2]),
        jnp.where((sub & 3) == 3, pattern_rows[4], pattern_rows[5]),
    )
    out = []
    for w in kinds:
        source = w >> 7
        own = (source == 2) | (source == 3)
        beside = jnp.where(w >= 2 * BRICKS_DEV, w - (2 * BRICKS_DEV - SPILL), w - (BRICKS_DEV - SPILL))
        lane = jnp.where(own, w & (LANES - 1), jnp.where(w >= BRICKS_DEV - SPILL, beside, LANES - 1))
        out.append((lane, source == 2, source == 3))
    return out


def face(kind, tiles):
    lane, first, second = kind
    return jnp.where(first, pick(tiles[0], lane), jnp.where(second, pick(tiles[1], lane), pick(tiles[2], lane)))


class Sources:
    def __init__(self, read):
        sub = rows()
        self.tile = [[read(c, t) for t in range(TILES)] for c in range(3)]
        self.turned = [[pltpu.roll(v, 4, 0) for v in column] for column in self.tile]
        self.y_edge = [
            [jnp.where(sub < 4, column[2 * i], column[2 * i + 1]) for i in range(4)]
            for column in self.tile
        ]


def neighbour_sum(src, here, turned, kinds):
    sub = rows()
    low, k = sub < 4, sub & 3
    x_low, x_high, y_both, z_both = kinds
    total = []
    for t in range(TILES):
        if t < 2:
            below = face(x_low, [src.tile[c][6 + t] for c in range(3)])
        else:
            below = here[t - 2]
        if t >= 6:
            above = face(x_high, [src.tile[c][t - 6] for c in range(3)])
        else:
            above = here[t + 2]
        total.append(below + above)
    for i in range(4):
        edge = pltpu.roll(face(y_both, [src.y_edge[c][i] for c in range(3)]), 4, 0)
        first, second = turned[2 * i], turned[2 * i + 1]
        middle = jnp.where(low, first, second)
        total[2 * i] += jnp.where(low, edge, first) + middle
        total[2 * i + 1] += jnp.where(low, second, edge) + middle
    for t in range(TILES):
        edge = face(z_both, [src.turned[c][t] for c in range(3)])
        total[t] += pltpu.roll(jnp.where(k == 3, edge, here[t]), 1, 0)
        total[t] += pltpu.roll(jnp.where(k == 0, edge, here[t]), 7, 0)
    return total


def is_even(axis):
    return (lax.axis_index(axis) & 1) == 0


def send_kernel(
    field_hbm, coef_hbm, owner_hbm, counts_ref,
    near_ref, far_ref, field_ref, coef_ref,
    owner_ref, sems,
):
    pairs = ((owner_hbm, owner_ref), (field_hbm, field_ref), (coef_hbm, coef_ref))
    copies = [pltpu.make_async_copy(a, b, sems.at[i]) for i, (a, b) in enumerate(pairs)]
    for copy in copies:
        copy.start()
    lane, sub = lanes(), rows()
    even = is_even("leaf")
    copies[0].wait()
    live = counts_ref[0]
    to_prev, to_next = spill_counts(owner_ref, live, lax.axis_index("leaf"))
    kept = jnp.where(sub == 1, live, jnp.where(sub == 2, to_prev, to_next)).astype(F32)
    prev_count = jnp.where(sub == 0, to_prev.astype(F32), kept)
    next_count = jnp.where(sub == 0, to_next.astype(F32), kept)
    near_ref[pl.ds(96, 8), :] = jnp.where(even, next_count, prev_count)
    far_ref[pl.ds(96, 8), :] = jnp.where(even, prev_count, next_count)
    for a in range(3):
        ref, lead = (field_ref, a) if a < 2 else (coef_ref, None)
        if a == 0:
            copies[1].wait()
        if a == 2:
            copies[2].wait()
        for r in range(4):
            at = pl.ds(32 * a + 8 * r, 8)
            front = old_tile(ref, lead, r, 0)
            back = old_tile(ref, lead, r + 4, 0)
            prev = jnp.where(lane < 64, front, pltpu.roll(back, 64, 1))
            early = lane >= live - 192
            front = jnp.where(early, old_tile(ref, lead, r, 1), old_tile(ref, lead, r, 2))
            back = jnp.where(early, old_tile(ref, lead, r + 4, 1), old_tile(ref, lead, r + 4, 2))
            next = jnp.where(lane < 64, spin(front, 64 - live), spin(back, 128 - live))
            near_ref[at, :] = jnp.where(even, next, prev)
            far_ref[at, :] = jnp.where(even, prev, next)


def place_kernel(
    field_ref, coef_ref, pattern_ref, kept_ref, near_ref, far_ref,
    pack_ref, coef_out, band_out, sum_near, sum_far,
):
    lane = lanes()
    even = is_even("leaf")
    live, to_prev, to_next = (kept_ref[96 + i, 0].astype(jnp.int32) for i in (1, 2, 3))
    from_near, from_far = near_ref[96, 0], far_ref[96, 0]
    from_prev = jnp.where(even, from_far, from_near).astype(jnp.int32)
    from_next = jnp.where(even, from_near, from_far).astype(jnp.int32)
    stay = live - to_prev - to_next
    drift = to_prev - from_prev
    tail = from_prev + stay - LANES
    for a in range(3):
        ref, lead = (field_ref, a) if a < 2 else (coef_ref, None)
        for t in range(TILES):
            h = 64 * (t // 4)
            at = pl.ds(32 * a + 8 * (t % 4), 8)
            near, far = near_ref[at, :], far_ref[at, :]
            before, after = jnp.where(even, far, near), jnp.where(even, near, far)
            x0, x1, x2 = (old_tile(ref, lead, t, c) for c in range(3))
            r0, r1, r2 = spin(x0, -drift), spin(x1, -drift), spin(x2, -drift)
            own0 = jnp.where(lane < LANES - drift, r0, r1)
            own1 = jnp.where(lane < -drift, r0, jnp.where(lane < LANES - drift, r1, r2))
            own0 = jnp.where(lane < from_prev, spin(before, from_prev - 64 - h), own0)
            own1 = jnp.where(lane >= tail, spin(after, tail - h), own1)
            low = jnp.where(
                lane < SPILL - to_prev,
                spin(before, from_prev - to_prev - SPILL - h),
                spin(x0, SPILL - to_prev),
            )
            end = jnp.where(lane >= live - to_next - LANES, x1, x2)
            high = jnp.where(
                lane < SPILL + to_next,
                spin(end, SPILL + to_next - live),
                spin(after, SPILL + to_next - from_next - h),
            )
            band = jnp.where(lane < SPILL, low, jnp.where(lane < 2 * SPILL, high, 0.0))
            if a < 2:
                pack_ref[pl.ds(128 * a + 8 * t, 8), :] = own0
                pack_ref[pl.ds(128 * a + 64 + 8 * t, 8), :] = own1
            else:
                coef_out[pl.ds(8 * t, 8), :] = own0
                coef_out[pl.ds(64 + 8 * t, 8), :] = own1
            band_out[pl.ds(64 * a + 8 * t, 8), :] = band
    edge_rows = []
    for direction in range(6):
        first = jnp.broadcast_to(pattern_ref[pl.ds(direction, 1), pl.ds(0, LANES)], (8, LANES))
        second = jnp.broadcast_to(pattern_ref[pl.ds(direction, 1), pl.ds(LANES, LANES)], (8, LANES))
        edge_rows.append(jnp.where(lane < 64, first, second))
    kinds = face_indices(edge_rows)
    for a in range(2):

        def read(c, t):
            if c < 2:
                return pack_ref[pl.ds(128 * a + 64 * c + 8 * t, 8), :]
            return band_out[pl.ds(64 * a + 8 * t, 8), :]

        src = Sources(read)
        for r in range(4):
            pack_ref[pl.ds(256 + 32 * a + 8 * r, 8), :] = jnp.where(
                lane < 64, src.tile[2][r], pltpu.roll(src.tile[2][r + 4], 64, 1)
            )
        here = [jnp.where(lane < 64, src.tile[0][t], src.tile[1][t]) for t in range(TILES)]
        turned = [jnp.where(lane < 64, src.turned[0][t], src.turned[1][t]) for t in range(TILES)]
        total = neighbour_sum(src, here, turned, kinds)
        for half in range(2):
            at = pl.ds(16 * a + 8 * half, 8)
            first = [spin(total[2 * q + half], 32 * q) for q in range(4)]
            last = [spin(total[2 * q + half], 32 * q + 32) for q in range(4)]
            first, last = (
                jnp.where(
                    lane < 64,
                    jnp.where(lane < 32, values[0], values[1]),
                    jnp.where(lane < 96, values[2], values[3]),
                )
                for values in (first, last)
            )
            sum_near[at, :] = jnp.where(even, last, first)
            sum_far[at, :] = jnp.where(even, first, last)


def own(ref, a, c, t):
    return ref[pl.ds(128 * a + 64 * c + 8 * t, 8), :]


def own_kinds(pattern_ref):
    return [
        face_indices(
            [
                jnp.broadcast_to(pattern_ref[pl.ds(d, 1), pl.ds(LANES * c, LANES)], (8, LANES))
                for d in range(6)
            ]
        )
        for c in range(2)
    ]


def gains(weights, coef):
    spread = weights[0] * coef
    return spread, OMEGA / (6.0 * spread + weights[4])


def bulge(weights, phase):
    return weights[3] * (2.0 * phase - phase * phase * phase)


def own_kernel(layers, table, pattern_ref, pack_ref, coef_ref, band_ref, half_ref):
    group = lax.axis_index("gy")
    kinds = own_kinds(pattern_ref)
    weights = [weights_at(table, group, layers, a) for a in range(2)]
    for a in range(2):
        src = Sources(
            lambda c, t: own(pack_ref, a, c, t) if c < 2 else band_ref[pl.ds(64 * a + 8 * t, 8), :]
        )
        for c in range(2):
            total = neighbour_sum(src, src.tile[c], src.turned[c], kinds[c])
            for t in range(TILES):
                now = src.tile[c][t]
                spread, gain = gains(weights[a], coef_ref[pl.ds(64 * c + 8 * t, 8), :])
                push = spread * total[t] + weights[a][2 - a] * own(pack_ref, 1 - a, c, t)
                if a == 0:
                    push = push + bulge(weights[0], now)
                half_ref[pl.ds(128 * a + 64 * c + 8 * t, 8), :] = (1.0 - OMEGA) * now + gain * push


def relax_kernel(
    layers, table,
    pattern_ref, pack_ref, coef_ref, band_ref, half_ref, side_far, side_near, sum_far, sum_near,
    out_ref, next_own, next_band, next_side,
):
    lane = lanes()
    group = lax.axis_index("gy")
    even = is_even("leaf")
    even_group = is_even("gy")
    kinds = own_kinds(pattern_ref)
    w_lower, w_first, w_second, w_upper = (weights_at(table, group, layers, o) for o in (-1, 0, 1, 2))

    def step(weights, now, total, below, above, coef, phase):
        spread, gain = gains(weights, coef)
        push = spread * total + weights[1] * below + weights[2] * above
        if phase is not None:
            push = push + bulge(weights, phase)
        return (1.0 - OMEGA) * now + gain * push

    def beside(upper, at):
        near, far = side_near[at, :], side_far[at, :]
        return jnp.where(even_group, near, far) if upper else jnp.where(even_group, far, near)

    def side(upper, a, c, t):
        return beside(upper, pl.ds(128 * a + 64 * c + 8 * t, 8))

    def side_band(upper, a, t):
        tile = beside(upper, pl.ds(256 + 32 * a + 8 * (t % 4), 8))
        tile = pltpu.roll(tile, 64, 1) if t >= 4 else tile
        return jnp.where(lane < 64, tile, 0.0)

    for a in range(2):
        weights = w_second if a else w_first
        for c in range(2):
            for t in range(TILES):
                _, gain = gains(weights, coef_ref[pl.ds(64 * c + 8 * t, 8), :])
                missing = weights[1 + a] * side(a, 1 - a, c, t)
                next_own[pl.ds(128 * a + 64 * c + 8 * t, 8), :] = own(half_ref, a, c, t) + gain * missing
        for t in range(TILES):
            now = band_ref[pl.ds(64 * a + 8 * t, 8), :]
            coef = band_ref[pl.ds(128 + 8 * t, 8), :]
            at = pl.ds(16 * a + 8 * (t % 2), 8)
            q = t // 2
            near, far = sum_near[at, :], sum_far[at, :]
            low, high = jnp.where(even, far, near), jnp.where(even, near, far)
            low, high = spin(low, -32 * q), spin(high, 32 - 32 * q)
            total_t = jnp.where(lane < 32, low, jnp.where(lane < 64, high, 0.0))
            if a == 0:
                below, above = side_band(0, 1, t), band_ref[pl.ds(64 + 8 * t, 8), :]
                new = step(w_first, now, total_t, below, above, coef, now)
            else:
                below, above = band_ref[pl.ds(8 * t, 8), :], side_band(1, 0, t)
                new = step(w_second, now, total_t, below, above, coef, None)
            next_band[pl.ds(64 * a + 8 * t, 8), :] = new

    for upper in range(2):
        a = 1 - upper
        src = Sources(lambda c, t: side(upper, a, c, t) if c < 2 else side_band(upper, a, t))
        for c in range(2):
            total = neighbour_sum(src, src.tile[c], src.turned[c], kinds[c])
            for t in range(TILES):
                coef = coef_ref[pl.ds(64 * c + 8 * t, 8), :]
                if upper:
                    below, above = own(pack_ref, 1, c, t), side(1, 1, c, t)
                    new = step(w_upper, src.tile[c][t], total[t], below, above, coef, None)
                else:
                    below, above = side(0, 0, c, t), own(pack_ref, 0, c, t)
                    new = step(w_lower, src.tile[c][t], total[t], below, above, coef, None)
                next_side[pl.ds(128 * upper + 64 * c + 8 * t, 8), :] = new

    for a in range(2):
        src = Sources(
            lambda c, t: own(next_own, a, c, t) if c < 2 else next_band[pl.ds(64 * a + 8 * t, 8), :]
        )
        for c in range(2):
            total = neighbour_sum(src, src.tile[c], src.turned[c], kinds[c])
            for t in range(TILES):
                coef = coef_ref[pl.ds(64 * c + 8 * t, 8), :]
                now = src.tile[c][t]
                if a == 0:
                    below, above = own(next_side, 0, c, t), own(next_own, 1, c, t)
                    new = step(w_first, now, total[t], below, above, coef, own(pack_ref, 0, c, t))
                else:
                    below, above = own(next_own, 0, c, t), own(next_side, 1, c, t)
                    new = step(w_second, now, total[t], below, above, coef, None)
                out_ref[a, pl.ds(8 * t, 8), pl.ds(LANES * c, LANES)] = new


def swap(block, axis, first):
    route = []
    for i in range(first, lax.axis_size(axis) - 1, 2):
        route += [(i, i + 1), (i + 1, i)]
    return lax.ppermute(block, axis, route)


def call(kernel, shapes, spaces, *operands, scratch=(), flops=0):
    vmem = pltpu.VMEM
    space = {"h": pltpu.HBM, "v": vmem, "s": pltpu.SMEM}
    moved = sum(4 * int(np.prod(o.shape)) for o in operands)
    return pl.pallas_call(
        kernel,
        out_shape=[jax.ShapeDtypeStruct(s, F32) for s in shapes],
        in_specs=[pl.BlockSpec(memory_space=space[s]) for s in spaces],
        out_specs=[pl.BlockSpec(memory_space=vmem) for _ in shapes],
        scratch_shapes=list(scratch),
        compiler_params=pltpu.CompilerParams(vmem_limit_bytes=16 * 2**20),
        cost_estimate=pl.CostEstimate(flops=flops, bytes_accessed=moved, transcendentals=0),
    )(*operands)


def local(table, field_old, coef_old, owner, counts, pattern):
    layers = field_old.shape[0]
    stored = [pltpu.with_memory_space_constraint(x, pltpu.HBM) for x in (field_old, coef_old, owner)]
    to_near, to_far, field, coef = call(
        send_kernel,
        [(104, LANES), (104, LANES), field_old.shape, coef_old.shape],
        "hhhs",
        *stored, counts,
        scratch=[
            pltpu.SMEM((OLD_SLOTS,), jnp.int32),
            pltpu.SemaphoreType.DMA((3,)),
        ],
    )
    from_far = swap(to_far, "leaf", 1)
    from_near = swap(to_near, "leaf", 0)
    pack, coef, band, sum_near, sum_far = call(
        place_kernel,
        [(320, LANES), (128, LANES), (192, LANES), (32, LANES), (32, LANES)],
        "vvvvvv",
        field, coef, pattern, to_near, from_near, from_far,
    )
    side_near = swap(pack, "gy", 0)
    side_far = swap(pack, "gy", 1)
    sum_far = swap(sum_far, "leaf", 1)
    sum_near = swap(sum_near, "leaf", 0)
    (half,) = call(
        functools.partial(own_kernel, layers, table),
        [(256, LANES)],
        "vvvv",
        pattern, pack, coef, band,
    )
    (out,) = call(
        functools.partial(relax_kernel, layers, table),
        [(layers, 64, BRICKS_DEV)],
        "vvvvvvvvv",
        pattern, pack, coef, band, half, side_far, side_near, sum_far, sum_near,
        scratch=[pltpu.VMEM((rows, LANES), F32) for rows in (256, 128, 256)],
    )
    return out


def solution(mesh):
    layers = Y // mesh.shape["gy"]
    return jax.shard_map(
        functools.partial(local, weight_table(layers)),
        mesh=mesh,
        in_specs=(P("gy", None, "leaf"), P(None, "leaf"), P("leaf"), P("leaf"), P(None, "leaf")),
        out_specs=P("gy", None, "leaf"),
        check_vma=False,
    )
```

```python
import functools

import jax
import jax.numpy as jnp
import numpy as np
from jax import lax
from jax.experimental import pallas as pl
from jax.experimental.pallas import tpu as pltpu
from jax.sharding import PartitionSpec as P

BRICKS_DEV = 256
SPILL = 32
Y = 8
OLD_SLOTS = 320
EXPONENT = 0.5
HEIGHT = 8.0
OMEGA = 0.8

F32 = jnp.float32
LANES = 128
TILES = 8
GATHER = lax.GatherDimensionNumbers(
    offset_dims=(),
    collapsed_slice_dims=(1,),
    start_index_map=(1,),
    operand_batching_dims=(0,),
    start_indices_batching_dims=(0,),
)


def weight_table(layers):
    rows = []
    for level in range(-1, Y + 1):
        if not 0 <= level < Y:
            rows.append((0.0, 0.0, 0.0, 0.0, 1.0))
            continue
        y_here = HEIGHT * (level / Y) ** 2
        y_next = HEIGHT * ((level + 1) / Y) ** 2
        y_prev = HEIGHT * ((level - 1) / Y) ** 2
        step_up, step_down = y_next - y_here, y_here - y_prev
        up_weight = ((y_here + y_next) * 0.5) ** EXPONENT
        down_weight = ((y_here + y_prev) * 0.5) ** EXPONENT
        has_lower = float(level > 0)
        up_link = up_weight / step_up
        down_link = has_lower * down_weight / step_down
        planar = 0.5 * (up_weight * step_up + has_lower * down_weight * step_down)
        surface = float(level == 0)
        rows.append((planar, down_link, up_link, surface, down_link + up_link + surface))
    return np.asarray(rows, np.float32)


def weights_at(table, group, layers, offset):
    groups = Y // layers
    out = []
    for column in range(5):
        value = F32(table[offset + 1, column])
        for g in range(1, groups):
            value = jnp.where(group == g, F32(table[g * layers + offset + 1, column]), value)
        out.append(value)
    return out


def lanes():
    return lax.broadcasted_iota(jnp.int32, (8, LANES), 1)


def rows():
    return lax.broadcasted_iota(jnp.int32, (8, LANES), 0)


def spin(tile, shift):
    if isinstance(shift, int):
        return pltpu.roll(tile, shift % LANES, 1) if shift % LANES else tile
    return pltpu.roll(tile, jnp.bitwise_and(shift, LANES - 1), 1)


def pick(tile, index):
    return lax.gather(
        tile,
        index[:, :, None],
        GATHER,
        (1, 1),
        mode=lax.GatherScatterMode.PROMISE_IN_BOUNDS,
    )


def spill_counts(owner_ref, live_count, device):
    to_prev = jnp.int32(0)
    to_next = jnp.int32(0)
    for step in (32, 16, 8, 4, 2, 1):
        near = jnp.minimum(to_prev + step, SPILL)
        hit = (to_prev + step <= SPILL) & (owner_ref[near - 1] < device)
        to_prev = jnp.where(hit, to_prev + step, to_prev)
        near = jnp.minimum(to_next + step, SPILL)
        hit = (to_next + step <= SPILL) & (owner_ref[live_count - near] > device)
        to_next = jnp.where(hit, to_next + step, to_next)
    return to_prev, to_next


def old_tile(ref, lead, t, c):
    at = (lead, pl.ds(8 * t, 8)) if lead is not None else (pl.ds(8 * t, 8),)
    if c < 2:
        return ref[at + (pl.ds(LANES * c, LANES),)]
    half = ref[at + (pl.ds(2 * LANES, OLD_SLOTS - 2 * LANES),)]
    return jnp.concatenate([half, jnp.zeros((8, 3 * LANES - OLD_SLOTS), F32)], axis=1)


def face_indices(pattern_rows):
    sub = rows()
    kinds = (
        pattern_rows[0],
        pattern_rows[1],
        jnp.where(sub < 4, pattern_rows[3], pattern_rows[2]),
        jnp.where((sub & 3) == 3, pattern_rows[4], pattern_rows[5]),
    )
    out = []
    for w in kinds:
        source = w >> 7
        own = (source == 2) | (source == 3)
        beside = jnp.where(w >= 2 * BRICKS_DEV, w - (2 * BRICKS_DEV - SPILL), w - (BRICKS_DEV - SPILL))
        lane = jnp.where(own, w & (LANES - 1), jnp.where(w >= BRICKS_DEV - SPILL, beside, LANES - 1))
        out.append((lane, source == 2, source == 3))
    return out


def face(kind, tiles):
    lane, first, second = kind
    return jnp.where(first, pick(tiles[0], lane), jnp.where(second, pick(tiles[1], lane), pick(tiles[2], lane)))


class Sources:
    def __init__(self, read):
        sub = rows()
        self.tile = [[read(c, t) for t in range(TILES)] for c in range(3)]
        self.turned = [[pltpu.roll(v, 4, 0) for v in column] for column in self.tile]
        self.y_edge = [
            [jnp.where(sub < 4, column[2 * i], column[2 * i + 1]) for i in range(4)]
            for column in self.tile
        ]


def neighbour_sum(src, here, turned, kinds):
    sub = rows()
    low, k = sub < 4, sub & 3
    x_low, x_high, y_both, z_both = kinds
    total = []
    for t in range(TILES):
        if t < 2:
            below = face(x_low, [src.tile[c][6 + t] for c in range(3)])
        else:
            below = here[t - 2]
        if t >= 6:
            above = face(x_high, [src.tile[c][t - 6] for c in range(3)])
        else:
            above = here[t + 2]
        total.append(below + above)
    for i in range(4):
        edge = pltpu.roll(face(y_both, [src.y_edge[c][i] for c in range(3)]), 4, 0)
        first, second = turned[2 * i], turned[2 * i + 1]
        middle = jnp.where(low, first, second)
        total[2 * i] += jnp.where(low, edge, first) + middle
        total[2 * i + 1] += jnp.where(low, second, edge) + middle
    for t in range(TILES):
        edge = face(z_both, [src.turned[c][t] for c in range(3)])
        total[t] += pltpu.roll(jnp.where(k == 3, edge, here[t]), 1, 0)
        total[t] += pltpu.roll(jnp.where(k == 0, edge, here[t]), 7, 0)
    return total


def is_even(axis):
    return (lax.axis_index(axis) & 1) == 0


def send_kernel(
    field_hbm, coef_hbm, owner_hbm, counts_ref,
    near_ref, far_ref, field_ref, coef_ref,
    owner_ref, sems,
):
    pairs = ((owner_hbm, owner_ref), (field_hbm, field_ref), (coef_hbm, coef_ref))
    copies = [pltpu.make_async_copy(a, b, sems.at[i]) for i, (a, b) in enumerate(pairs)]
    for copy in copies:
        copy.start()
    lane, sub = lanes(), rows()
    even = is_even("leaf")
    copies[0].wait()
    live = counts_ref[0]
    to_prev, to_next = spill_counts(owner_ref, live, lax.axis_index("leaf"))
    kept = jnp.where(sub == 1, live, jnp.where(sub == 2, to_prev, to_next)).astype(F32)
    prev_count = jnp.where(sub == 0, to_prev.astype(F32), kept)
    next_count = jnp.where(sub == 0, to_next.astype(F32), kept)
    near_ref[pl.ds(96, 8), :] = jnp.where(even, next_count, prev_count)
    far_ref[pl.ds(96, 8), :] = jnp.where(even, prev_count, next_count)
    for a in range(3):
        ref, lead = (field_ref, a) if a < 2 else (coef_ref, None)
        if a == 0:
            copies[1].wait()
        if a == 2:
            copies[2].wait()
        for r in range(4):
            at = pl.ds(32 * a + 8 * r, 8)
            front = old_tile(ref, lead, r, 0)
            back = old_tile(ref, lead, r + 4, 0)
            prev = jnp.where(lane < 64, front, pltpu.roll(back, 64, 1))
            early = lane >= live - 192
            front = jnp.where(early, old_tile(ref, lead, r, 1), old_tile(ref, lead, r, 2))
            back = jnp.where(early, old_tile(ref, lead, r + 4, 1), old_tile(ref, lead, r + 4, 2))
            next = jnp.where(lane < 64, spin(front, 64 - live), spin(back, 128 - live))
            near_ref[at, :] = jnp.where(even, next, prev)
            far_ref[at, :] = jnp.where(even, prev, next)


def place_kernel(
    field_ref, coef_ref, pattern_ref, kept_ref, near_ref, far_ref,
    pack_ref, coef_out, band_out, sum_near, sum_far,
):
    lane = lanes()
    even = is_even("leaf")
    live, to_prev, to_next = (kept_ref[96 + i, 0].astype(jnp.int32) for i in (1, 2, 3))
    from_near, from_far = near_ref[96, 0], far_ref[96, 0]
    from_prev = jnp.where(even, from_far, from_near).astype(jnp.int32)
    from_next = jnp.where(even, from_near, from_far).astype(jnp.int32)
    stay = live - to_prev - to_next
    drift = to_prev - from_prev
    tail = from_prev + stay - LANES
    for a in range(3):
        ref, lead = (field_ref, a) if a < 2 else (coef_ref, None)
        for t in range(TILES):
            h = 64 * (t // 4)
            at = pl.ds(32 * a + 8 * (t % 4), 8)
            near, far = near_ref[at, :], far_ref[at, :]
            before, after = jnp.where(even, far, near), jnp.where(even, near, far)
            x0, x1, x2 = (old_tile(ref, lead, t, c) for c in range(3))
            r0, r1, r2 = spin(x0, -drift), spin(x1, -drift), spin(x2, -drift)
            own0 = jnp.where(lane < LANES - drift, r0, r1)
            own1 = jnp.where(lane < -drift, r0, jnp.where(lane < LANES - drift, r1, r2))
            own0 = jnp.where(lane < from_prev, spin(before, from_prev - 64 - h), own0)
            own1 = jnp.where(lane >= tail, spin(after, tail - h), own1)
            low = jnp.where(
                lane < SPILL - to_prev,
                spin(before, from_prev - to_prev - SPILL - h),
                spin(x0, SPILL - to_prev),
            )
            end = jnp.where(lane >= live - to_next - LANES, x1, x2)
            high = jnp.where(
                lane < SPILL + to_next,
                spin(end, SPILL + to_next - live),
                spin(after, SPILL + to_next - from_next - h),
            )
            band = jnp.where(lane < SPILL, low, jnp.where(lane < 2 * SPILL, high, 0.0))
            if a < 2:
                pack_ref[pl.ds(128 * a + 8 * t, 8), :] = own0
                pack_ref[pl.ds(128 * a + 64 + 8 * t, 8), :] = own1
            else:
                coef_out[pl.ds(8 * t, 8), :] = own0
                coef_out[pl.ds(64 + 8 * t, 8), :] = own1
            band_out[pl.ds(64 * a + 8 * t, 8), :] = band
    edge_rows = []
    for direction in range(6):
        first = jnp.broadcast_to(pattern_ref[pl.ds(direction, 1), pl.ds(0, LANES)], (8, LANES))
        second = jnp.broadcast_to(pattern_ref[pl.ds(direction, 1), pl.ds(LANES, LANES)], (8, LANES))
        edge_rows.append(jnp.where(lane < 64, first, second))
    kinds = face_indices(edge_rows)
    for a in range(2):

        def read(c, t):
            if c < 2:
                return pack_ref[pl.ds(128 * a + 64 * c + 8 * t, 8), :]
            return band_out[pl.ds(64 * a + 8 * t, 8), :]

        src = Sources(read)
        for r in range(4):
            pack_ref[pl.ds(256 + 32 * a + 8 * r, 8), :] = jnp.where(
                lane < 64, src.tile[2][r], pltpu.roll(src.tile[2][r + 4], 64, 1)
            )
        here = [jnp.where(lane < 64, src.tile[0][t], src.tile[1][t]) for t in range(TILES)]
        turned = [jnp.where(lane < 64, src.turned[0][t], src.turned[1][t]) for t in range(TILES)]
        total = neighbour_sum(src, here, turned, kinds)
        for half in range(2):
            at = pl.ds(16 * a + 8 * half, 8)
            first = [spin(total[2 * q + half], 32 * q) for q in range(4)]
            last = [spin(total[2 * q + half], 32 * q + 32) for q in range(4)]
            first, last = (
                jnp.where(
                    lane < 64,
                    jnp.where(lane < 32, values[0], values[1]),
                    jnp.where(lane < 96, values[2], values[3]),
                )
                for values in (first, last)
            )
            sum_near[at, :] = jnp.where(even, last, first)
            sum_far[at, :] = jnp.where(even, first, last)


def own(ref, a, c, t):
    return ref[pl.ds(128 * a + 64 * c + 8 * t, 8), :]


def own_kinds(pattern_ref):
    return [
        face_indices(
            [
                jnp.broadcast_to(pattern_ref[pl.ds(d, 1), pl.ds(LANES * c, LANES)], (8, LANES))
                for d in range(6)
            ]
        )
        for c in range(2)
    ]


def gains(weights, coef):
    spread = weights[0] * coef
    return spread, OMEGA / (6.0 * spread + weights[4])


def bulge(weights, phase):
    return weights[3] * (2.0 * phase - phase * phase * phase)


def own_kernel(layers, table, pattern_ref, pack_ref, coef_ref, band_ref, half_ref):
    group = lax.axis_index("gy")
    kinds = own_kinds(pattern_ref)
    weights = [weights_at(table, group, layers, a) for a in range(2)]
    for a in range(2):
        src = Sources(
            lambda c, t: own(pack_ref, a, c, t) if c < 2 else band_ref[pl.ds(64 * a + 8 * t, 8), :]
        )
        for c in range(2):
            total = neighbour_sum(src, src.tile[c], src.turned[c], kinds[c])
            for t in range(TILES):
                now = src.tile[c][t]
                spread, gain = gains(weights[a], coef_ref[pl.ds(64 * c + 8 * t, 8), :])
                push = spread * total[t] + weights[a][2 - a] * own(pack_ref, 1 - a, c, t)
                if a == 0:
                    push = push + bulge(weights[0], now)
                half_ref[pl.ds(128 * a + 64 * c + 8 * t, 8), :] = (1.0 - OMEGA) * now + gain * push


def relax_kernel(
    layers, table,
    pattern_ref, pack_ref, coef_ref, band_ref, half_ref, column_ref, sum_far, sum_near,
    out_ref, next_own, next_band, next_side, lower_ref, upper_ref, sems,
):
    lane = lanes()
    group = lax.axis_index("gy")
    even = is_even("leaf")
    groups = Y // layers
    lower_at, upper_at = jnp.maximum(group - 1, 0), jnp.minimum(group + 1, groups - 1)
    copies = [
        pltpu.make_async_copy(column_ref.at[lower_at], lower_ref, sems.at[0]),
        pltpu.make_async_copy(column_ref.at[upper_at], upper_ref, sems.at[1]),
    ]
    for copy in copies:
        copy.start()
    kinds = own_kinds(pattern_ref)
    w_lower, w_first, w_second, w_upper = (weights_at(table, group, layers, o) for o in (-1, 0, 1, 2))

    def step(weights, now, total, below, above, coef, phase):
        spread, gain = gains(weights, coef)
        push = spread * total + weights[1] * below + weights[2] * above
        if phase is not None:
            push = push + bulge(weights, phase)
        return (1.0 - OMEGA) * now + gain * push

    def beside(upper, at):
        if upper:
            return jnp.where(group < groups - 1, upper_ref[at, :], 0.0)
        return jnp.where(group > 0, lower_ref[at, :], 0.0)

    def side(upper, a, c, t):
        return beside(upper, pl.ds(128 * a + 64 * c + 8 * t, 8))

    def side_band(upper, a, t):
        tile = beside(upper, pl.ds(256 + 32 * a + 8 * (t % 4), 8))
        tile = pltpu.roll(tile, 64, 1) if t >= 4 else tile
        return jnp.where(lane < 64, tile, 0.0)

    for copy in copies:
        copy.wait()

    for a in range(2):
        weights = w_second if a else w_first
        for c in range(2):
            for t in range(TILES):
                _, gain = gains(weights, coef_ref[pl.ds(64 * c + 8 * t, 8), :])
                missing = weights[1 + a] * side(a, 1 - a, c, t)
                next_own[pl.ds(128 * a + 64 * c + 8 * t, 8), :] = own(half_ref, a, c, t) + gain * missing
        for t in range(TILES):
            now = band_ref[pl.ds(64 * a + 8 * t, 8), :]
            coef = band_ref[pl.ds(128 + 8 * t, 8), :]
            at = pl.ds(16 * a + 8 * (t % 2), 8)
            q = t // 2
            near, far = sum_near[at, :], sum_far[at, :]
            low, high = jnp.where(even, far, near), jnp.where(even, near, far)
            low, high = spin(low, -32 * q), spin(high, 32 - 32 * q)
            total_t = jnp.where(lane < 32, low, jnp.where(lane < 64, high, 0.0))
            if a == 0:
                below, above = side_band(0, 1, t), band_ref[pl.ds(64 + 8 * t, 8), :]
                new = step(w_first, now, total_t, below, above, coef, now)
            else:
                below, above = band_ref[pl.ds(8 * t, 8), :], side_band(1, 0, t)
                new = step(w_second, now, total_t, below, above, coef, None)
            next_band[pl.ds(64 * a + 8 * t, 8), :] = new

    for upper in range(2):
        a = 1 - upper
        src = Sources(lambda c, t: side(upper, a, c, t) if c < 2 else side_band(upper, a, t))
        for c in range(2):
            total = neighbour_sum(src, src.tile[c], src.turned[c], kinds[c])
            for t in range(TILES):
                coef = coef_ref[pl.ds(64 * c + 8 * t, 8), :]
                if upper:
                    below, above = own(pack_ref, 1, c, t), side(1, 1, c, t)
                    new = step(w_upper, src.tile[c][t], total[t], below, above, coef, None)
                else:
                    below, above = side(0, 0, c, t), own(pack_ref, 0, c, t)
                    new = step(w_lower, src.tile[c][t], total[t], below, above, coef, None)
                next_side[pl.ds(128 * upper + 64 * c + 8 * t, 8), :] = new

    for a in range(2):
        src = Sources(
            lambda c, t: own(next_own, a, c, t) if c < 2 else next_band[pl.ds(64 * a + 8 * t, 8), :]
        )
        for c in range(2):
            total = neighbour_sum(src, src.tile[c], src.turned[c], kinds[c])
            for t in range(TILES):
                coef = coef_ref[pl.ds(64 * c + 8 * t, 8), :]
                now = src.tile[c][t]
                if a == 0:
                    below, above = own(next_side, 0, c, t), own(next_own, 1, c, t)
                    new = step(w_first, now, total[t], below, above, coef, own(pack_ref, 0, c, t))
                else:
                    below, above = own(next_own, 0, c, t), own(next_side, 1, c, t)
                    new = step(w_second, now, total[t], below, above, coef, None)
                out_ref[a, pl.ds(8 * t, 8), pl.ds(LANES * c, LANES)] = new


def swap(block, axis, first):
    route = []
    for i in range(first, lax.axis_size(axis) - 1, 2):
        route += [(i, i + 1), (i + 1, i)]
    return lax.ppermute(block, axis, route)


def call(kernel, shapes, spaces, *operands, scratch=(), flops=0):
    vmem = pltpu.VMEM
    space = {"h": pltpu.HBM, "v": vmem, "s": pltpu.SMEM}
    moved = sum(4 * int(np.prod(o.shape)) for o in operands)
    return pl.pallas_call(
        kernel,
        out_shape=[jax.ShapeDtypeStruct(s, F32) for s in shapes],
        in_specs=[pl.BlockSpec(memory_space=space[s]) for s in spaces],
        out_specs=[pl.BlockSpec(memory_space=vmem) for _ in shapes],
        scratch_shapes=list(scratch),
        compiler_params=pltpu.CompilerParams(vmem_limit_bytes=16 * 2**20),
        cost_estimate=pl.CostEstimate(flops=flops, bytes_accessed=moved, transcendentals=0),
    )(*operands)


def local(table, field_old, coef_old, owner, counts, pattern):
    layers = field_old.shape[0]
    stored = [pltpu.with_memory_space_constraint(x, pltpu.HBM) for x in (field_old, coef_old, owner)]
    to_near, to_far, field, coef = call(
        send_kernel,
        [(104, LANES), (104, LANES), field_old.shape, coef_old.shape],
        "hhhs",
        *stored, counts,
        scratch=[
            pltpu.SMEM((OLD_SLOTS,), jnp.int32),
            pltpu.SemaphoreType.DMA((3,)),
        ],
    )
    from_far = swap(to_far, "leaf", 1)
    from_near = swap(to_near, "leaf", 0)
    pack, coef, band, sum_near, sum_far = call(
        place_kernel,
        [(320, LANES), (128, LANES), (192, LANES), (32, LANES), (32, LANES)],
        "vvvvvv",
        field, coef, pattern, to_near, from_near, from_far,
    )
    column = pltpu.with_memory_space_constraint(lax.all_gather(pack, "gy"), pltpu.HBM)
    sum_far = swap(sum_far, "leaf", 1)
    sum_near = swap(sum_near, "leaf", 0)
    (half,) = call(
        functools.partial(own_kernel, layers, table),
        [(256, LANES)],
        "vvvv",
        pattern, pack, coef, band,
    )
    (out,) = call(
        functools.partial(relax_kernel, layers, table),
        [(layers, 64, BRICKS_DEV)],
        "vvvvvhvv",
        pattern, pack, coef, band, half, column, sum_far, sum_near,
        scratch=[pltpu.VMEM((rows, LANES), F32) for rows in (256, 128, 256, 320, 320)]
        + [pltpu.SemaphoreType.DMA((2,))],
    )
    return out


def solution(mesh):
    layers = Y // mesh.shape["gy"]
    return jax.shard_map(
        functools.partial(local, weight_table(layers)),
        mesh=mesh,
        in_specs=(P("gy", None, "leaf"), P(None, "leaf"), P("leaf"), P("leaf"), P(None, "leaf")),
        out_specs=P("gy", None, "leaf"),
        check_vma=False,
    )
```

```python
import functools

import jax
import jax.numpy as jnp
import numpy as np
from jax import lax
from jax.experimental import pallas as pl
from jax.experimental.pallas import tpu as pltpu
from jax.sharding import PartitionSpec as P

BRICKS_DEV = 256
SPILL = 32
Y = 8
OLD_SLOTS = 320
EXPONENT = 0.5
HEIGHT = 8.0
OMEGA = 0.8

F32 = jnp.float32
LANES = 128
TILES = 8
GATHER = lax.GatherDimensionNumbers(
    offset_dims=(),
    collapsed_slice_dims=(1,),
    start_index_map=(1,),
    operand_batching_dims=(0,),
    start_indices_batching_dims=(0,),
)


def weight_table(layers):
    rows = []
    for level in range(-1, Y + 1):
        if not 0 <= level < Y:
            rows.append((0.0, 0.0, 0.0, 0.0, 1.0))
            continue
        y_here = HEIGHT * (level / Y) ** 2
        y_next = HEIGHT * ((level + 1) / Y) ** 2
        y_prev = HEIGHT * ((level - 1) / Y) ** 2
        step_up, step_down = y_next - y_here, y_here - y_prev
        up_weight = ((y_here + y_next) * 0.5) ** EXPONENT
        down_weight = ((y_here + y_prev) * 0.5) ** EXPONENT
        has_lower = float(level > 0)
        up_link = up_weight / step_up
        down_link = has_lower * down_weight / step_down
        planar = 0.5 * (up_weight * step_up + has_lower * down_weight * step_down)
        surface = float(level == 0)
        rows.append((planar, down_link, up_link, surface, down_link + up_link + surface))
    return np.asarray(rows, np.float32)


def weights_at(table, group, layers, offset):
    groups = Y // layers
    out = []
    for column in range(5):
        value = F32(table[offset + 1, column])
        for g in range(1, groups):
            value = jnp.where(group == g, F32(table[g * layers + offset + 1, column]), value)
        out.append(value)
    return out


def lanes():
    return lax.broadcasted_iota(jnp.int32, (8, LANES), 1)


def rows():
    return lax.broadcasted_iota(jnp.int32, (8, LANES), 0)


def spin(tile, shift):
    if isinstance(shift, int):
        return pltpu.roll(tile, shift % LANES, 1) if shift % LANES else tile
    return pltpu.roll(tile, jnp.bitwise_and(shift, LANES - 1), 1)


def pick(tile, index):
    return lax.gather(
        tile,
        index[:, :, None],
        GATHER,
        (1, 1),
        mode=lax.GatherScatterMode.PROMISE_IN_BOUNDS,
    )


def spill_counts(owner_ref, live_count, device):
    to_prev = jnp.int32(0)
    to_next = jnp.int32(0)
    for step in (32, 16, 8, 4, 2, 1):
        near = jnp.minimum(to_prev + step, SPILL)
        hit = (to_prev + step <= SPILL) & (owner_ref[near - 1] < device)
        to_prev = jnp.where(hit, to_prev + step, to_prev)
        near = jnp.minimum(to_next + step, SPILL)
        hit = (to_next + step <= SPILL) & (owner_ref[live_count - near] > device)
        to_next = jnp.where(hit, to_next + step, to_next)
    return to_prev, to_next


def old_tile(ref, lead, t, c):
    at = (lead, pl.ds(8 * t, 8)) if lead is not None else (pl.ds(8 * t, 8),)
    if c < 2:
        return ref[at + (pl.ds(LANES * c, LANES),)]
    half = ref[at + (pl.ds(2 * LANES, OLD_SLOTS - 2 * LANES),)]
    return jnp.concatenate([half, jnp.zeros((8, 3 * LANES - OLD_SLOTS), F32)], axis=1)


def face_rows(pattern_rows):
    sub = rows()
    return (
        pattern_rows[0],
        pattern_rows[1],
        jnp.where(sub < 4, pattern_rows[3], pattern_rows[2]),
        jnp.where((sub & 3) == 3, pattern_rows[4], pattern_rows[5]),
    )


def face_indices(pattern_rows):
    out = []
    for w in face_rows(pattern_rows):
        source = w >> 7
        own = (source == 2) | (source == 3)
        beside = jnp.where(w >= 2 * BRICKS_DEV, w - (2 * BRICKS_DEV - SPILL), w - (BRICKS_DEV - SPILL))
        lane = jnp.where(own, w & (LANES - 1), jnp.where(w >= BRICKS_DEV - SPILL, beside, LANES - 1))
        out.append((lane, source == 2, source == 3))
    return out


def face(kind, tiles):
    if len(tiles) == 1:
        return pick(tiles[0], kind[0])
    lane, first, second = kind
    return jnp.where(first, pick(tiles[0], lane), jnp.where(second, pick(tiles[1], lane), pick(tiles[2], lane)))


class Sources:
    def __init__(self, read, count=3):
        sub = rows()
        self.columns = range(count)
        self.tile = [[read(c, t) for t in range(TILES)] for c in self.columns]
        self.turned = [[pltpu.roll(v, 4, 0) for v in column] for column in self.tile]
        self.y_edge = [
            [jnp.where(sub < 4, column[2 * i], column[2 * i + 1]) for i in range(4)]
            for column in self.tile
        ]


def neighbour_sum(src, here, turned, kinds):
    sub = rows()
    low, k = sub < 4, sub & 3
    x_low, x_high, y_both, z_both = kinds
    total = []
    for t in range(TILES):
        if t < 2:
            below = face(x_low, [src.tile[c][6 + t] for c in src.columns])
        else:
            below = here[t - 2]
        if t >= 6:
            above = face(x_high, [src.tile[c][t - 6] for c in src.columns])
        else:
            above = here[t + 2]
        total.append(below + above)
    for i in range(4):
        edge = pltpu.roll(face(y_both, [src.y_edge[c][i] for c in src.columns]), 4, 0)
        first, second = turned[2 * i], turned[2 * i + 1]
        middle = jnp.where(low, first, second)
        total[2 * i] += jnp.where(low, edge, first) + middle
        total[2 * i + 1] += jnp.where(low, second, edge) + middle
    for t in range(TILES):
        edge = face(z_both, [src.turned[c][t] for c in src.columns])
        total[t] += pltpu.roll(jnp.where(k == 3, edge, here[t]), 1, 0)
        total[t] += pltpu.roll(jnp.where(k == 0, edge, here[t]), 7, 0)
    return total


def is_even(axis):
    return (lax.axis_index(axis) & 1) == 0


def ends(ref, lead, r, live, next_side):
    lane = lanes()
    front, back = old_tile(ref, lead, r, 0), old_tile(ref, lead, r + 4, 0)
    prev = jnp.where(lane < 64, front, pltpu.roll(back, 64, 1))
    early = lane >= live - 192
    front = jnp.where(early, old_tile(ref, lead, r, 1), old_tile(ref, lead, r, 2))
    back = jnp.where(early, old_tile(ref, lead, r + 4, 1), old_tile(ref, lead, r + 4, 2))
    next = jnp.where(lane < 64, spin(front, 64 - live), spin(back, 128 - live))
    return jnp.where(next_side, next, prev)


def near_kernel(
    field_hbm, coef_hbm, owner_hbm, counts_ref, near_ref, field_ref, coef_ref, owner_ref, sems
):
    pairs = ((owner_hbm, owner_ref), (field_hbm, field_ref), (coef_hbm, coef_ref))
    copies = [pltpu.make_async_copy(a, b, sems.at[i]) for i, (a, b) in enumerate(pairs)]
    for copy in copies:
        copy.start()
    sub = rows()
    even = is_even("leaf")
    live = counts_ref[0]
    copies[0].wait()
    to_prev, to_next = spill_counts(owner_ref, live, lax.axis_index("leaf"))
    handed = jnp.where(even, to_next, to_prev)
    kept = jnp.where(sub == 1, live, jnp.where(sub == 2, to_prev, to_next))
    near_ref[pl.ds(96, 8), :] = jnp.where(sub == 0, handed, kept).astype(F32)
    for a in range(3):
        ref, lead = (field_ref, a) if a < 2 else (coef_ref, None)
        if a != 1:
            copies[1 + a // 2].wait()
        for r in range(4):
            near_ref[pl.ds(32 * a + 8 * r, 8), :] = ends(ref, lead, r, live, even)


def pattern_row(pattern_ref, direction, c):
    row = pattern_ref[pl.ds(direction, 1), pl.ds(LANES * c, LANES)]
    return jnp.broadcast_to(row, (8, LANES))


def pack_quarters(total, half, first):
    lane = lanes()
    base = jnp.where(first, 0, 32)
    q = [spin(total[2 * i + half], base + 32 * i) for i in range(4)]
    return jnp.where(
        lane < 64, jnp.where(lane < 32, q[0], q[1]), jnp.where(lane < 96, q[2], q[3])
    )


def far_kernel(field_ref, coef_ref, pattern_ref, kept_ref, near_ref, far_ref, own_ref, band_ref):
    lane, sub = lanes(), rows()
    even = is_even("leaf")
    live, to_prev, to_next = (kept_ref[96 + i, 0].astype(jnp.int32) for i in (1, 2, 3))
    from_near = near_ref[96, 0].astype(jnp.int32)
    stay = live - to_prev - to_next
    from_far = BRICKS_DEV - stay - from_near
    from_prev, from_next = jnp.where(even, from_far, from_near), jnp.where(even, from_near, from_far)
    drift = to_prev - from_prev
    tail = from_prev + stay - LANES
    handed = jnp.where(even, to_prev, to_next)
    values = (handed, live, to_prev, to_next, from_prev, from_next, 0, 0)
    counts = jnp.zeros((8, LANES), jnp.int32)
    for i, value in enumerate(values):
        counts = jnp.where(sub == i, value, counts)
    far_ref[pl.ds(96, 8), :] = counts.astype(F32)
    spill = (lane >= SPILL - to_prev) & (lane < SPILL + to_next)
    near_low, near_high = jnp.where(even, SPILL, 0), jnp.where(even, 2 * SPILL, SPILL)
    near_lanes = (lane >= near_low) & (lane < near_high)
    arrive_by = jnp.where(even, tail, from_prev - 64)
    band_by = jnp.where(even, SPILL + to_next - from_next, from_prev - to_prev - SPILL)
    for a in range(3):
        ref, lead = (field_ref, a) if a < 2 else (coef_ref, None)
        for r in range(4):
            far_ref[pl.ds(32 * a + 8 * r, 8), :] = ends(ref, lead, r, live, jnp.logical_not(even))
        for t in range(TILES):
            h = 64 * (t // 4)
            near = near_ref[pl.ds(32 * a + 8 * (t % 4), 8), :]
            x0, x1, x2 = (old_tile(ref, lead, t, c) for c in range(3))
            r0, r1, r2 = spin(x0, -drift), spin(x1, -drift), spin(x2, -drift)
            own0 = jnp.where(lane < LANES - drift, r0, r1)
            own1 = jnp.where(lane < -drift, r0, jnp.where(lane < LANES - drift, r1, r2))
            arrived = spin(near, arrive_by - h)
            own0 = jnp.where(lane < from_prev, jnp.where(even, 0.0, arrived), own0)
            own1 = jnp.where(lane >= tail, jnp.where(even, arrived, 0.0), own1)
            last = jnp.where(lane >= live - to_next - LANES, x1, x2)
            gone = jnp.where(lane < SPILL, spin(x0, SPILL - to_prev), spin(last, SPILL + to_next - live))
            band = jnp.where(spill, gone, jnp.where(near_lanes, spin(near, band_by - h), 0.0))
            own_ref[pl.ds(128 * a + 8 * t, 8), :] = own0
            own_ref[pl.ds(128 * a + 64 + 8 * t, 8), :] = own1
            band_ref[pl.ds(64 * a + 8 * t, 8), :] = band
    far_rows = [
        jnp.where(even, pattern_row(pattern_ref, d, 0), pattern_row(pattern_ref, d, 1)) for d in range(6)
    ]
    sent = jnp.zeros((8, LANES), jnp.int32)
    for d in range(6):
        row = spin(far_rows[d], jnp.where(even, 0, 32))
        sent = jnp.where(sub == d, row, sent)
    sent = jnp.where(lane < 32, sent, pltpu.roll(sent, 32, 1))
    far_ref[pl.ds(104, 8), :] = sent.astype(F32)
    kinds = face_indices(far_rows)
    for a in range(2):

        def read(c, t):
            if c < 2:
                return own_ref[pl.ds(128 * a + 64 * c + 8 * t, 8), :]
            return jnp.where(near_lanes, band_ref[pl.ds(64 * a + 8 * t, 8), :], 0.0)

        src = Sources(read)
        here = [jnp.where(even, src.tile[0][t], src.tile[1][t]) for t in range(TILES)]
        turned = [jnp.where(even, src.turned[0][t], src.turned[1][t]) for t in range(TILES)]
        total = neighbour_sum(src, here, turned, kinds)
        for half in range(2):
            far_ref[pl.ds(112 + 16 * a + 8 * half, 8), :] = pack_quarters(total, half, even)


def place_kernel(
    pattern_ref, kept_ref, own_ref, band_ref, far_ref,
    pack_near, pack_far, coef_out, band_out, sum_near, sum_far,
):
    lane, sub = lanes(), rows()
    even = is_even("leaf")
    even_group = is_even("gy")
    _, live, to_prev, to_next, from_prev, from_next = (
        kept_ref[96 + i, 0].astype(jnp.int32) for i in range(6)
    )
    tail = from_prev + live - to_prev - to_next - LANES
    first = jnp.where(even, from_prev, 0)
    final = jnp.where(even, LANES, tail)
    stays_low = jnp.where(even, 0, SPILL + to_next)
    stays_high = jnp.where(even, SPILL - to_prev, 2 * SPILL)
    stays = (lane >= stays_low) & (lane < stays_high)
    arrive_by = jnp.where(even, from_prev - 64, tail)
    band_by = jnp.where(even, from_prev - to_prev - SPILL, SPILL + to_next - from_next)
    for a in range(3):
        for t in range(TILES):
            h = 64 * (t // 4)
            far = far_ref[pl.ds(32 * a + 8 * (t % 4), 8), :]
            arrived = spin(far, arrive_by - h)
            own0 = jnp.where(lane < first, arrived, own_ref[pl.ds(128 * a + 8 * t, 8), :])
            own1 = jnp.where(lane >= final, arrived, own_ref[pl.ds(128 * a + 64 + 8 * t, 8), :])
            at = pl.ds(64 * a + 8 * t, 8)
            band_out[at, :] = jnp.where(stays, spin(far, band_by - h), band_ref[at, :])
            if a < 2:
                for pack in (pack_near, pack_far):
                    pack[pl.ds(128 * a + 8 * t, 8), :] = own0
                    pack[pl.ds(128 * a + 64 + 8 * t, 8), :] = own1
            else:
                coef_out[pl.ds(8 * t, 8), :] = own0
                coef_out[pl.ds(64 + 8 * t, 8), :] = own1
    for r in range(4):
        packed = [
            jnp.where(
                lane < 64,
                band_out[pl.ds(64 * a + 8 * r, 8), :],
                pltpu.roll(band_out[pl.ds(64 * a + 8 * r + 32, 8), :], 64, 1),
            )
            for a in range(2)
        ]
        pack_near[pl.ds(256 + 8 * r, 8), :] = jnp.where(even_group, packed[1], packed[0])
        pack_far[pl.ds(256 + 8 * r, 8), :] = jnp.where(even_group, packed[0], packed[1])

    near_kinds = face_indices(
        [jnp.where(even, pattern_row(pattern_ref, d, 1), pattern_row(pattern_ref, d, 0)) for d in range(6)]
    )
    shift = jnp.where(even, 480, 224)
    window = [
        jnp.broadcast_to(far_ref[pl.ds(104 + d, 1), :], (8, LANES)).astype(jnp.int32) - shift
        for d in range(6)
    ]
    window = [jnp.where((w >= 0) & (w < 2 * SPILL), w, LANES - 1) for w in window]
    far_kinds = [(w,) for w in face_rows(window)]
    far_low, far_high = jnp.where(even, 0, SPILL), jnp.where(even, SPILL, 2 * SPILL)
    far_lanes = (lane >= far_low) & (lane < far_high)
    mine = (lane < 2 * SPILL) & jnp.logical_not(far_lanes)
    given = far_lanes & (lane >= SPILL - to_prev) & (lane < SPILL + to_next)
    unpack_by = jnp.where(even, 0, 32)
    for a in range(2):

        def read(c, t):
            if c < 2:
                return pack_near[pl.ds(128 * a + 64 * c + 8 * t, 8), :]
            return band_out[pl.ds(64 * a + 8 * t, 8), :]

        src = Sources(read)
        here = [jnp.where(even, src.tile[1][t], src.tile[0][t]) for t in range(TILES)]
        turned = [jnp.where(even, src.turned[1][t], src.turned[0][t]) for t in range(TILES)]
        total = neighbour_sum(src, here, turned, near_kinds)
        for half in range(2):
            sum_near[pl.ds(16 * a + 8 * half, 8), :] = pack_quarters(total, half, jnp.logical_not(even))

        def meet(_, t):
            facing = spin(jnp.where(even, src.tile[0][t], src.tile[1][t]), 32)
            return jnp.where(given, src.tile[2][t], jnp.where(mine, facing, 0.0))

        joint = Sources(meet, 1)
        total = neighbour_sum(joint, joint.tile[0], joint.turned[0], far_kinds)
        for t in range(TILES):
            part = far_ref[pl.ds(112 + 16 * a + 8 * (t % 2), 8), :]
            part = spin(part, unpack_by - 32 * (t // 2))
            sum_far[pl.ds(64 * a + 8 * t, 8), :] = jnp.where(far_lanes, total[t] + part, 0.0)


def own(ref, a, c, t):
    return ref[pl.ds(128 * a + 64 * c + 8 * t, 8), :]


def own_kinds(pattern_ref):
    return [
        face_indices(
            [
                jnp.broadcast_to(pattern_ref[pl.ds(d, 1), pl.ds(LANES * c, LANES)], (8, LANES))
                for d in range(6)
            ]
        )
        for c in range(2)
    ]


def gains(weights, coef):
    spread = weights[0] * coef
    return spread, OMEGA / (6.0 * spread + weights[4])


def bulge(weights, phase):
    return weights[3] * (2.0 * phase - phase * phase * phase)


def own_kernel(layers, table, pattern_ref, pack_ref, coef_ref, band_ref, half_ref):
    group = lax.axis_index("gy")
    kinds = own_kinds(pattern_ref)
    weights = [weights_at(table, group, layers, a) for a in range(2)]
    for a in range(2):
        src = Sources(
            lambda c, t: own(pack_ref, a, c, t) if c < 2 else band_ref[pl.ds(64 * a + 8 * t, 8), :]
        )
        for c in range(2):
            total = neighbour_sum(src, src.tile[c], src.turned[c], kinds[c])
            for t in range(TILES):
                now = src.tile[c][t]
                spread, gain = gains(weights[a], coef_ref[pl.ds(64 * c + 8 * t, 8), :])
                push = spread * total[t] + weights[a][2 - a] * own(pack_ref, 1 - a, c, t)
                if a == 0:
                    push = push + bulge(weights[0], now)
                half_ref[pl.ds(128 * a + 64 * c + 8 * t, 8), :] = (1.0 - OMEGA) * now + gain * push


def relax_kernel(
    layers, table,
    pattern_ref, pack_ref, coef_ref, band_ref, half_ref, side_far, side_near, sum_far, sum_near,
    out_ref, next_own, next_band, next_side,
):
    lane = lanes()
    group = lax.axis_index("gy")
    even = is_even("leaf")
    even_group = is_even("gy")
    unpack_by = jnp.where(even, SPILL, 0)
    near_lanes = (lane >= unpack_by) & (lane < unpack_by + SPILL)
    kinds = own_kinds(pattern_ref)
    w_lower, w_first, w_second, w_upper = (weights_at(table, group, layers, o) for o in (-1, 0, 1, 2))

    def step(weights, now, total, below, above, coef, phase):
        spread, gain = gains(weights, coef)
        push = spread * total + weights[1] * below + weights[2] * above
        if phase is not None:
            push = push + bulge(weights, phase)
        return (1.0 - OMEGA) * now + gain * push

    def beside(upper, at):
        near, far = side_near[at, :], side_far[at, :]
        return jnp.where(even_group, near, far) if upper else jnp.where(even_group, far, near)

    def side(upper, a, c, t):
        return beside(upper, pl.ds(128 * a + 64 * c + 8 * t, 8))

    def side_band(upper, t):
        tile = beside(upper, pl.ds(256 + 8 * (t % 4), 8))
        tile = pltpu.roll(tile, 64, 1) if t >= 4 else tile
        return jnp.where(lane < 64, tile, 0.0)

    for a in range(2):
        weights = w_second if a else w_first
        for c in range(2):
            for t in range(TILES):
                _, gain = gains(weights, coef_ref[pl.ds(64 * c + 8 * t, 8), :])
                missing = weights[1 + a] * side(a, 1 - a, c, t)
                next_own[pl.ds(128 * a + 64 * c + 8 * t, 8), :] = own(half_ref, a, c, t) + gain * missing
        for t in range(TILES):
            now = band_ref[pl.ds(64 * a + 8 * t, 8), :]
            coef = band_ref[pl.ds(128 + 8 * t, 8), :]
            near = sum_near[pl.ds(16 * a + 8 * (t % 2), 8), :]
            near = spin(near, unpack_by - 32 * (t // 2))
            total_t = jnp.where(near_lanes, near, sum_far[pl.ds(64 * a + 8 * t, 8), :])
            if a == 0:
                below, above = side_band(0, t), band_ref[pl.ds(64 + 8 * t, 8), :]
                new = step(w_first, now, total_t, below, above, coef, now)
            else:
                below, above = band_ref[pl.ds(8 * t, 8), :], side_band(1, t)
                new = step(w_second, now, total_t, below, above, coef, None)
            next_band[pl.ds(64 * a + 8 * t, 8), :] = new

    for upper in range(2):
        a = 1 - upper
        src = Sources(lambda c, t: side(upper, a, c, t) if c < 2 else side_band(upper, t))
        for c in range(2):
            total = neighbour_sum(src, src.tile[c], src.turned[c], kinds[c])
            for t in range(TILES):
                coef = coef_ref[pl.ds(64 * c + 8 * t, 8), :]
                if upper:
                    below, above = own(pack_ref, 1, c, t), side(1, 1, c, t)
                    new = step(w_upper, src.tile[c][t], total[t], below, above, coef, None)
                else:
                    below, above = side(0, 0, c, t), own(pack_ref, 0, c, t)
                    new = step(w_lower, src.tile[c][t], total[t], below, above, coef, None)
                next_side[pl.ds(128 * upper + 64 * c + 8 * t, 8), :] = new

    for a in range(2):
        src = Sources(
            lambda c, t: own(next_own, a, c, t) if c < 2 else next_band[pl.ds(64 * a + 8 * t, 8), :]
        )
        for c in range(2):
            total = neighbour_sum(src, src.tile[c], src.turned[c], kinds[c])
            for t in range(TILES):
                coef = coef_ref[pl.ds(64 * c + 8 * t, 8), :]
                now = src.tile[c][t]
                if a == 0:
                    below, above = own(next_side, 0, c, t), own(next_own, 1, c, t)
                    new = step(w_first, now, total[t], below, above, coef, own(pack_ref, 0, c, t))
                else:
                    below, above = own(next_own, 0, c, t), own(next_side, 1, c, t)
                    new = step(w_second, now, total[t], below, above, coef, None)
                out_ref[a, pl.ds(8 * t, 8), pl.ds(LANES * c, LANES)] = new


def swap(block, axis, first):
    route = []
    for i in range(first, lax.axis_size(axis) - 1, 2):
        route += [(i, i + 1), (i + 1, i)]
    return lax.ppermute(block, axis, route)


def call(kernel, shapes, spaces, *operands, scratch=(), flops=0):
    vmem = pltpu.VMEM
    space = {"h": pltpu.HBM, "v": vmem, "s": pltpu.SMEM}
    moved = sum(4 * int(np.prod(o.shape)) for o in operands)
    return pl.pallas_call(
        kernel,
        out_shape=[jax.ShapeDtypeStruct(s, F32) for s in shapes],
        in_specs=[pl.BlockSpec(memory_space=space[s]) for s in spaces],
        out_specs=[pl.BlockSpec(memory_space=vmem) for _ in shapes],
        scratch_shapes=list(scratch),
        compiler_params=pltpu.CompilerParams(vmem_limit_bytes=16 * 2**20),
        cost_estimate=pl.CostEstimate(flops=flops, bytes_accessed=moved, transcendentals=0),
    )(*operands)


def local(table, field_old, coef_old, owner, counts, pattern):
    layers = field_old.shape[0]
    stored = [pltpu.with_memory_space_constraint(x, pltpu.HBM) for x in (field_old, coef_old, owner)]
    to_near, field, coef = call(
        near_kernel,
        [(104, LANES), field_old.shape, coef_old.shape],
        "hhhs",
        *stored, counts,
        scratch=[pltpu.SMEM((OLD_SLOTS,), jnp.int32), pltpu.SemaphoreType.DMA((3,))],
    )
    from_near = swap(to_near, "leaf", 0)
    to_far, own_part, band_part = call(
        far_kernel,
        [(144, LANES), (384, LANES), (192, LANES)],
        "vvvvv",
        field, coef, pattern, to_near, from_near,
    )
    from_far = swap(to_far, "leaf", 1)
    pack, pack_far, coef, band, sum_near, sum_far = call(
        place_kernel,
        [(288, LANES), (288, LANES), (128, LANES), (192, LANES), (32, LANES), (128, LANES)],
        "vvvvv",
        pattern, to_far, own_part, band_part, from_far,
    )
    side_near = swap(pack, "gy", 0)
    side_far = swap(pack_far, "gy", 1)
    sum_near = swap(sum_near, "leaf", 0)
    (half,) = call(
        functools.partial(own_kernel, layers, table),
        [(256, LANES)],
        "vvvv",
        pattern, pack, coef, band,
    )
    (out,) = call(
        functools.partial(relax_kernel, layers, table),
        [(layers, 64, BRICKS_DEV)],
        "vvvvvvvvv",
        pattern, pack, coef, band, half, side_far, side_near, sum_far, sum_near,
        scratch=[pltpu.VMEM((rows, LANES), F32) for rows in (256, 128, 256)],
    )
    return out


def solution(mesh):
    layers = Y // mesh.shape["gy"]
    return jax.shard_map(
        functools.partial(local, weight_table(layers)),
        mesh=mesh,
        in_specs=(P("gy", None, "leaf"), P(None, "leaf"), P("leaf"), P("leaf"), P(None, "leaf")),
        out_specs=P("gy", None, "leaf"),
        check_vma=False,
    )
```

```python
import functools

import jax
import jax.numpy as jnp
import numpy as np
from jax import lax
from jax.experimental import pallas as pl
from jax.experimental.pallas import tpu as pltpu
from jax.sharding import PartitionSpec as P

BRICKS_DEV = 256
SPILL = 32
Y = 8
OLD_SLOTS = 320
EXPONENT = 0.5
HEIGHT = 8.0
OMEGA = 0.8

F32 = jnp.float32
LANES = 128
TILES = 8
GATHER = lax.GatherDimensionNumbers(
    offset_dims=(),
    collapsed_slice_dims=(1,),
    start_index_map=(1,),
    operand_batching_dims=(0,),
    start_indices_batching_dims=(0,),
)


def weight_table(layers):
    rows = []
    for level in range(-1, Y + 1):
        if not 0 <= level < Y:
            rows.append((0.0, 0.0, 0.0, 0.0, 1.0))
            continue
        y_here = HEIGHT * (level / Y) ** 2
        y_next = HEIGHT * ((level + 1) / Y) ** 2
        y_prev = HEIGHT * ((level - 1) / Y) ** 2
        step_up, step_down = y_next - y_here, y_here - y_prev
        up_weight = ((y_here + y_next) * 0.5) ** EXPONENT
        down_weight = ((y_here + y_prev) * 0.5) ** EXPONENT
        has_lower = float(level > 0)
        up_link = up_weight / step_up
        down_link = has_lower * down_weight / step_down
        planar = 0.5 * (up_weight * step_up + has_lower * down_weight * step_down)
        surface = float(level == 0)
        rows.append((planar, down_link, up_link, surface, down_link + up_link + surface))
    return np.asarray(rows, np.float32)


def weights_at(table, group, layers, offset):
    groups = Y // layers
    out = []
    for column in range(5):
        value = F32(table[offset + 1, column])
        for g in range(1, groups):
            value = jnp.where(group == g, F32(table[g * layers + offset + 1, column]), value)
        out.append(value)
    return out


def lanes():
    return lax.broadcasted_iota(jnp.int32, (8, LANES), 1)


def rows():
    return lax.broadcasted_iota(jnp.int32, (8, LANES), 0)


def spin(tile, shift):
    if isinstance(shift, int):
        return pltpu.roll(tile, shift % LANES, 1) if shift % LANES else tile
    return pltpu.roll(tile, jnp.bitwise_and(shift, LANES - 1), 1)


def pick(tile, index):
    return lax.gather(
        tile,
        index[:, :, None],
        GATHER,
        (1, 1),
        mode=lax.GatherScatterMode.PROMISE_IN_BOUNDS,
    )


def spill_counts(owner_ref, live_count, device):
    to_prev = jnp.int32(0)
    to_next = jnp.int32(0)
    for step in (32, 16, 8, 4, 2, 1):
        near = jnp.minimum(to_prev + step, SPILL)
        hit = (to_prev + step <= SPILL) & (owner_ref[near - 1] < device)
        to_prev = jnp.where(hit, to_prev + step, to_prev)
        near = jnp.minimum(to_next + step, SPILL)
        hit = (to_next + step <= SPILL) & (owner_ref[live_count - near] > device)
        to_next = jnp.where(hit, to_next + step, to_next)
    return to_prev, to_next


def old_tile(ref, lead, t, c):
    at = (lead, pl.ds(8 * t, 8)) if lead is not None else (pl.ds(8 * t, 8),)
    if c < 2:
        return ref[at + (pl.ds(LANES * c, LANES),)]
    half = ref[at + (pl.ds(2 * LANES, OLD_SLOTS - 2 * LANES),)]
    return jnp.concatenate([half, jnp.zeros((8, 3 * LANES - OLD_SLOTS), F32)], axis=1)


def face_rows(pattern_rows):
    sub = rows()
    return (
        pattern_rows[0],
        pattern_rows[1],
        jnp.where(sub < 4, pattern_rows[3], pattern_rows[2]),
        jnp.where((sub & 3) == 3, pattern_rows[4], pattern_rows[5]),
    )


def face_indices(pattern_rows):
    out = []
    for w in face_rows(pattern_rows):
        source = w >> 7
        own = (source == 2) | (source == 3)
        beside = jnp.where(w >= 2 * BRICKS_DEV, w - (2 * BRICKS_DEV - SPILL), w - (BRICKS_DEV - SPILL))
        lane = jnp.where(own, w & (LANES - 1), jnp.where(w >= BRICKS_DEV - SPILL, beside, LANES - 1))
        out.append((lane, source == 2, source == 3))
    return out


def face(kind, tiles):
    if len(tiles) == 1:
        return pick(tiles[0], kind[0])
    lane, first, second = kind
    return jnp.where(first, pick(tiles[0], lane), jnp.where(second, pick(tiles[1], lane), pick(tiles[2], lane)))


class Sources:
    def __init__(self, read, count=3):
        sub = rows()
        self.columns = range(count)
        self.tile = [[read(c, t) for t in range(TILES)] for c in self.columns]
        self.turned = [[pltpu.roll(v, 4, 0) for v in column] for column in self.tile]
        self.y_edge = [
            [jnp.where(sub < 4, column[2 * i], column[2 * i + 1]) for i in range(4)]
            for column in self.tile
        ]


def neighbour_sum(src, here, turned, kinds):
    sub = rows()
    low, k = sub < 4, sub & 3
    x_low, x_high, y_both, z_both = kinds
    total = []
    for t in range(TILES):
        if t < 2:
            below = face(x_low, [src.tile[c][6 + t] for c in src.columns])
        else:
            below = here[t - 2]
        if t >= 6:
            above = face(x_high, [src.tile[c][t - 6] for c in src.columns])
        else:
            above = here[t + 2]
        total.append(below + above)
    for i in range(4):
        edge = pltpu.roll(face(y_both, [src.y_edge[c][i] for c in src.columns]), 4, 0)
        first, second = turned[2 * i], turned[2 * i + 1]
        middle = jnp.where(low, first, second)
        total[2 * i] += jnp.where(low, edge, first) + middle
        total[2 * i + 1] += jnp.where(low, second, edge) + middle
    for t in range(TILES):
        edge = face(z_both, [src.turned[c][t] for c in src.columns])
        total[t] += pltpu.roll(jnp.where(k == 3, edge, here[t]), 1, 0)
        total[t] += pltpu.roll(jnp.where(k == 0, edge, here[t]), 7, 0)
    return total


def is_even(axis):
    return (lax.axis_index(axis) & 1) == 0


def ends(ref, lead, r, live, next_side):
    lane = lanes()
    front, back = old_tile(ref, lead, r, 0), old_tile(ref, lead, r + 4, 0)
    prev = jnp.where(lane < 64, front, pltpu.roll(back, 64, 1))
    early = lane >= live - 192
    front = jnp.where(early, old_tile(ref, lead, r, 1), old_tile(ref, lead, r, 2))
    back = jnp.where(early, old_tile(ref, lead, r + 4, 1), old_tile(ref, lead, r + 4, 2))
    next = jnp.where(lane < 64, spin(front, 64 - live), spin(back, 128 - live))
    return jnp.where(next_side, next, prev)


def near_kernel(
    field_hbm, coef_hbm, owner_hbm, counts_ref, near_ref, field_ref, coef_ref, owner_ref, sems
):
    pairs = ((owner_hbm, owner_ref), (field_hbm, field_ref), (coef_hbm, coef_ref))
    copies = [pltpu.make_async_copy(a, b, sems.at[i]) for i, (a, b) in enumerate(pairs)]
    for copy in copies:
        copy.start()
    sub = rows()
    even = is_even("leaf")
    live = counts_ref[0]
    copies[0].wait()
    to_prev, to_next = spill_counts(owner_ref, live, lax.axis_index("leaf"))
    handed = jnp.where(even, to_next, to_prev)
    kept = jnp.where(sub == 1, live, jnp.where(sub == 2, to_prev, to_next))
    near_ref[pl.ds(96, 8), :] = jnp.where(sub == 0, handed, kept).astype(F32)
    for a in range(3):
        ref, lead = (field_ref, a) if a < 2 else (coef_ref, None)
        if a != 1:
            copies[1 + a // 2].wait()
        for r in range(4):
            near_ref[pl.ds(32 * a + 8 * r, 8), :] = ends(ref, lead, r, live, even)


def pattern_row(pattern_ref, direction, c):
    row = pattern_ref[pl.ds(direction, 1), pl.ds(LANES * c, LANES)]
    return jnp.broadcast_to(row, (8, LANES))


def pack_quarters(total, half, first):
    lane = lanes()
    base = jnp.where(first, 0, 32)
    q = [spin(total[2 * i + half], base + 32 * i) for i in range(4)]
    return jnp.where(
        lane < 64, jnp.where(lane < 32, q[0], q[1]), jnp.where(lane < 96, q[2], q[3])
    )


def ready_kernel(field_ref, coef_ref, kept_ref, ends_ref, gone_ref):
    lane = lanes()
    even = is_even("leaf")
    live, to_prev, to_next = (kept_ref[96 + i, 0].astype(jnp.int32) for i in (1, 2, 3))
    for a in range(3):
        ref, lead = (field_ref, a) if a < 2 else (coef_ref, None)
        for r in range(4):
            ends_ref[pl.ds(32 * a + 8 * r, 8), :] = ends(ref, lead, r, live, jnp.logical_not(even))
        for t in range(TILES):
            x0, x1, x2 = (old_tile(ref, lead, t, c) for c in range(3))
            last = jnp.where(lane >= live - to_next - LANES, x1, x2)
            gone_ref[pl.ds(64 * a + 8 * t, 8), :] = jnp.where(
                lane < SPILL, spin(x0, SPILL - to_prev), spin(last, SPILL + to_next - live)
            )


def far_kernel(
    field_ref, coef_ref, pattern_ref, kept_ref, ends_ref, gone_ref, near_ref, far_ref, own_ref, band_ref
):
    lane, sub = lanes(), rows()
    even = is_even("leaf")
    live, to_prev, to_next = (kept_ref[96 + i, 0].astype(jnp.int32) for i in (1, 2, 3))
    from_near = near_ref[96, 0].astype(jnp.int32)
    stay = live - to_prev - to_next
    from_far = BRICKS_DEV - stay - from_near
    from_prev, from_next = jnp.where(even, from_far, from_near), jnp.where(even, from_near, from_far)
    drift = to_prev - from_prev
    tail = from_prev + stay - LANES
    handed = jnp.where(even, to_prev, to_next)
    values = (handed, live, to_prev, to_next, from_prev, from_next, 0, 0)
    counts = jnp.zeros((8, LANES), jnp.int32)
    for i, value in enumerate(values):
        counts = jnp.where(sub == i, value, counts)
    far_ref[pl.ds(96, 8), :] = counts.astype(F32)
    spill = (lane >= SPILL - to_prev) & (lane < SPILL + to_next)
    near_low, near_high = jnp.where(even, SPILL, 0), jnp.where(even, 2 * SPILL, SPILL)
    near_lanes = (lane >= near_low) & (lane < near_high)
    arrive_by = jnp.where(even, tail, from_prev - 64)
    band_by = jnp.where(even, SPILL + to_next - from_next, from_prev - to_prev - SPILL)
    for a in range(3):
        ref, lead = (field_ref, a) if a < 2 else (coef_ref, None)
        for r in range(4):
            at = pl.ds(32 * a + 8 * r, 8)
            far_ref[at, :] = ends_ref[at, :]
        for t in range(TILES):
            h = 64 * (t // 4)
            near = near_ref[pl.ds(32 * a + 8 * (t % 4), 8), :]
            x0, x1, x2 = (old_tile(ref, lead, t, c) for c in range(3))
            r0, r1, r2 = spin(x0, -drift), spin(x1, -drift), spin(x2, -drift)
            own0 = jnp.where(lane < LANES - drift, r0, r1)
            own1 = jnp.where(lane < -drift, r0, jnp.where(lane < LANES - drift, r1, r2))
            arrived = spin(near, arrive_by - h)
            own0 = jnp.where(lane < from_prev, jnp.where(even, 0.0, arrived), own0)
            own1 = jnp.where(lane >= tail, jnp.where(even, arrived, 0.0), own1)
            gone = gone_ref[pl.ds(64 * a + 8 * t, 8), :]
            band = jnp.where(spill, gone, jnp.where(near_lanes, spin(near, band_by - h), 0.0))
            own_ref[pl.ds(128 * a + 8 * t, 8), :] = own0
            own_ref[pl.ds(128 * a + 64 + 8 * t, 8), :] = own1
            band_ref[pl.ds(64 * a + 8 * t, 8), :] = band
    far_rows = [
        jnp.where(even, pattern_row(pattern_ref, d, 0), pattern_row(pattern_ref, d, 1)) for d in range(6)
    ]
    sent = jnp.zeros((8, LANES), jnp.int32)
    for d in range(6):
        row = spin(far_rows[d], jnp.where(even, 0, 32))
        sent = jnp.where(sub == d, row, sent)
    sent = jnp.where(lane < 32, sent, pltpu.roll(sent, 32, 1))
    far_ref[pl.ds(104, 8), :] = sent.astype(F32)
    kinds = face_indices(far_rows)
    for a in range(2):

        def read(c, t):
            if c < 2:
                return own_ref[pl.ds(128 * a + 64 * c + 8 * t, 8), :]
            return jnp.where(near_lanes, band_ref[pl.ds(64 * a + 8 * t, 8), :], 0.0)

        src = Sources(read)
        here = [jnp.where(even, src.tile[0][t], src.tile[1][t]) for t in range(TILES)]
        turned = [jnp.where(even, src.turned[0][t], src.turned[1][t]) for t in range(TILES)]
        total = neighbour_sum(src, here, turned, kinds)
        for half in range(2):
            far_ref[pl.ds(112 + 16 * a + 8 * half, 8), :] = pack_quarters(total, half, even)


def place_kernel(
    kept_ref, own_ref, band_ref, far_ref, pack_near, pack_far, coef_out, band_out
):
    lane = lanes()
    even = is_even("leaf")
    even_group = is_even("gy")
    _, live, to_prev, to_next, from_prev, from_next = (
        kept_ref[96 + i, 0].astype(jnp.int32) for i in range(6)
    )
    tail = from_prev + live - to_prev - to_next - LANES
    first = jnp.where(even, from_prev, 0)
    final = jnp.where(even, LANES, tail)
    stays_low = jnp.where(even, 0, SPILL + to_next)
    stays_high = jnp.where(even, SPILL - to_prev, 2 * SPILL)
    stays = (lane >= stays_low) & (lane < stays_high)
    arrive_by = jnp.where(even, from_prev - 64, tail)
    band_by = jnp.where(even, from_prev - to_prev - SPILL, SPILL + to_next - from_next)
    for a in range(3):
        for t in range(TILES):
            h = 64 * (t // 4)
            far = far_ref[pl.ds(32 * a + 8 * (t % 4), 8), :]
            arrived = spin(far, arrive_by - h)
            own0 = jnp.where(lane < first, arrived, own_ref[pl.ds(128 * a + 8 * t, 8), :])
            own1 = jnp.where(lane >= final, arrived, own_ref[pl.ds(128 * a + 64 + 8 * t, 8), :])
            at = pl.ds(64 * a + 8 * t, 8)
            band_out[at, :] = jnp.where(stays, spin(far, band_by - h), band_ref[at, :])
            if a < 2:
                for pack in (pack_near, pack_far):
                    pack[pl.ds(128 * a + 8 * t, 8), :] = own0
                    pack[pl.ds(128 * a + 64 + 8 * t, 8), :] = own1
            else:
                coef_out[pl.ds(8 * t, 8), :] = own0
                coef_out[pl.ds(64 + 8 * t, 8), :] = own1
    for r in range(4):
        packed = [
            jnp.where(
                lane < 64,
                band_out[pl.ds(64 * a + 8 * r, 8), :],
                pltpu.roll(band_out[pl.ds(64 * a + 8 * r + 32, 8), :], 64, 1),
            )
            for a in range(2)
        ]
        pack_near[pl.ds(256 + 8 * r, 8), :] = jnp.where(even_group, packed[1], packed[0])
        pack_far[pl.ds(256 + 8 * r, 8), :] = jnp.where(even_group, packed[0], packed[1])


def facing_kernel(
    pattern_ref, kept_ref, far_ref, pack_ref, band_ref, sum_near, sum_far
):
    lane = lanes()
    even = is_even("leaf")
    to_prev, to_next = (kept_ref[96 + i, 0].astype(jnp.int32) for i in (2, 3))
    near_kinds = face_indices(
        [jnp.where(even, pattern_row(pattern_ref, d, 1), pattern_row(pattern_ref, d, 0)) for d in range(6)]
    )
    shift = jnp.where(even, 480, 224)
    window = [
        jnp.broadcast_to(far_ref[pl.ds(104 + d, 1), :], (8, LANES)).astype(jnp.int32) - shift
        for d in range(6)
    ]
    window = [jnp.where((w >= 0) & (w < 2 * SPILL), w, LANES - 1) for w in window]
    far_kinds = [(w,) for w in face_rows(window)]
    far_low, far_high = jnp.where(even, 0, SPILL), jnp.where(even, SPILL, 2 * SPILL)
    far_lanes = (lane >= far_low) & (lane < far_high)
    mine = (lane < 2 * SPILL) & jnp.logical_not(far_lanes)
    given = far_lanes & (lane >= SPILL - to_prev) & (lane < SPILL + to_next)
    unpack_by = jnp.where(even, 0, 32)
    for a in range(2):

        def read(c, t):
            if c < 2:
                return pack_ref[pl.ds(128 * a + 64 * c + 8 * t, 8), :]
            return band_ref[pl.ds(64 * a + 8 * t, 8), :]

        src = Sources(read)
        here = [jnp.where(even, src.tile[1][t], src.tile[0][t]) for t in range(TILES)]
        turned = [jnp.where(even, src.turned[1][t], src.turned[0][t]) for t in range(TILES)]
        total = neighbour_sum(src, here, turned, near_kinds)
        for half in range(2):
            sum_near[pl.ds(16 * a + 8 * half, 8), :] = pack_quarters(total, half, jnp.logical_not(even))

        def meet(_, t):
            facing = spin(jnp.where(even, src.tile[0][t], src.tile[1][t]), 32)
            return jnp.where(given, src.tile[2][t], jnp.where(mine, facing, 0.0))

        joint = Sources(meet, 1)
        total = neighbour_sum(joint, joint.tile[0], joint.turned[0], far_kinds)
        for t in range(TILES):
            part = far_ref[pl.ds(112 + 16 * a + 8 * (t % 2), 8), :]
            part = spin(part, unpack_by - 32 * (t // 2))
            sum_far[pl.ds(64 * a + 8 * t, 8), :] = jnp.where(far_lanes, total[t] + part, 0.0)


def own(ref, a, c, t):
    return ref[pl.ds(128 * a + 64 * c + 8 * t, 8), :]


def own_kinds(pattern_ref):
    return [
        face_indices(
            [
                jnp.broadcast_to(pattern_ref[pl.ds(d, 1), pl.ds(LANES * c, LANES)], (8, LANES))
                for d in range(6)
            ]
        )
        for c in range(2)
    ]


def gains(weights, coef):
    spread = weights[0] * coef
    return spread, OMEGA / (6.0 * spread + weights[4])


def bulge(weights, phase):
    return weights[3] * (2.0 * phase - phase * phase * phase)


def own_kernel(layers, table, pattern_ref, pack_ref, coef_ref, band_ref, half_ref):
    group = lax.axis_index("gy")
    kinds = own_kinds(pattern_ref)
    weights = [weights_at(table, group, layers, a) for a in range(2)]
    for a in range(2):
        src = Sources(
            lambda c, t: own(pack_ref, a, c, t) if c < 2 else band_ref[pl.ds(64 * a + 8 * t, 8), :]
        )
        for c in range(2):
            total = neighbour_sum(src, src.tile[c], src.turned[c], kinds[c])
            for t in range(TILES):
                now = src.tile[c][t]
                spread, gain = gains(weights[a], coef_ref[pl.ds(64 * c + 8 * t, 8), :])
                push = spread * total[t] + weights[a][2 - a] * own(pack_ref, 1 - a, c, t)
                if a == 0:
                    push = push + bulge(weights[0], now)
                half_ref[pl.ds(128 * a + 64 * c + 8 * t, 8), :] = (1.0 - OMEGA) * now + gain * push


def side_kernel(
    layers, table, final,
    pattern_ref, pack_ref, coef_ref, band_ref, half_ref, side_ref, sum_near, sum_far, *refs,
):
    if final:
        other_once, other_twice, out_ref, next_own, next_band, next_side = refs
    else:
        next_own, twice_ref, next_band, next_side = refs
    lane = lanes()
    group = lax.axis_index("gy")
    even = is_even("leaf")
    upper = is_even("gy") if final else jnp.logical_not(is_even("gy"))
    a = jnp.where(upper, 1, 0)
    unpack_by = jnp.where(even, SPILL, 0)
    near_lanes = (lane >= unpack_by) & (lane < unpack_by + SPILL)
    kinds = own_kinds(pattern_ref)
    w_lower, w_first, w_second, w_upper = (weights_at(table, group, layers, o) for o in (-1, 0, 1, 2))
    w_own = [jnp.where(upper, u, v) for u, v in zip(w_second, w_first)]
    w_side = [jnp.where(upper, u, v) for u, v in zip(w_upper, w_lower)]
    own_to_side, own_to_other = jnp.where(upper, w_own[2], w_own[1]), jnp.where(upper, w_own[1], w_own[2])
    side_to_own, side_to_next = jnp.where(upper, w_side[1], w_side[2]), jnp.where(upper, w_side[2], w_side[1])
    other_link = jnp.where(upper, w_first[2], w_second[1])
    w_other = [jnp.where(upper, u, v) for u, v in zip(w_first, w_second)]

    def at(base, offset):
        return pl.ds(pl.multiple_of(base + offset, 8), 8)

    here, there = 128 * a, 128 * (1 - a)

    def side_band(t):
        tile = side_ref[pl.ds(256 + 8 * (t % 4), 8), :]
        return jnp.where(lane < 64, pltpu.roll(tile, 64, 1) if t >= 4 else tile, 0.0)

    for c in range(2):
        for t in range(TILES):
            k = 64 * c + 8 * t
            _, gain = gains(w_own, coef_ref[pl.ds(k, 8), :])
            next_own[pl.ds(k, 8), :] = (
                half_ref[at(here, k), :] + gain * own_to_side * side_ref[at(there, k), :]
            )
    for t in range(TILES):
        now = band_ref[at(64 * a, 8 * t), :]
        spread, gain = gains(w_own, band_ref[pl.ds(128 + 8 * t, 8), :])
        near = spin(sum_near[at(16 * a, 8 * (t % 2)), :], unpack_by - 32 * (t // 2))
        total = jnp.where(near_lanes, near, sum_far[at(64 * a, 8 * t), :])
        push = spread * total + own_to_side * side_band(t) + bulge(w_own, now)
        push = push + own_to_other * band_ref[at(64 * (1 - a), 8 * t), :]
        next_band[pl.ds(8 * t, 8), :] = (1.0 - OMEGA) * now + gain * push

    src = Sources(lambda c, t: side_ref[at(there, 64 * c + 8 * t), :] if c < 2 else side_band(t))
    for c in range(2):
        total = neighbour_sum(src, src.tile[c], src.turned[c], kinds[c])
        for t in range(TILES):
            k = 64 * c + 8 * t
            spread, gain = gains(w_side, coef_ref[pl.ds(k, 8), :])
            push = spread * total[t] + side_to_own * pack_ref[at(here, k), :]
            push = push + side_to_next * side_ref[at(here, k), :]
            next_side[pl.ds(k, 8), :] = (1.0 - OMEGA) * src.tile[c][t] + gain * push

    src = Sources(
        lambda c, t: next_own[pl.ds(64 * c + 8 * t, 8), :] if c < 2 else next_band[pl.ds(8 * t, 8), :]
    )
    for c in range(2):
        total = neighbour_sum(src, src.tile[c], src.turned[c], kinds[c])
        for t in range(TILES):
            k = 64 * c + 8 * t
            coef = coef_ref[pl.ds(k, 8), :]
            spread, gain = gains(w_own, coef)
            once = src.tile[c][t]
            push = spread * total[t] + own_to_side * next_side[pl.ds(k, 8), :]
            push = push + bulge(w_own, pack_ref[at(here, k), :])
            if not final:
                twice_ref[pl.ds(k, 8), :] = (1.0 - OMEGA) * once + gain * push
                continue
            push = push + own_to_other * other_once[pl.ds(k, 8), :]
            _, other_gain = gains(w_other, coef)
            lanes_at = pl.ds(LANES * c, LANES)
            out_ref[a, pl.ds(8 * t, 8), lanes_at] = (1.0 - OMEGA) * once + gain * push
            out_ref[1 - a, pl.ds(8 * t, 8), lanes_at] = (
                other_twice[pl.ds(k, 8), :] + other_gain * other_link * once
            )


def swap(block, axis, first):
    route = []
    for i in range(first, lax.axis_size(axis) - 1, 2):
        route += [(i, i + 1), (i + 1, i)]
    return lax.ppermute(block, axis, route)


def call(kernel, shapes, spaces, *operands, scratch=(), flops=0):
    vmem = pltpu.VMEM
    space = {"h": pltpu.HBM, "v": vmem, "s": pltpu.SMEM}
    moved = sum(4 * int(np.prod(o.shape)) for o in operands)
    return pl.pallas_call(
        kernel,
        out_shape=[jax.ShapeDtypeStruct(s, F32) for s in shapes],
        in_specs=[pl.BlockSpec(memory_space=space[s]) for s in spaces],
        out_specs=[pl.BlockSpec(memory_space=vmem) for _ in shapes],
        scratch_shapes=list(scratch),
        compiler_params=pltpu.CompilerParams(vmem_limit_bytes=16 * 2**20),
        cost_estimate=pl.CostEstimate(flops=flops, bytes_accessed=moved, transcendentals=0),
    )(*operands)


def local(table, field_old, coef_old, owner, counts, pattern):
    layers = field_old.shape[0]
    stored = [pltpu.with_memory_space_constraint(x, pltpu.HBM) for x in (field_old, coef_old, owner)]
    to_near, field, coef = call(
        near_kernel,
        [(104, LANES), field_old.shape, coef_old.shape],
        "hhhs",
        *stored, counts,
        scratch=[pltpu.SMEM((OLD_SLOTS,), jnp.int32), pltpu.SemaphoreType.DMA((3,))],
    )
    from_near = swap(to_near, "leaf", 0)
    ends_far, gone = call(
        ready_kernel, [(96, LANES), (192, LANES)], "vvv", field, coef, to_near
    )
    to_far, own_part, band_part = call(
        far_kernel,
        [(144, LANES), (384, LANES), (192, LANES)],
        "vvvvvvv",
        field, coef, pattern, to_near, ends_far, gone, from_near,
    )
    from_far = swap(to_far, "leaf", 1)
    pack, pack_far, coef, band = call(
        place_kernel,
        [(288, LANES), (288, LANES), (128, LANES), (192, LANES)],
        "vvvv",
        to_far, own_part, band_part, from_far,
    )
    side_near = swap(pack, "gy", 0)
    side_far = swap(pack_far, "gy", 1)
    sum_near, sum_far = call(
        facing_kernel, [(32, LANES), (128, LANES)], "vvvvv", pattern, to_far, from_far, pack, band
    )
    sum_near = swap(sum_near, "leaf", 0)
    (half,) = call(
        functools.partial(own_kernel, layers, table),
        [(256, LANES)],
        "vvvv",
        pattern, pack, coef, band,
    )
    once, twice = call(
        functools.partial(side_kernel, layers, table, False),
        [(128, LANES), (128, LANES)],
        "vvvvvvvv",
        pattern, pack, coef, band, half, side_far, sum_near, sum_far,
        scratch=[pltpu.VMEM((64, LANES), F32), pltpu.VMEM((128, LANES), F32)],
    )
    (out,) = call(
        functools.partial(side_kernel, layers, table, True),
        [(layers, 64, BRICKS_DEV)],
        "vvvvvvvvvv",
        pattern, pack, coef, band, half, side_near, sum_near, sum_far, once, twice,
        scratch=[pltpu.VMEM((rows, LANES), F32) for rows in (128, 64, 128)],
    )
    return out


def solution(mesh):
    layers = Y // mesh.shape["gy"]
    return jax.shard_map(
        functools.partial(local, weight_table(layers)),
        mesh=mesh,
        in_specs=(P("gy", None, "leaf"), P(None, "leaf"), P("leaf"), P("leaf"), P(None, "leaf")),
        out_specs=P("gy", None, "leaf"),
        check_vma=False,
    )
```

```python
import functools

import jax
import jax.numpy as jnp
import numpy as np
from jax import lax
from jax.experimental import pallas as pl
from jax.experimental.pallas import tpu as pltpu
from jax.sharding import PartitionSpec as P

BRICKS_DEV = 256
SPILL = 32
Y = 8
OLD_SLOTS = 320
EXPONENT = 0.5
HEIGHT = 8.0
OMEGA = 0.8

F32 = jnp.float32
LANES = 128
TILES = 8
GATHER = lax.GatherDimensionNumbers(
    offset_dims=(),
    collapsed_slice_dims=(1,),
    start_index_map=(1,),
    operand_batching_dims=(0,),
    start_indices_batching_dims=(0,),
)


def weight_table(layers):
    rows = []
    for level in range(-1, Y + 1):
        if not 0 <= level < Y:
            rows.append((0.0, 0.0, 0.0, 0.0, 1.0))
            continue
        y_here = HEIGHT * (level / Y) ** 2
        y_next = HEIGHT * ((level + 1) / Y) ** 2
        y_prev = HEIGHT * ((level - 1) / Y) ** 2
        step_up, step_down = y_next - y_here, y_here - y_prev
        up_weight = ((y_here + y_next) * 0.5) ** EXPONENT
        down_weight = ((y_here + y_prev) * 0.5) ** EXPONENT
        has_lower = float(level > 0)
        up_link = up_weight / step_up
        down_link = has_lower * down_weight / step_down
        planar = 0.5 * (up_weight * step_up + has_lower * down_weight * step_down)
        surface = float(level == 0)
        rows.append((planar, down_link, up_link, surface, down_link + up_link + surface))
    return np.asarray(rows, np.float32)


def weights_at(table, group, layers, offset):
    groups = Y // layers
    out = []
    for column in range(5):
        value = F32(table[offset + 1, column])
        for g in range(1, groups):
            value = jnp.where(group == g, F32(table[g * layers + offset + 1, column]), value)
        out.append(value)
    return out


def lanes():
    return lax.broadcasted_iota(jnp.int32, (8, LANES), 1)


def rows():
    return lax.broadcasted_iota(jnp.int32, (8, LANES), 0)


def spin(tile, shift):
    if isinstance(shift, int):
        return pltpu.roll(tile, shift % LANES, 1) if shift % LANES else tile
    return pltpu.roll(tile, jnp.bitwise_and(shift, LANES - 1), 1)


def pick(tile, index):
    return lax.gather(
        tile,
        index[:, :, None],
        GATHER,
        (1, 1),
        mode=lax.GatherScatterMode.PROMISE_IN_BOUNDS,
    )


def spill_counts(owner_ref, live_count, device):
    lane, sub = lanes(), rows()
    hits = jnp.zeros((8, LANES), F32)
    for c in range(3):
        width = min(LANES, OLD_SLOTS - LANES * c)
        row = owner_ref[pl.ds(LANES * c, width)].reshape(1, width)
        if width < LANES:
            row = jnp.concatenate([row, jnp.zeros((1, LANES - width), jnp.int32)], axis=1)
        row = jnp.broadcast_to(row, (8, LANES))
        wanted = device + jnp.where(sub == 0, -1, 1)
        hits += jnp.where((row == wanted) & (lane + LANES * c < live_count), 1.0, 0.0)
    return jnp.sum(hits, axis=1, keepdims=True)


def old_tile(ref, lead, t, c):
    at = (lead, pl.ds(8 * t, 8)) if lead is not None else (pl.ds(8 * t, 8),)
    if c < 2:
        return ref[at + (pl.ds(LANES * c, LANES),)]
    half = ref[at + (pl.ds(2 * LANES, OLD_SLOTS - 2 * LANES),)]
    return jnp.concatenate([half, jnp.zeros((8, 3 * LANES - OLD_SLOTS), F32)], axis=1)


def face_rows(pattern_rows):
    sub = rows()
    return (
        pattern_rows[0],
        pattern_rows[1],
        jnp.where(sub < 4, pattern_rows[3], pattern_rows[2]),
        jnp.where((sub & 3) == 3, pattern_rows[4], pattern_rows[5]),
    )


def face_indices(pattern_rows):
    out = []
    for w in face_rows(pattern_rows):
        source = w >> 7
        own = (source == 2) | (source == 3)
        beside = jnp.where(w >= 2 * BRICKS_DEV, w - (2 * BRICKS_DEV - SPILL), w - (BRICKS_DEV - SPILL))
        lane = jnp.where(own, w & (LANES - 1), jnp.where(w >= BRICKS_DEV - SPILL, beside, LANES - 1))
        out.append((lane, source == 2, source == 3))
    return out


def face(kind, tiles):
    if len(tiles) == 1:
        return pick(tiles[0], kind[0])
    lane, first, second = kind
    return jnp.where(first, pick(tiles[0], lane), jnp.where(second, pick(tiles[1], lane), pick(tiles[2], lane)))


class Sources:
    def __init__(self, read, count=3):
        sub = rows()
        self.columns = range(count)
        self.tile = [[read(c, t) for t in range(TILES)] for c in self.columns]
        self.turned = [[pltpu.roll(v, 4, 0) for v in column] for column in self.tile]
        self.y_edge = [
            [jnp.where(sub < 4, column[2 * i], column[2 * i + 1]) for i in range(4)]
            for column in self.tile
        ]


def neighbour_sum(src, here, turned, kinds):
    sub = rows()
    low, k = sub < 4, sub & 3
    x_low, x_high, y_both, z_both = kinds
    total = []
    for t in range(TILES):
        if t < 2:
            below = face(x_low, [src.tile[c][6 + t] for c in src.columns])
        else:
            below = here[t - 2]
        if t >= 6:
            above = face(x_high, [src.tile[c][t - 6] for c in src.columns])
        else:
            above = here[t + 2]
        total.append(below + above)
    for i in range(4):
        edge = pltpu.roll(face(y_both, [src.y_edge[c][i] for c in src.columns]), 4, 0)
        first, second = turned[2 * i], turned[2 * i + 1]
        middle = jnp.where(low, first, second)
        total[2 * i] += jnp.where(low, edge, first) + middle
        total[2 * i + 1] += jnp.where(low, second, edge) + middle
    for t in range(TILES):
        edge = face(z_both, [src.turned[c][t] for c in src.columns])
        total[t] += pltpu.roll(jnp.where(k == 3, edge, here[t]), 1, 0)
        total[t] += pltpu.roll(jnp.where(k == 0, edge, here[t]), 7, 0)
    return total


def is_even(axis):
    return (lax.axis_index(axis) & 1) == 0


def ends(ref, lead, r, live, next_side):
    lane = lanes()
    front, back = old_tile(ref, lead, r, 0), old_tile(ref, lead, r + 4, 0)
    prev = jnp.where(lane < 64, front, pltpu.roll(back, 64, 1))
    early = lane >= live - 192
    front = jnp.where(early, old_tile(ref, lead, r, 1), old_tile(ref, lead, r, 2))
    back = jnp.where(early, old_tile(ref, lead, r + 4, 1), old_tile(ref, lead, r + 4, 2))
    next = jnp.where(lane < 64, spin(front, 64 - live), spin(back, 128 - live))
    return jnp.where(next_side, next, prev)


def near_kernel(
    field_hbm, coef_hbm, owner_hbm, counts_ref, near_ref, field_ref, coef_ref, owner_ref, sems
):
    pairs = ((owner_hbm, owner_ref), (field_hbm, field_ref), (coef_hbm, coef_ref))
    copies = [pltpu.make_async_copy(a, b, sems.at[i]) for i, (a, b) in enumerate(pairs)]
    for copy in copies:
        copy.start()
    sub = rows()
    even = is_even("leaf")
    live = counts_ref[0]
    copies[0].wait()
    spills = spill_counts(owner_ref, live, lax.axis_index("leaf"))
    to_prev, to_next = (jnp.broadcast_to(spills[i : i + 1], (8, LANES)) for i in range(2))
    kept = jnp.where(sub == 1, live.astype(F32), jnp.where(sub == 2, to_prev, to_next))
    near_ref[pl.ds(96, 8), :] = jnp.where(sub == 0, jnp.where(even, to_next, to_prev), kept)
    for a in range(3):
        ref, lead = (field_ref, a) if a < 2 else (coef_ref, None)
        if a != 1:
            copies[1 + a // 2].wait()
        for r in range(4):
            near_ref[pl.ds(32 * a + 8 * r, 8), :] = ends(ref, lead, r, live, even)


def pattern_row(pattern_ref, direction, c):
    row = pattern_ref[pl.ds(direction, 1), pl.ds(LANES * c, LANES)]
    return jnp.broadcast_to(row, (8, LANES))


def pack_quarters(total, half, first):
    lane = lanes()
    base = jnp.where(first, 0, 32)
    q = [spin(total[2 * i + half], base + 32 * i) for i in range(4)]
    return jnp.where(
        lane < 64, jnp.where(lane < 32, q[0], q[1]), jnp.where(lane < 96, q[2], q[3])
    )


def ready_kernel(field_ref, coef_ref, kept_ref, ends_ref, gone_ref):
    lane = lanes()
    even = is_even("leaf")
    live, to_prev, to_next = (kept_ref[96 + i, 0].astype(jnp.int32) for i in (1, 2, 3))
    for a in range(3):
        ref, lead = (field_ref, a) if a < 2 else (coef_ref, None)
        for r in range(4):
            ends_ref[pl.ds(32 * a + 8 * r, 8), :] = ends(ref, lead, r, live, jnp.logical_not(even))
        for t in range(TILES):
            x0, x1, x2 = (old_tile(ref, lead, t, c) for c in range(3))
            last = jnp.where(lane >= live - to_next - LANES, x1, x2)
            gone_ref[pl.ds(64 * a + 8 * t, 8), :] = jnp.where(
                lane < SPILL, spin(x0, SPILL - to_prev), spin(last, SPILL + to_next - live)
            )


def place_part(sources, counts, gone_ref, near_ref, own_ref, band_ref):
    lane = lanes()
    even = is_even("leaf")
    live, to_prev, to_next, from_prev, from_next = counts
    drift = to_prev - from_prev
    tail = from_prev + live - to_prev - to_next - LANES
    spill = (lane >= SPILL - to_prev) & (lane < SPILL + to_next)
    near_low = jnp.where(even, SPILL, 0)
    near_lanes = (lane >= near_low) & (lane < near_low + SPILL)
    arrive_by = jnp.where(even, tail, from_prev - 64)
    band_by = jnp.where(even, SPILL + to_next - from_next, from_prev - to_prev - SPILL)
    for out, (a, ref, lead) in enumerate(sources):
        for t in range(TILES):
            h = 64 * (t // 4)
            near = near_ref[pl.ds(32 * a + 8 * (t % 4), 8), :]
            x0, x1, x2 = (old_tile(ref, lead, t, c) for c in range(3))
            r0, r1, r2 = spin(x0, -drift), spin(x1, -drift), spin(x2, -drift)
            own0 = jnp.where(lane < LANES - drift, r0, r1)
            own1 = jnp.where(lane < -drift, r0, jnp.where(lane < LANES - drift, r1, r2))
            arrived = spin(near, arrive_by - h)
            own0 = jnp.where(lane < from_prev, jnp.where(even, 0.0, arrived), own0)
            own1 = jnp.where(lane >= tail, jnp.where(even, arrived, 0.0), own1)
            gone = gone_ref[pl.ds(64 * a + 8 * t, 8), :]
            band = jnp.where(spill, gone, jnp.where(near_lanes, spin(near, band_by - h), 0.0))
            own_ref[pl.ds(128 * out + 8 * t, 8), :] = own0
            own_ref[pl.ds(128 * out + 64 + 8 * t, 8), :] = own1
            band_ref[pl.ds(64 * out + 8 * t, 8), :] = band
    return near_lanes


def coef_kernel(coef_ref, kept_ref, gone_ref, near_ref, own_ref, band_ref):
    counts = [kept_ref[96 + i, 0].astype(jnp.int32) for i in range(1, 6)]
    place_part([(2, coef_ref, None)], counts, gone_ref, near_ref, own_ref, band_ref)


def far_kernel(
    field_ref, pattern_ref, kept_ref, ends_ref, gone_ref, near_ref, far_ref, own_ref, band_ref
):
    lane, sub = lanes(), rows()
    even = is_even("leaf")
    live, to_prev, to_next = (kept_ref[96 + i, 0].astype(jnp.int32) for i in (1, 2, 3))
    from_near = near_ref[96, 0].astype(jnp.int32)
    from_far = BRICKS_DEV - (live - to_prev - to_next) - from_near
    from_prev, from_next = jnp.where(even, from_far, from_near), jnp.where(even, from_near, from_far)
    handed = jnp.where(even, to_prev, to_next)
    counts = jnp.zeros((8, LANES), jnp.int32)
    for i, value in enumerate((handed, live, to_prev, to_next, from_prev, from_next)):
        counts = jnp.where(sub == i, value, counts)
    far_ref[pl.ds(96, 8), :] = counts.astype(F32)
    for r in range(12):
        far_ref[pl.ds(8 * r, 8), :] = ends_ref[pl.ds(8 * r, 8), :]
    near_lanes = place_part(
        [(a, field_ref, a) for a in range(2)],
        (live, to_prev, to_next, from_prev, from_next),
        gone_ref, near_ref, own_ref, band_ref,
    )
    far_rows = [
        jnp.where(even, pattern_row(pattern_ref, d, 0), pattern_row(pattern_ref, d, 1)) for d in range(6)
    ]
    sent = jnp.zeros((8, LANES), jnp.int32)
    for d in range(6):
        row = spin(far_rows[d], jnp.where(even, 0, 32))
        sent = jnp.where(sub == d, row, sent)
    sent = jnp.where(lane < 32, sent, pltpu.roll(sent, 32, 1))
    far_ref[pl.ds(104, 8), :] = sent.astype(F32)
    kinds = face_indices(far_rows)
    for a in range(2):

        def read(c, t):
            if c < 2:
                return own_ref[pl.ds(128 * a + 64 * c + 8 * t, 8), :]
            return jnp.where(near_lanes, band_ref[pl.ds(64 * a + 8 * t, 8), :], 0.0)

        src = Sources(read)
        here = [jnp.where(even, src.tile[0][t], src.tile[1][t]) for t in range(TILES)]
        turned = [jnp.where(even, src.turned[0][t], src.turned[1][t]) for t in range(TILES)]
        total = neighbour_sum(src, here, turned, kinds)
        for half in range(2):
            far_ref[pl.ds(112 + 16 * a + 8 * half, 8), :] = pack_quarters(total, half, even)


def place_kernel(
    kept_ref, own_ref, band_ref, coef_own, coef_band, far_ref, pack_near, pack_far, coef_out, band_out
):
    lane = lanes()
    even = is_even("leaf")
    even_group = is_even("gy")
    _, live, to_prev, to_next, from_prev, from_next = (
        kept_ref[96 + i, 0].astype(jnp.int32) for i in range(6)
    )
    tail = from_prev + live - to_prev - to_next - LANES
    first = jnp.where(even, from_prev, 0)
    final = jnp.where(even, LANES, tail)
    stays_low = jnp.where(even, 0, SPILL + to_next)
    stays_high = jnp.where(even, SPILL - to_prev, 2 * SPILL)
    stays = (lane >= stays_low) & (lane < stays_high)
    arrive_by = jnp.where(even, from_prev - 64, tail)
    band_by = jnp.where(even, from_prev - to_prev - SPILL, SPILL + to_next - from_next)
    for a in range(3):
        for t in range(TILES):
            h = 64 * (t // 4)
            far = far_ref[pl.ds(32 * a + 8 * (t % 4), 8), :]
            arrived = spin(far, arrive_by - h)
            part, side, b = (own_ref, band_ref, a) if a < 2 else (coef_own, coef_band, 0)
            own0 = jnp.where(lane < first, arrived, part[pl.ds(128 * b + 8 * t, 8), :])
            own1 = jnp.where(lane >= final, arrived, part[pl.ds(128 * b + 64 + 8 * t, 8), :])
            band = jnp.where(stays, spin(far, band_by - h), side[pl.ds(64 * b + 8 * t, 8), :])
            band_out[pl.ds(64 * a + 8 * t, 8), :] = band
            if a < 2:
                for pack in (pack_near, pack_far):
                    pack[pl.ds(128 * a + 8 * t, 8), :] = own0
                    pack[pl.ds(128 * a + 64 + 8 * t, 8), :] = own1
            else:
                coef_out[pl.ds(8 * t, 8), :] = own0
                coef_out[pl.ds(64 + 8 * t, 8), :] = own1
    for r in range(4):
        packed = [
            jnp.where(
                lane < 64,
                band_out[pl.ds(64 * a + 8 * r, 8), :],
                pltpu.roll(band_out[pl.ds(64 * a + 8 * r + 32, 8), :], 64, 1),
            )
            for a in range(2)
        ]
        pack_near[pl.ds(256 + 8 * r, 8), :] = jnp.where(even_group, packed[1], packed[0])
        pack_far[pl.ds(256 + 8 * r, 8), :] = jnp.where(even_group, packed[0], packed[1])


def facing_kernel(pattern_ref, pack_ref, band_ref, sum_near):
    even = is_even("leaf")
    kinds = face_indices(
        [jnp.where(even, pattern_row(pattern_ref, d, 1), pattern_row(pattern_ref, d, 0)) for d in range(6)]
    )
    for a in range(2):
        src = Sources(
            lambda c, t: own(pack_ref, a, c, t) if c < 2 else band_ref[pl.ds(64 * a + 8 * t, 8), :]
        )
        here = [jnp.where(even, src.tile[1][t], src.tile[0][t]) for t in range(TILES)]
        turned = [jnp.where(even, src.turned[1][t], src.turned[0][t]) for t in range(TILES)]
        total = neighbour_sum(src, here, turned, kinds)
        for half in range(2):
            sum_near[pl.ds(16 * a + 8 * half, 8), :] = pack_quarters(total, half, jnp.logical_not(even))


def far_sums(kept_ref, far_ref, pack_ref, band_ref, sum_far):
    lane = lanes()
    even = is_even("leaf")
    to_prev, to_next = (kept_ref[96 + i, 0].astype(jnp.int32) for i in (2, 3))
    shift = jnp.where(even, 480, 224)
    window = [
        jnp.broadcast_to(far_ref[pl.ds(104 + d, 1), :], (8, LANES)).astype(jnp.int32) - shift
        for d in range(6)
    ]
    window = [jnp.where((w >= 0) & (w < 2 * SPILL), w, LANES - 1) for w in window]
    kinds = [(w,) for w in face_rows(window)]
    far_low = jnp.where(even, 0, SPILL)
    far_lanes = (lane >= far_low) & (lane < far_low + SPILL)
    mine = (lane < 2 * SPILL) & jnp.logical_not(far_lanes)
    given = far_lanes & (lane >= SPILL - to_prev) & (lane < SPILL + to_next)
    for a in range(2):

        def meet(_, t):
            facing = spin(jnp.where(even, own(pack_ref, a, 0, t), own(pack_ref, a, 1, t)), 32)
            return jnp.where(given, band_ref[pl.ds(64 * a + 8 * t, 8), :], jnp.where(mine, facing, 0.0))

        joint = Sources(meet, 1)
        total = neighbour_sum(joint, joint.tile[0], joint.turned[0], kinds)
        for t in range(TILES):
            part = far_ref[pl.ds(112 + 16 * a + 8 * (t % 2), 8), :]
            part = spin(part, far_low - 32 * (t // 2))
            sum_far[pl.ds(64 * a + 8 * t, 8), :] = jnp.where(far_lanes, total[t] + part, 0.0)


def own(ref, a, c, t):
    return ref[pl.ds(128 * a + 64 * c + 8 * t, 8), :]


def own_kinds(pattern_ref):
    return [
        face_indices(
            [
                jnp.broadcast_to(pattern_ref[pl.ds(d, 1), pl.ds(LANES * c, LANES)], (8, LANES))
                for d in range(6)
            ]
        )
        for c in range(2)
    ]


def gains(weights, coef):
    spread = weights[0] * coef
    return spread, OMEGA / (6.0 * spread + weights[4])


def bulge(weights, phase):
    return weights[3] * (2.0 * phase - phase * phase * phase)


def own_kernel(
    layers, table, pattern_ref, pack_ref, coef_ref, band_ref, kept_ref, far_ref, half_ref, sum_far
):
    far_sums(kept_ref, far_ref, pack_ref, band_ref, sum_far)
    group = lax.axis_index("gy")
    kinds = own_kinds(pattern_ref)
    weights = [weights_at(table, group, layers, a) for a in range(2)]
    for a in range(2):
        src = Sources(
            lambda c, t: own(pack_ref, a, c, t) if c < 2 else band_ref[pl.ds(64 * a + 8 * t, 8), :]
        )
        for c in range(2):
            total = neighbour_sum(src, src.tile[c], src.turned[c], kinds[c])
            for t in range(TILES):
                now = src.tile[c][t]
                spread, gain = gains(weights[a], coef_ref[pl.ds(64 * c + 8 * t, 8), :])
                push = spread * total[t] + weights[a][2 - a] * own(pack_ref, 1 - a, c, t)
                if a == 0:
                    push = push + bulge(weights[0], now)
                half_ref[pl.ds(128 * a + 64 * c + 8 * t, 8), :] = (1.0 - OMEGA) * now + gain * push


def side_kernel(
    layers, table, final,
    pattern_ref, pack_ref, coef_ref, band_ref, half_ref, side_ref, sum_near, sum_far, *refs,
):
    if final:
        other_once, other_twice, out_ref, next_own, next_band, next_side = refs
    else:
        next_own, twice_ref, next_band, next_side = refs
    lane = lanes()
    group = lax.axis_index("gy")
    even = is_even("leaf")
    upper = is_even("gy") if final else jnp.logical_not(is_even("gy"))
    a = jnp.where(upper, 1, 0)
    unpack_by = jnp.where(even, SPILL, 0)
    near_lanes = (lane >= unpack_by) & (lane < unpack_by + SPILL)
    kinds = own_kinds(pattern_ref)
    w_lower, w_first, w_second, w_upper = (weights_at(table, group, layers, o) for o in (-1, 0, 1, 2))
    w_own = [jnp.where(upper, u, v) for u, v in zip(w_second, w_first)]
    w_side = [jnp.where(upper, u, v) for u, v in zip(w_upper, w_lower)]
    own_to_side, own_to_other = jnp.where(upper, w_own[2], w_own[1]), jnp.where(upper, w_own[1], w_own[2])
    side_to_own, side_to_next = jnp.where(upper, w_side[1], w_side[2]), jnp.where(upper, w_side[2], w_side[1])
    other_link = jnp.where(upper, w_first[2], w_second[1])
    w_other = [jnp.where(upper, u, v) for u, v in zip(w_first, w_second)]

    def at(base, offset):
        return pl.ds(pl.multiple_of(base + offset, 8), 8)

    here, there = 128 * a, 128 * (1 - a)

    def side_band(t):
        tile = side_ref[pl.ds(256 + 8 * (t % 4), 8), :]
        return jnp.where(lane < 64, pltpu.roll(tile, 64, 1) if t >= 4 else tile, 0.0)

    for c in range(2):
        for t in range(TILES):
            k = 64 * c + 8 * t
            _, gain = gains(w_own, coef_ref[pl.ds(k, 8), :])
            next_own[pl.ds(k, 8), :] = (
                half_ref[at(here, k), :] + gain * own_to_side * side_ref[at(there, k), :]
            )
    for t in range(TILES):
        now = band_ref[at(64 * a, 8 * t), :]
        spread, gain = gains(w_own, band_ref[pl.ds(128 + 8 * t, 8), :])
        near = spin(sum_near[at(16 * a, 8 * (t % 2)), :], unpack_by - 32 * (t // 2))
        total = jnp.where(near_lanes, near, sum_far[at(64 * a, 8 * t), :])
        push = spread * total + own_to_side * side_band(t) + bulge(w_own, now)
        push = push + own_to_other * band_ref[at(64 * (1 - a), 8 * t), :]
        next_band[pl.ds(8 * t, 8), :] = (1.0 - OMEGA) * now + gain * push

    src = Sources(lambda c, t: side_ref[at(there, 64 * c + 8 * t), :] if c < 2 else side_band(t))
    for c in range(2):
        total = neighbour_sum(src, src.tile[c], src.turned[c], kinds[c])
        for t in range(TILES):
            k = 64 * c + 8 * t
            spread, gain = gains(w_side, coef_ref[pl.ds(k, 8), :])
            push = spread * total[t] + side_to_own * pack_ref[at(here, k), :]
            push = push + side_to_next * side_ref[at(here, k), :]
            next_side[pl.ds(k, 8), :] = (1.0 - OMEGA) * src.tile[c][t] + gain * push

    src = Sources(
        lambda c, t: next_own[pl.ds(64 * c + 8 * t, 8), :] if c < 2 else next_band[pl.ds(8 * t, 8), :]
    )
    for c in range(2):
        total = neighbour_sum(src, src.tile[c], src.turned[c], kinds[c])
        for t in range(TILES):
            k = 64 * c + 8 * t
            coef = coef_ref[pl.ds(k, 8), :]
            spread, gain = gains(w_own, coef)
            once = src.tile[c][t]
            push = spread * total[t] + own_to_side * next_side[pl.ds(k, 8), :]
            push = push + bulge(w_own, pack_ref[at(here, k), :])
            if not final:
                twice_ref[pl.ds(k, 8), :] = (1.0 - OMEGA) * once + gain * push
                continue
            push = push + own_to_other * other_once[pl.ds(k, 8), :]
            _, other_gain = gains(w_other, coef)
            lanes_at = pl.ds(LANES * c, LANES)
            out_ref[a, pl.ds(8 * t, 8), lanes_at] = (1.0 - OMEGA) * once + gain * push
            out_ref[1 - a, pl.ds(8 * t, 8), lanes_at] = (
                other_twice[pl.ds(k, 8), :] + other_gain * other_link * once
            )


def swap(block, axis, first):
    route = []
    for i in range(first, lax.axis_size(axis) - 1, 2):
        route += [(i, i + 1), (i + 1, i)]
    return lax.ppermute(block, axis, route)


def call(kernel, shapes, spaces, *operands, scratch=(), flops=0):
    vmem = pltpu.VMEM
    space = {"h": pltpu.HBM, "v": vmem, "s": pltpu.SMEM}
    moved = sum(4 * int(np.prod(o.shape)) for o in operands)
    return pl.pallas_call(
        kernel,
        out_shape=[jax.ShapeDtypeStruct(s, F32) for s in shapes],
        in_specs=[pl.BlockSpec(memory_space=space[s]) for s in spaces],
        out_specs=[pl.BlockSpec(memory_space=vmem) for _ in shapes],
        scratch_shapes=list(scratch),
        compiler_params=pltpu.CompilerParams(vmem_limit_bytes=16 * 2**20),
        cost_estimate=pl.CostEstimate(flops=flops, bytes_accessed=moved, transcendentals=0),
    )(*operands)


def local(table, field_old, coef_old, owner, counts, pattern):
    layers = field_old.shape[0]
    stored = [pltpu.with_memory_space_constraint(x, pltpu.HBM) for x in (field_old, coef_old, owner)]
    to_near, field, coef = call(
        near_kernel,
        [(104, LANES), field_old.shape, coef_old.shape],
        "hhhs",
        *stored, counts,
        scratch=[pltpu.VMEM((OLD_SLOTS,), jnp.int32), pltpu.SemaphoreType.DMA((3,))],
    )
    from_near = swap(to_near, "leaf", 0)
    ends_far, gone = call(
        ready_kernel, [(96, LANES), (192, LANES)], "vvv", field, coef, to_near
    )
    to_far, own_part, band_part = call(
        far_kernel,
        [(144, LANES), (256, LANES), (128, LANES)],
        "vvvvvv",
        field, pattern, to_near, ends_far, gone, from_near,
    )
    from_far = swap(to_far, "leaf", 1)
    coef_part, coef_side = call(
        coef_kernel, [(128, LANES), (64, LANES)], "vvvv", coef, to_far, gone, from_near
    )
    pack, pack_far, coef, band = call(
        place_kernel,
        [(288, LANES), (288, LANES), (128, LANES), (192, LANES)],
        "vvvvvv",
        to_far, own_part, band_part, coef_part, coef_side, from_far,
    )
    side_near = swap(pack, "gy", 0)
    side_far = swap(pack_far, "gy", 1)
    (sum_near,) = call(facing_kernel, [(32, LANES)], "vvv", pattern, pack, band)
    sum_near = swap(sum_near, "leaf", 0)
    half, sum_far = call(
        functools.partial(own_kernel, layers, table),
        [(256, LANES), (128, LANES)],
        "vvvvvv",
        pattern, pack, coef, band, to_far, from_far,
    )
    once, twice = call(
        functools.partial(side_kernel, layers, table, False),
        [(128, LANES), (128, LANES)],
        "vvvvvvvv",
        pattern, pack, coef, band, half, side_far, sum_near, sum_far,
        scratch=[pltpu.VMEM((64, LANES), F32), pltpu.VMEM((128, LANES), F32)],
    )
    (out,) = call(
        functools.partial(side_kernel, layers, table, True),
        [(layers, 64, BRICKS_DEV)],
        "vvvvvvvvvv",
        pattern, pack, coef, band, half, side_near, sum_near, sum_far, once, twice,
        scratch=[pltpu.VMEM((rows, LANES), F32) for rows in (128, 64, 128)],
    )
    return out


def solution(mesh):
    layers = Y // mesh.shape["gy"]
    return jax.shard_map(
        functools.partial(local, weight_table(layers)),
        mesh=mesh,
        in_specs=(P("gy", None, "leaf"), P(None, "leaf"), P("leaf"), P("leaf"), P(None, "leaf")),
        out_specs=P("gy", None, "leaf"),
        check_vma=False,
    )
```

```python
import functools

import jax
import jax.numpy as jnp
import numpy as np
from jax import lax
from jax.experimental import pallas as pl
from jax.experimental.pallas import tpu as pltpu
from jax.sharding import PartitionSpec as P

BRICKS_DEV = 256
SPILL = 32
Y = 8
OLD_SLOTS = 320
EXPONENT = 0.5
HEIGHT = 8.0
OMEGA = 0.8

F32 = jnp.float32
LANES = 128
TILES = 8
GATHER = lax.GatherDimensionNumbers(
    offset_dims=(),
    collapsed_slice_dims=(1,),
    start_index_map=(1,),
    operand_batching_dims=(0,),
    start_indices_batching_dims=(0,),
)


def weight_table(layers):
    rows = []
    for level in range(-1, Y + 1):
        if not 0 <= level < Y:
            rows.append((0.0, 0.0, 0.0, 0.0, 1.0))
            continue
        y_here = HEIGHT * (level / Y) ** 2
        y_next = HEIGHT * ((level + 1) / Y) ** 2
        y_prev = HEIGHT * ((level - 1) / Y) ** 2
        step_up, step_down = y_next - y_here, y_here - y_prev
        up_weight = ((y_here + y_next) * 0.5) ** EXPONENT
        down_weight = ((y_here + y_prev) * 0.5) ** EXPONENT
        has_lower = float(level > 0)
        up_link = up_weight / step_up
        down_link = has_lower * down_weight / step_down
        planar = 0.5 * (up_weight * step_up + has_lower * down_weight * step_down)
        surface = float(level == 0)
        rows.append((planar, down_link, up_link, surface, down_link + up_link + surface))
    return np.asarray(rows, np.float32)


def weights_at(table, group, layers, offset):
    groups = Y // layers
    out = []
    for column in range(5):
        value = F32(table[offset + 1, column])
        for g in range(1, groups):
            value = jnp.where(group == g, F32(table[g * layers + offset + 1, column]), value)
        out.append(value)
    return out


def lanes():
    return lax.broadcasted_iota(jnp.int32, (8, LANES), 1)


def rows():
    return lax.broadcasted_iota(jnp.int32, (8, LANES), 0)


def spin(tile, shift):
    if isinstance(shift, int):
        return pltpu.roll(tile, shift % LANES, 1) if shift % LANES else tile
    return pltpu.roll(tile, jnp.bitwise_and(shift, LANES - 1), 1)


def pick(tile, index):
    return lax.gather(
        tile,
        index[:, :, None],
        GATHER,
        (1, 1),
        mode=lax.GatherScatterMode.PROMISE_IN_BOUNDS,
    )


def spill_counts(owner_ref, live_count, device):
    lane, sub = lanes(), rows()
    hits = jnp.zeros((8, LANES), F32)
    for c in range(3):
        width = min(LANES, OLD_SLOTS - LANES * c)
        row = owner_ref[pl.ds(LANES * c, width)].reshape(1, width)
        if width < LANES:
            row = jnp.concatenate([row, jnp.zeros((1, LANES - width), jnp.int32)], axis=1)
        row = jnp.broadcast_to(row, (8, LANES))
        wanted = device + jnp.where(sub == 0, -1, 1)
        hits += jnp.where((row == wanted) & (lane + LANES * c < live_count), 1.0, 0.0)
    return jnp.sum(hits, axis=1, keepdims=True)


def old_tile(ref, lead, t, c):
    at = (lead, pl.ds(8 * t, 8)) if lead is not None else (pl.ds(8 * t, 8),)
    if c < 2:
        return ref[at + (pl.ds(LANES * c, LANES),)]
    half = ref[at + (pl.ds(2 * LANES, OLD_SLOTS - 2 * LANES),)]
    return jnp.concatenate([half, jnp.zeros((8, 3 * LANES - OLD_SLOTS), F32)], axis=1)


def face_rows(pattern_rows):
    sub = rows()
    return (
        pattern_rows[0],
        pattern_rows[1],
        jnp.where(sub < 4, pattern_rows[3], pattern_rows[2]),
        jnp.where((sub & 3) == 3, pattern_rows[4], pattern_rows[5]),
    )


def face_indices(pattern_rows):
    out = []
    for w in face_rows(pattern_rows):
        source = w >> 7
        own = (source == 2) | (source == 3)
        beside = jnp.where(w >= 2 * BRICKS_DEV, w - (2 * BRICKS_DEV - SPILL), w - (BRICKS_DEV - SPILL))
        lane = jnp.where(own, w & (LANES - 1), jnp.where(w >= BRICKS_DEV - SPILL, beside, LANES - 1))
        out.append((lane, source == 2, source == 3))
    return out


def face(kind, tiles):
    if len(tiles) == 1:
        return pick(tiles[0], kind[0])
    lane, first, second = kind
    return jnp.where(first, pick(tiles[0], lane), jnp.where(second, pick(tiles[1], lane), pick(tiles[2], lane)))


class Sources:
    def __init__(self, read, count=3):
        sub = rows()
        self.columns = range(count)
        self.tile = [[read(c, t) for t in range(TILES)] for c in self.columns]
        self.turned = [[pltpu.roll(v, 4, 0) for v in column] for column in self.tile]
        self.y_edge = [
            [jnp.where(sub < 4, column[2 * i], column[2 * i + 1]) for i in range(4)]
            for column in self.tile
        ]


def neighbour_sum(src, here, turned, kinds):
    sub = rows()
    low, k = sub < 4, sub & 3
    x_low, x_high, y_both, z_both = kinds
    total = []
    for t in range(TILES):
        if t < 2:
            below = face(x_low, [src.tile[c][6 + t] for c in src.columns])
        else:
            below = here[t - 2]
        if t >= 6:
            above = face(x_high, [src.tile[c][t - 6] for c in src.columns])
        else:
            above = here[t + 2]
        total.append(below + above)
    for i in range(4):
        edge = pltpu.roll(face(y_both, [src.y_edge[c][i] for c in src.columns]), 4, 0)
        first, second = turned[2 * i], turned[2 * i + 1]
        middle = jnp.where(low, first, second)
        total[2 * i] += jnp.where(low, edge, first) + middle
        total[2 * i + 1] += jnp.where(low, second, edge) + middle
    for t in range(TILES):
        edge = face(z_both, [src.turned[c][t] for c in src.columns])
        total[t] += pltpu.roll(jnp.where(k == 3, edge, here[t]), 1, 0)
        total[t] += pltpu.roll(jnp.where(k == 0, edge, here[t]), 7, 0)
    return total


def is_even(axis):
    return (lax.axis_index(axis) & 1) == 0


def ends(ref, lead, r, live, next_side):
    lane = lanes()
    front, back = old_tile(ref, lead, r, 0), old_tile(ref, lead, r + 4, 0)
    prev = jnp.where(lane < 64, front, pltpu.roll(back, 64, 1))
    early = lane >= live - 192
    front = jnp.where(early, old_tile(ref, lead, r, 1), old_tile(ref, lead, r, 2))
    back = jnp.where(early, old_tile(ref, lead, r + 4, 1), old_tile(ref, lead, r + 4, 2))
    next = jnp.where(lane < 64, spin(front, 64 - live), spin(back, 128 - live))
    return jnp.where(next_side, next, prev)


def near_kernel(
    field_hbm, coef_hbm, owner_hbm, counts_ref, near_ref, field_ref, coef_ref, owner_ref, sems
):
    pairs = ((owner_hbm, owner_ref), (field_hbm, field_ref), (coef_hbm, coef_ref))
    copies = [pltpu.make_async_copy(a, b, sems.at[i]) for i, (a, b) in enumerate(pairs)]
    for copy in copies:
        copy.start()
    sub = rows()
    even = is_even("leaf")
    live = counts_ref[0]
    copies[0].wait()
    spills = spill_counts(owner_ref, live, lax.axis_index("leaf"))
    to_prev, to_next = (jnp.broadcast_to(spills[i : i + 1], (8, LANES)) for i in range(2))
    kept = jnp.where(sub == 1, live.astype(F32), jnp.where(sub == 2, to_prev, to_next))
    near_ref[pl.ds(96, 8), :] = jnp.where(sub == 0, jnp.where(even, to_next, to_prev), kept)
    for a in range(3):
        ref, lead = (field_ref, a) if a < 2 else (coef_ref, None)
        if a != 1:
            copies[1 + a // 2].wait()
        for r in range(4):
            near_ref[pl.ds(32 * a + 8 * r, 8), :] = ends(ref, lead, r, live, even)


def pattern_row(pattern_ref, direction, c):
    row = pattern_ref[pl.ds(direction, 1), pl.ds(LANES * c, LANES)]
    return jnp.broadcast_to(row, (8, LANES))


def pack_quarters(total, half, first):
    lane = lanes()
    base = jnp.where(first, 0, 32)
    q = [spin(total[2 * i + half], base + 32 * i) for i in range(4)]
    return jnp.where(
        lane < 64, jnp.where(lane < 32, q[0], q[1]), jnp.where(lane < 96, q[2], q[3])
    )


def ready_kernel(field_ref, coef_ref, kept_ref, ends_ref, gone_ref):
    lane = lanes()
    even = is_even("leaf")
    live, to_prev, to_next = (kept_ref[96 + i, 0].astype(jnp.int32) for i in (1, 2, 3))
    for a in range(3):
        ref, lead = (field_ref, a) if a < 2 else (coef_ref, None)
        for r in range(4):
            ends_ref[pl.ds(32 * a + 8 * r, 8), :] = ends(ref, lead, r, live, jnp.logical_not(even))
        for t in range(TILES):
            x0, x1, x2 = (old_tile(ref, lead, t, c) for c in range(3))
            last = jnp.where(lane >= live - to_next - LANES, x1, x2)
            gone_ref[pl.ds(64 * a + 8 * t, 8), :] = jnp.where(
                lane < SPILL, spin(x0, SPILL - to_prev), spin(last, SPILL + to_next - live)
            )


def place_part(sources, counts, gone_ref, near_ref, own_ref, band_ref):
    lane = lanes()
    even = is_even("leaf")
    live, to_prev, to_next, from_prev, from_next = counts
    drift = to_prev - from_prev
    tail = from_prev + live - to_prev - to_next - LANES
    spill = (lane >= SPILL - to_prev) & (lane < SPILL + to_next)
    near_low = jnp.where(even, SPILL, 0)
    near_lanes = (lane >= near_low) & (lane < near_low + SPILL)
    arrive_by = jnp.where(even, tail, from_prev - 64)
    band_by = jnp.where(even, SPILL + to_next - from_next, from_prev - to_prev - SPILL)
    for out, (a, ref, lead) in enumerate(sources):
        for t in range(TILES):
            h = 64 * (t // 4)
            near = near_ref[pl.ds(32 * a + 8 * (t % 4), 8), :]
            x0, x1, x2 = (old_tile(ref, lead, t, c) for c in range(3))
            r0, r1, r2 = spin(x0, -drift), spin(x1, -drift), spin(x2, -drift)
            own0 = jnp.where(lane < LANES - drift, r0, r1)
            own1 = jnp.where(lane < -drift, r0, jnp.where(lane < LANES - drift, r1, r2))
            arrived = spin(near, arrive_by - h)
            own0 = jnp.where(lane < from_prev, jnp.where(even, 0.0, arrived), own0)
            own1 = jnp.where(lane >= tail, jnp.where(even, arrived, 0.0), own1)
            gone = gone_ref[pl.ds(64 * a + 8 * t, 8), :]
            band = jnp.where(spill, gone, jnp.where(near_lanes, spin(near, band_by - h), 0.0))
            own_ref[pl.ds(128 * out + 8 * t, 8), :] = own0
            own_ref[pl.ds(128 * out + 64 + 8 * t, 8), :] = own1
            band_ref[pl.ds(64 * out + 8 * t, 8), :] = band
    return near_lanes


def coef_kernel(coef_ref, kept_ref, gone_ref, near_ref, own_ref, band_ref):
    counts = [kept_ref[96 + i, 0].astype(jnp.int32) for i in range(1, 6)]
    place_part([(2, coef_ref, None)], counts, gone_ref, near_ref, own_ref, band_ref)


def far_kernel(
    field_ref, pattern_ref, kept_ref, ends_ref, gone_ref, near_ref, far_ref, own_ref, band_ref
):
    lane, sub = lanes(), rows()
    even = is_even("leaf")
    live, to_prev, to_next = (kept_ref[96 + i, 0].astype(jnp.int32) for i in (1, 2, 3))
    from_near = near_ref[96, 0].astype(jnp.int32)
    from_far = BRICKS_DEV - (live - to_prev - to_next) - from_near
    from_prev, from_next = jnp.where(even, from_far, from_near), jnp.where(even, from_near, from_far)
    handed = jnp.where(even, to_prev, to_next)
    counts = jnp.zeros((8, LANES), jnp.int32)
    for i, value in enumerate((handed, live, to_prev, to_next, from_prev, from_next)):
        counts = jnp.where(sub == i, value, counts)
    far_ref[pl.ds(96, 8), :] = counts.astype(F32)
    for r in range(12):
        far_ref[pl.ds(8 * r, 8), :] = ends_ref[pl.ds(8 * r, 8), :]
    near_lanes = place_part(
        [(a, field_ref, a) for a in range(2)],
        (live, to_prev, to_next, from_prev, from_next),
        gone_ref, near_ref, own_ref, band_ref,
    )
    far_rows = [
        jnp.where(even, pattern_row(pattern_ref, d, 0), pattern_row(pattern_ref, d, 1)) for d in range(6)
    ]
    sent = jnp.zeros((8, LANES), jnp.int32)
    for d in range(6):
        row = spin(far_rows[d], jnp.where(even, 0, 32))
        sent = jnp.where(sub == d, row, sent)
    sent = jnp.where(lane < 32, sent, pltpu.roll(sent, 32, 1))
    far_ref[pl.ds(104, 8), :] = sent.astype(F32)
    kinds = face_indices(far_rows)
    for a in range(2):

        def read(c, t):
            if c < 2:
                return own_ref[pl.ds(128 * a + 64 * c + 8 * t, 8), :]
            return jnp.where(near_lanes, band_ref[pl.ds(64 * a + 8 * t, 8), :], 0.0)

        src = Sources(read)
        here = [jnp.where(even, src.tile[0][t], src.tile[1][t]) for t in range(TILES)]
        turned = [jnp.where(even, src.turned[0][t], src.turned[1][t]) for t in range(TILES)]
        total = neighbour_sum(src, here, turned, kinds)
        for half in range(2):
            far_ref[pl.ds(112 + 16 * a + 8 * half, 8), :] = pack_quarters(total, half, even)


def place_kernel(
    kept_ref, own_ref, band_ref, coef_own, coef_band, far_ref, pack_near, pack_far, coef_out, band_out
):
    lane = lanes()
    even = is_even("leaf")
    even_group = is_even("gy")
    _, live, to_prev, to_next, from_prev, from_next = (
        kept_ref[96 + i, 0].astype(jnp.int32) for i in range(6)
    )
    tail = from_prev + live - to_prev - to_next - LANES
    first = jnp.where(even, from_prev, 0)
    final = jnp.where(even, LANES, tail)
    stays_low = jnp.where(even, 0, SPILL + to_next)
    stays_high = jnp.where(even, SPILL - to_prev, 2 * SPILL)
    stays = (lane >= stays_low) & (lane < stays_high)
    arrive_by = jnp.where(even, from_prev - 64, tail)
    band_by = jnp.where(even, from_prev - to_prev - SPILL, SPILL + to_next - from_next)
    for a in range(3):
        for t in range(TILES):
            h = 64 * (t // 4)
            far = far_ref[pl.ds(32 * a + 8 * (t % 4), 8), :]
            arrived = spin(far, arrive_by - h)
            part, side, b = (own_ref, band_ref, a) if a < 2 else (coef_own, coef_band, 0)
            own0 = jnp.where(lane < first, arrived, part[pl.ds(128 * b + 8 * t, 8), :])
            own1 = jnp.where(lane >= final, arrived, part[pl.ds(128 * b + 64 + 8 * t, 8), :])
            band = jnp.where(stays, spin(far, band_by - h), side[pl.ds(64 * b + 8 * t, 8), :])
            band_out[pl.ds(64 * a + 8 * t, 8), :] = band
            if a < 2:
                for pack in (pack_near, pack_far):
                    pack[pl.ds(128 * a + 8 * t, 8), :] = own0
                    pack[pl.ds(128 * a + 64 + 8 * t, 8), :] = own1
            else:
                coef_out[pl.ds(8 * t, 8), :] = own0
                coef_out[pl.ds(64 + 8 * t, 8), :] = own1
    for r in range(4):
        packed = [
            jnp.where(
                lane < 64,
                band_out[pl.ds(64 * a + 8 * r, 8), :],
                pltpu.roll(band_out[pl.ds(64 * a + 8 * r + 32, 8), :], 64, 1),
            )
            for a in range(2)
        ]
        pack_near[pl.ds(256 + 8 * r, 8), :] = jnp.where(even_group, packed[1], packed[0])
        pack_far[pl.ds(256 + 8 * r, 8), :] = jnp.where(even_group, packed[0], packed[1])


def facing_kernel(pattern_ref, pack_ref, band_ref, sum_near):
    even = is_even("leaf")
    kinds = face_indices(
        [jnp.where(even, pattern_row(pattern_ref, d, 1), pattern_row(pattern_ref, d, 0)) for d in range(6)]
    )
    for a in range(2):
        src = Sources(
            lambda c, t: own(pack_ref, a, c, t) if c < 2 else band_ref[pl.ds(64 * a + 8 * t, 8), :]
        )
        here = [jnp.where(even, src.tile[1][t], src.tile[0][t]) for t in range(TILES)]
        turned = [jnp.where(even, src.turned[1][t], src.turned[0][t]) for t in range(TILES)]
        total = neighbour_sum(src, here, turned, kinds)
        for half in range(2):
            sum_near[pl.ds(16 * a + 8 * half, 8), :] = pack_quarters(total, half, jnp.logical_not(even))


def far_sums(kept_ref, far_ref, pack_ref, band_ref, sum_far):
    lane = lanes()
    even = is_even("leaf")
    to_prev, to_next = (kept_ref[96 + i, 0].astype(jnp.int32) for i in (2, 3))
    shift = jnp.where(even, 480, 224)
    window = [
        jnp.broadcast_to(far_ref[pl.ds(104 + d, 1), :], (8, LANES)).astype(jnp.int32) - shift
        for d in range(6)
    ]
    window = [jnp.where((w >= 0) & (w < 2 * SPILL), w, LANES - 1) for w in window]
    kinds = [(w,) for w in face_rows(window)]
    far_low = jnp.where(even, 0, SPILL)
    far_lanes = (lane >= far_low) & (lane < far_low + SPILL)
    mine = (lane < 2 * SPILL) & jnp.logical_not(far_lanes)
    given = far_lanes & (lane >= SPILL - to_prev) & (lane < SPILL + to_next)
    for a in range(2):

        def meet(_, t):
            facing = spin(jnp.where(even, own(pack_ref, a, 0, t), own(pack_ref, a, 1, t)), 32)
            return jnp.where(given, band_ref[pl.ds(64 * a + 8 * t, 8), :], jnp.where(mine, facing, 0.0))

        joint = Sources(meet, 1)
        total = neighbour_sum(joint, joint.tile[0], joint.turned[0], kinds)
        for t in range(TILES):
            part = far_ref[pl.ds(112 + 16 * a + 8 * (t % 2), 8), :]
            part = spin(part, far_low - 32 * (t // 2))
            sum_far[pl.ds(64 * a + 8 * t, 8), :] = jnp.where(far_lanes, total[t] + part, 0.0)


def own(ref, a, c, t):
    return ref[pl.ds(128 * a + 64 * c + 8 * t, 8), :]


def own_kinds(pattern_ref):
    return [
        face_indices(
            [
                jnp.broadcast_to(pattern_ref[pl.ds(d, 1), pl.ds(LANES * c, LANES)], (8, LANES))
                for d in range(6)
            ]
        )
        for c in range(2)
    ]


def gains(weights, coef):
    spread = weights[0] * coef
    return spread, OMEGA / (6.0 * spread + weights[4])


def bulge(weights, phase):
    return weights[3] * (2.0 * phase - phase * phase * phase)


def own_kernel(
    layers, table, pattern_ref, pack_ref, coef_ref, band_ref, kept_ref, far_ref, half_ref, sum_far
):
    far_sums(kept_ref, far_ref, pack_ref, band_ref, sum_far)
    group = lax.axis_index("gy")
    kinds = own_kinds(pattern_ref)
    weights = [weights_at(table, group, layers, a) for a in range(2)]
    for a in range(2):
        src = Sources(
            lambda c, t: own(pack_ref, a, c, t) if c < 2 else band_ref[pl.ds(64 * a + 8 * t, 8), :]
        )
        for c in range(2):
            total = neighbour_sum(src, src.tile[c], src.turned[c], kinds[c])
            for t in range(TILES):
                now = src.tile[c][t]
                spread, gain = gains(weights[a], coef_ref[pl.ds(64 * c + 8 * t, 8), :])
                push = spread * total[t] + weights[a][2 - a] * own(pack_ref, 1 - a, c, t)
                if a == 0:
                    push = push + bulge(weights[0], now)
                half_ref[pl.ds(128 * a + 64 * c + 8 * t, 8), :] = (1.0 - OMEGA) * now + gain * push


def at(base, offset):
    return pl.ds(pl.multiple_of(base + offset, 8), 8)


def side_weights(layers, table, upper):
    group = lax.axis_index("gy")
    lower, first, second, over = (weights_at(table, group, layers, o) for o in (-1, 0, 1, 2))
    own_w = [jnp.where(upper, u, v) for u, v in zip(second, first)]
    side_w = [jnp.where(upper, u, v) for u, v in zip(over, lower)]

    def link(weights, outward):
        return jnp.where(upper == outward, weights[2], weights[1])

    return own_w, side_w, link(own_w, True), link(own_w, False), link(side_w, False), link(side_w, True)


def side_kernel(
    layers, table, near_side,
    pattern_ref, pack_ref, coef_ref, band_ref, half_ref, side_ref, once_ref, next_ref, edge_ref,
):
    lane = lanes()
    upper = is_even("gy") if near_side else jnp.logical_not(is_even("gy"))
    a = jnp.where(upper, 1, 0)
    kinds = own_kinds(pattern_ref)
    w_own, w_side, own_to_side, own_to_other, side_to_own, side_to_next = side_weights(
        layers, table, upper
    )
    here, there = 128 * a, 128 * (1 - a)

    def side_band(t):
        tile = side_ref[pl.ds(256 + 8 * (t % 4), 8), :]
        return jnp.where(lane < 64, pltpu.roll(tile, 64, 1) if t >= 4 else tile, 0.0)

    for c in range(2):
        for t in range(TILES):
            k = 64 * c + 8 * t
            _, gain = gains(w_own, coef_ref[pl.ds(k, 8), :])
            once_ref[pl.ds(k, 8), :] = (
                half_ref[at(here, k), :] + gain * own_to_side * side_ref[at(there, k), :]
            )
    for t in range(TILES):
        now = band_ref[at(64 * a, 8 * t), :]
        _, gain = gains(w_own, band_ref[pl.ds(128 + 8 * t, 8), :])
        push = own_to_side * side_band(t) + bulge(w_own, now)
        push = push + own_to_other * band_ref[at(64 * (1 - a), 8 * t), :]
        edge_ref[pl.ds(8 * t, 8), :] = (1.0 - OMEGA) * now + gain * push

    src = Sources(lambda c, t: side_ref[at(there, 64 * c + 8 * t), :] if c < 2 else side_band(t))
    for c in range(2):
        total = neighbour_sum(src, src.tile[c], src.turned[c], kinds[c])
        for t in range(TILES):
            k = 64 * c + 8 * t
            spread, gain = gains(w_side, coef_ref[pl.ds(k, 8), :])
            push = spread * total[t] + side_to_own * pack_ref[at(here, k), :]
            push = push + side_to_next * side_ref[at(here, k), :]
            next_ref[pl.ds(k, 8), :] = (1.0 - OMEGA) * src.tile[c][t] + gain * push


def final_kernel(
    layers, table,
    pattern_ref, pack_ref, coef_ref, band_ref, sum_near, sum_far,
    far_once, far_next, far_edge, near_once, near_next, near_edge,
    out_hbm, edge_ref, left_ref, right_ref, sems,
):
    even = is_even("leaf")
    unpack_by = jnp.where(even, SPILL, 0)
    lane = lanes()
    near_lanes = (lane >= unpack_by) & (lane < unpack_by + SPILL)
    kinds = own_kinds(pattern_ref)
    sides = []
    for side, (once, next, edge) in enumerate(
        ((near_once, near_next, near_edge), (far_once, far_next, far_edge))
    ):
        upper = jnp.logical_not(is_even("gy")) if side else is_even("gy")
        a = jnp.where(upper, 1, 0)
        w_own, _, own_to_side, own_to_other, _, _ = side_weights(layers, table, upper)
        for t in range(TILES):
            spread, gain = gains(w_own, band_ref[pl.ds(128 + 8 * t, 8), :])
            near = spin(sum_near[at(16 * a, 8 * (t % 2)), :], unpack_by - 32 * (t // 2))
            total = jnp.where(near_lanes, near, sum_far[at(64 * a, 8 * t), :])
            k = 64 * side + 8 * t
            edge_ref[pl.ds(k, 8), :] = edge[pl.ds(8 * t, 8), :] + gain * (spread * total)

        def read(c, t):
            return once[pl.ds(64 * c + 8 * t, 8), :] if c < 2 else edge_ref[pl.ds(64 * side + 8 * t, 8), :]

        sides.append((a, w_own, own_to_side, own_to_other, Sources(read), next))
    copies = []
    for c, buffer in enumerate((left_ref, right_ref)):
        for side, (a, w_own, own_to_side, own_to_other, src, next) in enumerate(sides):
            other = sides[1 - side][4]
            total = neighbour_sum(src, src.tile[c], src.turned[c], kinds[c])
            for t in range(TILES):
                k = 64 * c + 8 * t
                spread, gain = gains(w_own, coef_ref[pl.ds(k, 8), :])
                push = spread * total[t] + own_to_side * next[pl.ds(k, 8), :]
                push = push + own_to_other * other.tile[c][t]
                push = push + bulge(w_own, pack_ref[at(128 * a, k), :])
                buffer[a, pl.ds(8 * t, 8), :] = (1.0 - OMEGA) * src.tile[c][t] + gain * push
        copies.append(
            pltpu.make_async_copy(buffer, out_hbm.at[:, :, pl.ds(LANES * c, LANES)], sems.at[c])
        )
        copies[-1].start()
    for copy in copies:
        copy.wait()


def swap(block, axis, first):
    route = []
    for i in range(first, lax.axis_size(axis) - 1, 2):
        route += [(i, i + 1), (i + 1, i)]
    return lax.ppermute(block, axis, route)


def call(kernel, shapes, spaces, *operands, scratch=(), out_space=pltpu.VMEM):
    vmem = pltpu.VMEM
    space = {"h": pltpu.HBM, "v": vmem, "s": pltpu.SMEM}
    moved = sum(4 * int(np.prod(o.shape)) for o in operands)
    return pl.pallas_call(
        kernel,
        out_shape=[jax.ShapeDtypeStruct(s, F32) for s in shapes],
        in_specs=[pl.BlockSpec(memory_space=space[s]) for s in spaces],
        out_specs=[pl.BlockSpec(memory_space=out_space) for _ in shapes],
        scratch_shapes=list(scratch),
        compiler_params=pltpu.CompilerParams(vmem_limit_bytes=16 * 2**20),
        cost_estimate=pl.CostEstimate(flops=0, bytes_accessed=moved, transcendentals=0),
    )(*operands)


def local(table, field_old, coef_old, owner, counts, pattern):
    layers = field_old.shape[0]
    stored = [pltpu.with_memory_space_constraint(x, pltpu.HBM) for x in (field_old, coef_old, owner)]
    to_near, field, coef = call(
        near_kernel,
        [(104, LANES), field_old.shape, coef_old.shape],
        "hhhs",
        *stored, counts,
        scratch=[pltpu.VMEM((OLD_SLOTS,), jnp.int32), pltpu.SemaphoreType.DMA((3,))],
    )
    from_near = swap(to_near, "leaf", 0)
    ends_far, gone = call(
        ready_kernel, [(96, LANES), (192, LANES)], "vvv", field, coef, to_near
    )
    to_far, own_part, band_part = call(
        far_kernel,
        [(144, LANES), (256, LANES), (128, LANES)],
        "vvvvvv",
        field, pattern, to_near, ends_far, gone, from_near,
    )
    from_far = swap(to_far, "leaf", 1)
    coef_part, coef_side = call(
        coef_kernel, [(128, LANES), (64, LANES)], "vvvv", coef, to_far, gone, from_near
    )
    pack, pack_far, coef, band = call(
        place_kernel,
        [(288, LANES), (288, LANES), (128, LANES), (192, LANES)],
        "vvvvvv",
        to_far, own_part, band_part, coef_part, coef_side, from_far,
    )
    side_near = swap(pack, "gy", 0)
    side_far = swap(pack_far, "gy", 1)
    (sum_near,) = call(facing_kernel, [(32, LANES)], "vvv", pattern, pack, band)
    sum_near = swap(sum_near, "leaf", 0)
    half, sum_far = call(
        functools.partial(own_kernel, layers, table),
        [(256, LANES), (128, LANES)],
        "vvvvvv",
        pattern, pack, coef, band, to_far, from_far,
    )
    sides = []
    for near_side, side in ((True, side_near), (False, side_far)):
        sides += call(
            functools.partial(side_kernel, layers, table, near_side),
            [(128, LANES), (128, LANES), (64, LANES)],
            "vvvvvv",
            pattern, pack, coef, band, half, side,
        )
    (out,) = call(
        functools.partial(final_kernel, layers, table),
        [(layers, 64, BRICKS_DEV)],
        "v" * 12,
        pattern, pack, coef, band, sum_near, sum_far, *sides[3:], *sides[:3],
        out_space=pltpu.HBM,
        scratch=[pltpu.VMEM((128, LANES), F32)]
        + [pltpu.VMEM((layers, 64, LANES), F32)] * 2
        + [pltpu.SemaphoreType.DMA((2,))],
    )
    return out


def solution(mesh):
    layers = Y // mesh.shape["gy"]
    return jax.shard_map(
        functools.partial(local, weight_table(layers)),
        mesh=mesh,
        in_specs=(P("gy", None, "leaf"), P(None, "leaf"), P("leaf"), P("leaf"), P(None, "leaf")),
        out_specs=P("gy", None, "leaf"),
        check_vma=False,
    )
```

```python
import functools

import jax
import jax.numpy as jnp
import numpy as np
from jax import lax
from jax.experimental import pallas as pl
from jax.experimental.pallas import tpu as pltpu
from jax.sharding import PartitionSpec as P

BRICKS_DEV = 256
SPILL = 32
Y = 8
OLD_SLOTS = 320
EXPONENT = 0.5
HEIGHT = 8.0
OMEGA = 0.8

F32 = jnp.float32
LANES = 128
TILES = 8
GATHER = lax.GatherDimensionNumbers(
    offset_dims=(),
    collapsed_slice_dims=(1,),
    start_index_map=(1,),
    operand_batching_dims=(0,),
    start_indices_batching_dims=(0,),
)


def weight_table(layers):
    rows = []
    for level in range(-1, Y + 1):
        if not 0 <= level < Y:
            rows.append((0.0, 0.0, 0.0, 0.0, 1.0))
            continue
        y_here = HEIGHT * (level / Y) ** 2
        y_next = HEIGHT * ((level + 1) / Y) ** 2
        y_prev = HEIGHT * ((level - 1) / Y) ** 2
        step_up, step_down = y_next - y_here, y_here - y_prev
        up_weight = ((y_here + y_next) * 0.5) ** EXPONENT
        down_weight = ((y_here + y_prev) * 0.5) ** EXPONENT
        has_lower = float(level > 0)
        up_link = up_weight / step_up
        down_link = has_lower * down_weight / step_down
        planar = 0.5 * (up_weight * step_up + has_lower * down_weight * step_down)
        surface = float(level == 0)
        rows.append((planar, down_link, up_link, surface, down_link + up_link + surface))
    return np.asarray(rows, np.float32)


def weights_at(table, group, layers, offset):
    groups = Y // layers
    out = []
    for column in range(5):
        value = F32(table[offset + 1, column])
        for g in range(1, groups):
            value = jnp.where(group == g, F32(table[g * layers + offset + 1, column]), value)
        out.append(value)
    return out


def lanes():
    return lax.broadcasted_iota(jnp.int32, (8, LANES), 1)


def rows():
    return lax.broadcasted_iota(jnp.int32, (8, LANES), 0)


def spin(tile, shift):
    if isinstance(shift, int):
        return pltpu.roll(tile, shift % LANES, 1) if shift % LANES else tile
    return pltpu.roll(tile, jnp.bitwise_and(shift, LANES - 1), 1)


def pick(tile, index):
    return lax.gather(
        tile,
        index[:, :, None],
        GATHER,
        (1, 1),
        mode=lax.GatherScatterMode.PROMISE_IN_BOUNDS,
    )


def spill_counts(owner_ref, live_count, device):
    lane, sub = lanes(), rows()
    hits = jnp.zeros((8, LANES), F32)
    for c in range(3):
        width = min(LANES, OLD_SLOTS - LANES * c)
        row = owner_ref[pl.ds(LANES * c, width)].reshape(1, width)
        if width < LANES:
            row = jnp.concatenate([row, jnp.zeros((1, LANES - width), jnp.int32)], axis=1)
        row = jnp.broadcast_to(row, (8, LANES))
        wanted = device + jnp.where(sub == 0, -1, 1)
        hits += jnp.where((row == wanted) & (lane + LANES * c < live_count), 1.0, 0.0)
    return jnp.sum(hits, axis=1, keepdims=True)


def old_tile(ref, lead, t, c):
    at = (lead, pl.ds(8 * t, 8)) if lead is not None else (pl.ds(8 * t, 8),)
    if c < 2:
        return ref[at + (pl.ds(LANES * c, LANES),)]
    half = ref[at + (pl.ds(2 * LANES, OLD_SLOTS - 2 * LANES),)]
    return jnp.concatenate([half, jnp.zeros((8, 3 * LANES - OLD_SLOTS), F32)], axis=1)


def face_rows(pattern_rows):
    sub = rows()
    return (
        pattern_rows[0],
        pattern_rows[1],
        jnp.where(sub < 4, pattern_rows[3], pattern_rows[2]),
        jnp.where((sub & 3) == 3, pattern_rows[4], pattern_rows[5]),
    )


def face_indices(pattern_rows):
    out = []
    for w in face_rows(pattern_rows):
        source = w >> 7
        own = (source == 2) | (source == 3)
        beside = jnp.where(w >= 2 * BRICKS_DEV, w - (2 * BRICKS_DEV - SPILL), w - (BRICKS_DEV - SPILL))
        lane = jnp.where(own, w & (LANES - 1), jnp.where(w >= BRICKS_DEV - SPILL, beside, LANES - 1))
        out.append((lane, source == 2, source == 3))
    return out


def face(kind, tiles):
    if len(tiles) == 1:
        return pick(tiles[0], kind[0])
    lane, first, second = kind
    return jnp.where(first, pick(tiles[0], lane), jnp.where(second, pick(tiles[1], lane), pick(tiles[2], lane)))


class Sources:
    def __init__(self, read, count=3):
        sub = rows()
        self.columns = range(count)
        self.tile = [[read(c, t) for t in range(TILES)] for c in self.columns]
        self.turned = [[pltpu.roll(v, 4, 0) for v in column] for column in self.tile]
        self.y_edge = [
            [jnp.where(sub < 4, column[2 * i], column[2 * i + 1]) for i in range(4)]
            for column in self.tile
        ]


def neighbour_sum(src, here, turned, kinds):
    sub = rows()
    low, k = sub < 4, sub & 3
    x_low, x_high, y_both, z_both = kinds
    total = []
    for t in range(TILES):
        if t < 2:
            below = face(x_low, [src.tile[c][6 + t] for c in src.columns])
        else:
            below = here[t - 2]
        if t >= 6:
            above = face(x_high, [src.tile[c][t - 6] for c in src.columns])
        else:
            above = here[t + 2]
        total.append(below + above)
    for i in range(4):
        edge = pltpu.roll(face(y_both, [src.y_edge[c][i] for c in src.columns]), 4, 0)
        first, second = turned[2 * i], turned[2 * i + 1]
        middle = jnp.where(low, first, second)
        total[2 * i] += jnp.where(low, edge, first) + middle
        total[2 * i + 1] += jnp.where(low, second, edge) + middle
    for t in range(TILES):
        edge = face(z_both, [src.turned[c][t] for c in src.columns])
        total[t] += pltpu.roll(jnp.where(k == 3, edge, here[t]), 1, 0)
        total[t] += pltpu.roll(jnp.where(k == 0, edge, here[t]), 7, 0)
    return total


def is_even(axis):
    return (lax.axis_index(axis) & 1) == 0


def ends(ref, lead, r, live, next_side):
    lane = lanes()
    front, back = old_tile(ref, lead, r, 0), old_tile(ref, lead, r + 4, 0)
    prev = jnp.where(lane < 64, front, pltpu.roll(back, 64, 1))
    early = lane >= live - 192
    front = jnp.where(early, old_tile(ref, lead, r, 1), old_tile(ref, lead, r, 2))
    back = jnp.where(early, old_tile(ref, lead, r + 4, 1), old_tile(ref, lead, r + 4, 2))
    next = jnp.where(lane < 64, spin(front, 64 - live), spin(back, 128 - live))
    return jnp.where(next_side, next, prev)


def near_kernel(
    field_hbm, coef_hbm, owner_hbm, counts_ref, near_ref, field_ref, coef_ref, owner_ref, sems
):
    pairs = ((owner_hbm, owner_ref), (field_hbm, field_ref), (coef_hbm, coef_ref))
    copies = [pltpu.make_async_copy(a, b, sems.at[i]) for i, (a, b) in enumerate(pairs)]
    for copy in copies:
        copy.start()
    sub = rows()
    even = is_even("leaf")
    live = counts_ref[0]
    copies[0].wait()
    spills = spill_counts(owner_ref, live, lax.axis_index("leaf"))
    to_prev, to_next = (jnp.broadcast_to(spills[i : i + 1], (8, LANES)) for i in range(2))
    kept = jnp.where(sub == 1, live.astype(F32), jnp.where(sub == 2, to_prev, to_next))
    near_ref[pl.ds(96, 8), :] = jnp.where(sub == 0, jnp.where(even, to_next, to_prev), kept)
    for a in range(3):
        ref, lead = (field_ref, a) if a < 2 else (coef_ref, None)
        if a != 1:
            copies[1 + a // 2].wait()
        for r in range(4):
            near_ref[pl.ds(32 * a + 8 * r, 8), :] = ends(ref, lead, r, live, even)


def pattern_row(pattern_ref, direction, c):
    row = pattern_ref[pl.ds(direction, 1), pl.ds(LANES * c, LANES)]
    return jnp.broadcast_to(row, (8, LANES))


def pack_quarters(total, half, first):
    lane = lanes()
    base = jnp.where(first, 0, 32)
    q = [spin(total[2 * i + half], base + 32 * i) for i in range(4)]
    return jnp.where(
        lane < 64, jnp.where(lane < 32, q[0], q[1]), jnp.where(lane < 96, q[2], q[3])
    )


def ready_kernel(field_ref, coef_ref, kept_ref, ends_ref, gone_ref):
    lane = lanes()
    even = is_even("leaf")
    live, to_prev, to_next = (kept_ref[96 + i, 0].astype(jnp.int32) for i in (1, 2, 3))
    for a in range(3):
        ref, lead = (field_ref, a) if a < 2 else (coef_ref, None)
        for r in range(4):
            ends_ref[pl.ds(32 * a + 8 * r, 8), :] = ends(ref, lead, r, live, jnp.logical_not(even))
        for t in range(TILES):
            x0, x1, x2 = (old_tile(ref, lead, t, c) for c in range(3))
            last = jnp.where(lane >= live - to_next - LANES, x1, x2)
            gone_ref[pl.ds(64 * a + 8 * t, 8), :] = jnp.where(
                lane < SPILL, spin(x0, SPILL - to_prev), spin(last, SPILL + to_next - live)
            )


def place_part(sources, counts, gone_ref, near_ref, own_ref, band_ref):
    lane = lanes()
    even = is_even("leaf")
    live, to_prev, to_next, from_prev, from_next = counts
    drift = to_prev - from_prev
    tail = from_prev + live - to_prev - to_next - LANES
    spill = (lane >= SPILL - to_prev) & (lane < SPILL + to_next)
    near_low = jnp.where(even, SPILL, 0)
    near_lanes = (lane >= near_low) & (lane < near_low + SPILL)
    arrive_by = jnp.where(even, tail, from_prev - 64)
    band_by = jnp.where(even, SPILL + to_next - from_next, from_prev - to_prev - SPILL)
    for out, (a, ref, lead) in enumerate(sources):
        for t in range(TILES):
            h = 64 * (t // 4)
            near = near_ref[pl.ds(32 * a + 8 * (t % 4), 8), :]
            x0, x1, x2 = (old_tile(ref, lead, t, c) for c in range(3))
            r0, r1, r2 = spin(x0, -drift), spin(x1, -drift), spin(x2, -drift)
            own0 = jnp.where(lane < LANES - drift, r0, r1)
            own1 = jnp.where(lane < -drift, r0, jnp.where(lane < LANES - drift, r1, r2))
            arrived = spin(near, arrive_by - h)
            own0 = jnp.where(lane < from_prev, jnp.where(even, 0.0, arrived), own0)
            own1 = jnp.where(lane >= tail, jnp.where(even, arrived, 0.0), own1)
            gone = gone_ref[pl.ds(64 * a + 8 * t, 8), :]
            band = jnp.where(spill, gone, jnp.where(near_lanes, spin(near, band_by - h), 0.0))
            own_ref[pl.ds(128 * out + 8 * t, 8), :] = own0
            own_ref[pl.ds(128 * out + 64 + 8 * t, 8), :] = own1
            band_ref[pl.ds(64 * out + 8 * t, 8), :] = band
    return near_lanes


def coef_kernel(coef_ref, kept_ref, gone_ref, near_ref, own_ref, band_ref):
    counts = [kept_ref[96 + i, 0].astype(jnp.int32) for i in range(1, 6)]
    place_part([(2, coef_ref, None)], counts, gone_ref, near_ref, own_ref, band_ref)


def far_kernel(
    field_ref, pattern_ref, kept_ref, ends_ref, gone_ref, near_ref, far_ref, own_ref, band_ref
):
    lane, sub = lanes(), rows()
    even = is_even("leaf")
    live, to_prev, to_next = (kept_ref[96 + i, 0].astype(jnp.int32) for i in (1, 2, 3))
    from_near = near_ref[96, 0].astype(jnp.int32)
    from_far = BRICKS_DEV - (live - to_prev - to_next) - from_near
    from_prev, from_next = jnp.where(even, from_far, from_near), jnp.where(even, from_near, from_far)
    handed = jnp.where(even, to_prev, to_next)
    counts = jnp.zeros((8, LANES), jnp.int32)
    for i, value in enumerate((handed, live, to_prev, to_next, from_prev, from_next)):
        counts = jnp.where(sub == i, value, counts)
    far_ref[pl.ds(96, 8), :] = counts.astype(F32)
    for r in range(12):
        far_ref[pl.ds(8 * r, 8), :] = ends_ref[pl.ds(8 * r, 8), :]
    near_lanes = place_part(
        [(a, field_ref, a) for a in range(2)],
        (live, to_prev, to_next, from_prev, from_next),
        gone_ref, near_ref, own_ref, band_ref,
    )
    far_rows = [
        jnp.where(even, pattern_row(pattern_ref, d, 0), pattern_row(pattern_ref, d, 1)) for d in range(6)
    ]
    sent = jnp.zeros((8, LANES), jnp.int32)
    for d in range(6):
        row = spin(far_rows[d], jnp.where(even, 0, 32))
        sent = jnp.where(sub == d, row, sent)
    sent = jnp.where(lane < 32, sent, pltpu.roll(sent, 32, 1))
    far_ref[pl.ds(104, 8), :] = sent.astype(F32)
    kinds = face_indices(far_rows)
    for a in range(2):

        def read(c, t):
            if c < 2:
                return own_ref[pl.ds(128 * a + 64 * c + 8 * t, 8), :]
            return jnp.where(near_lanes, band_ref[pl.ds(64 * a + 8 * t, 8), :], 0.0)

        src = Sources(read)
        here = [jnp.where(even, src.tile[0][t], src.tile[1][t]) for t in range(TILES)]
        turned = [jnp.where(even, src.turned[0][t], src.turned[1][t]) for t in range(TILES)]
        total = neighbour_sum(src, here, turned, kinds)
        for half in range(2):
            far_ref[pl.ds(112 + 16 * a + 8 * half, 8), :] = pack_quarters(total, half, even)


def place_kernel(
    kept_ref, own_ref, band_ref, coef_own, coef_band, far_ref, pack_near, pack_far, coef_out, band_out
):
    lane = lanes()
    even = is_even("leaf")
    even_group = is_even("gy")
    _, live, to_prev, to_next, from_prev, from_next = (
        kept_ref[96 + i, 0].astype(jnp.int32) for i in range(6)
    )
    tail = from_prev + live - to_prev - to_next - LANES
    first = jnp.where(even, from_prev, 0)
    final = jnp.where(even, LANES, tail)
    stays_low = jnp.where(even, 0, SPILL + to_next)
    stays_high = jnp.where(even, SPILL - to_prev, 2 * SPILL)
    stays = (lane >= stays_low) & (lane < stays_high)
    arrive_by = jnp.where(even, from_prev - 64, tail)
    band_by = jnp.where(even, from_prev - to_prev - SPILL, SPILL + to_next - from_next)
    for a in range(3):
        for t in range(TILES):
            h = 64 * (t // 4)
            far = far_ref[pl.ds(32 * a + 8 * (t % 4), 8), :]
            arrived = spin(far, arrive_by - h)
            part, side, b = (own_ref, band_ref, a) if a < 2 else (coef_own, coef_band, 0)
            own0 = jnp.where(lane < first, arrived, part[pl.ds(128 * b + 8 * t, 8), :])
            own1 = jnp.where(lane >= final, arrived, part[pl.ds(128 * b + 64 + 8 * t, 8), :])
            band = jnp.where(stays, spin(far, band_by - h), side[pl.ds(64 * b + 8 * t, 8), :])
            band_out[pl.ds(64 * a + 8 * t, 8), :] = band
            if a < 2:
                for pack in (pack_near, pack_far):
                    pack[pl.ds(128 * a + 8 * t, 8), :] = own0
                    pack[pl.ds(128 * a + 64 + 8 * t, 8), :] = own1
            else:
                coef_out[pl.ds(8 * t, 8), :] = own0
                coef_out[pl.ds(64 + 8 * t, 8), :] = own1
    for r in range(4):
        packed = [
            jnp.where(
                lane < 64,
                band_out[pl.ds(64 * a + 8 * r, 8), :],
                pltpu.roll(band_out[pl.ds(64 * a + 8 * r + 32, 8), :], 64, 1),
            )
            for a in range(2)
        ]
        pack_near[pl.ds(256 + 8 * r, 8), :] = jnp.where(even_group, packed[1], packed[0])
        pack_far[pl.ds(256 + 8 * r, 8), :] = jnp.where(even_group, packed[0], packed[1])


def facing_kernel(pattern_ref, pack_ref, band_ref, sum_near):
    even = is_even("leaf")
    kinds = face_indices(
        [jnp.where(even, pattern_row(pattern_ref, d, 1), pattern_row(pattern_ref, d, 0)) for d in range(6)]
    )
    for a in range(2):
        src = Sources(
            lambda c, t: own(pack_ref, a, c, t) if c < 2 else band_ref[pl.ds(64 * a + 8 * t, 8), :]
        )
        here = [jnp.where(even, src.tile[1][t], src.tile[0][t]) for t in range(TILES)]
        turned = [jnp.where(even, src.turned[1][t], src.turned[0][t]) for t in range(TILES)]
        total = neighbour_sum(src, here, turned, kinds)
        for half in range(2):
            sum_near[pl.ds(16 * a + 8 * half, 8), :] = pack_quarters(total, half, jnp.logical_not(even))


def far_sums(kept_ref, far_ref, pack_ref, band_ref, sum_far):
    lane = lanes()
    even = is_even("leaf")
    to_prev, to_next = (kept_ref[96 + i, 0].astype(jnp.int32) for i in (2, 3))
    shift = jnp.where(even, 480, 224)
    window = [
        jnp.broadcast_to(far_ref[pl.ds(104 + d, 1), :], (8, LANES)).astype(jnp.int32) - shift
        for d in range(6)
    ]
    window = [jnp.where((w >= 0) & (w < 2 * SPILL), w, LANES - 1) for w in window]
    kinds = [(w,) for w in face_rows(window)]
    far_low = jnp.where(even, 0, SPILL)
    far_lanes = (lane >= far_low) & (lane < far_low + SPILL)
    mine = (lane < 2 * SPILL) & jnp.logical_not(far_lanes)
    given = far_lanes & (lane >= SPILL - to_prev) & (lane < SPILL + to_next)
    for a in range(2):

        def meet(_, t):
            facing = spin(jnp.where(even, own(pack_ref, a, 0, t), own(pack_ref, a, 1, t)), 32)
            return jnp.where(given, band_ref[pl.ds(64 * a + 8 * t, 8), :], jnp.where(mine, facing, 0.0))

        joint = Sources(meet, 1)
        total = neighbour_sum(joint, joint.tile[0], joint.turned[0], kinds)
        for t in range(TILES):
            part = far_ref[pl.ds(112 + 16 * a + 8 * (t % 2), 8), :]
            part = spin(part, far_low - 32 * (t // 2))
            sum_far[pl.ds(64 * a + 8 * t, 8), :] = jnp.where(far_lanes, total[t] + part, 0.0)


def own(ref, a, c, t):
    return ref[pl.ds(128 * a + 64 * c + 8 * t, 8), :]


def own_kinds(pattern_ref):
    return [
        face_indices(
            [
                jnp.broadcast_to(pattern_ref[pl.ds(d, 1), pl.ds(LANES * c, LANES)], (8, LANES))
                for d in range(6)
            ]
        )
        for c in range(2)
    ]


def gains(weights, coef):
    spread = weights[0] * coef
    return spread, OMEGA / (6.0 * spread + weights[4])


def bulge(weights, phase):
    return weights[3] * (2.0 * phase - phase * phase * phase)


def own_kernel(
    layers, table, pattern_ref, pack_ref, coef_ref, band_ref, kept_ref, far_ref, half_ref, sum_far
):
    far_sums(kept_ref, far_ref, pack_ref, band_ref, sum_far)
    group = lax.axis_index("gy")
    kinds = own_kinds(pattern_ref)
    weights = [weights_at(table, group, layers, a) for a in range(2)]
    for a in range(2):
        src = Sources(
            lambda c, t: own(pack_ref, a, c, t) if c < 2 else band_ref[pl.ds(64 * a + 8 * t, 8), :]
        )
        for c in range(2):
            total = neighbour_sum(src, src.tile[c], src.turned[c], kinds[c])
            for t in range(TILES):
                now = src.tile[c][t]
                spread, gain = gains(weights[a], coef_ref[pl.ds(64 * c + 8 * t, 8), :])
                push = spread * total[t] + weights[a][2 - a] * own(pack_ref, 1 - a, c, t)
                if a == 0:
                    push = push + bulge(weights[0], now)
                half_ref[pl.ds(128 * a + 64 * c + 8 * t, 8), :] = (1.0 - OMEGA) * now + gain * push


def at(base, offset):
    return pl.ds(pl.multiple_of(base + offset, 8), 8)


def side_weights(layers, table, upper):
    group = lax.axis_index("gy")
    lower, first, second, over = (weights_at(table, group, layers, o) for o in (-1, 0, 1, 2))
    own_w = [jnp.where(upper, u, v) for u, v in zip(second, first)]
    side_w = [jnp.where(upper, u, v) for u, v in zip(over, lower)]

    def link(weights, outward):
        return jnp.where(upper == outward, weights[2], weights[1])

    return own_w, side_w, link(own_w, True), link(own_w, False), link(side_w, False), link(side_w, True)


def side_kernel(
    layers, table, near_side,
    pattern_ref, pack_ref, coef_ref, band_ref, half_ref, side_ref, once_ref, next_ref, edge_ref,
):
    lane = lanes()
    upper = is_even("gy") if near_side else jnp.logical_not(is_even("gy"))
    a = jnp.where(upper, 1, 0)
    kinds = own_kinds(pattern_ref)
    w_own, w_side, own_to_side, own_to_other, side_to_own, side_to_next = side_weights(
        layers, table, upper
    )
    here, there = 128 * a, 128 * (1 - a)

    def side_band(t):
        tile = side_ref[pl.ds(256 + 8 * (t % 4), 8), :]
        return jnp.where(lane < 64, pltpu.roll(tile, 64, 1) if t >= 4 else tile, 0.0)

    for c in range(2):
        for t in range(TILES):
            k = 64 * c + 8 * t
            _, gain = gains(w_own, coef_ref[pl.ds(k, 8), :])
            once_ref[pl.ds(k, 8), :] = (
                half_ref[at(here, k), :] + gain * own_to_side * side_ref[at(there, k), :]
            )
    for t in range(TILES):
        now = band_ref[at(64 * a, 8 * t), :]
        _, gain = gains(w_own, band_ref[pl.ds(128 + 8 * t, 8), :])
        push = own_to_side * side_band(t) + bulge(w_own, now)
        push = push + own_to_other * band_ref[at(64 * (1 - a), 8 * t), :]
        edge_ref[pl.ds(8 * t, 8), :] = (1.0 - OMEGA) * now + gain * push

    src = Sources(lambda c, t: side_ref[at(there, 64 * c + 8 * t), :] if c < 2 else side_band(t))
    for c in range(2):
        total = neighbour_sum(src, src.tile[c], src.turned[c], kinds[c])
        for t in range(TILES):
            k = 64 * c + 8 * t
            spread, gain = gains(w_side, coef_ref[pl.ds(k, 8), :])
            push = spread * total[t] + side_to_own * pack_ref[at(here, k), :]
            push = push + side_to_next * side_ref[at(here, k), :]
            next_ref[pl.ds(k, 8), :] = (1.0 - OMEGA) * src.tile[c][t] + gain * push


def final_kernel(
    layers, table,
    pattern_ref, pack_ref, coef_ref, band_ref, half_ref, side_ref, sum_near, sum_far,
    near_once, near_next, near_edge,
    out_hbm, far_once, far_next, far_edge, edge_ref, left_ref, right_ref, sems,
):
    side_kernel(
        layers, table, False,
        pattern_ref, pack_ref, coef_ref, band_ref, half_ref, side_ref, far_once, far_next, far_edge,
    )
    even = is_even("leaf")
    unpack_by = jnp.where(even, SPILL, 0)
    lane = lanes()
    near_lanes = (lane >= unpack_by) & (lane < unpack_by + SPILL)
    kinds = own_kinds(pattern_ref)
    sides = []
    for side, (once, next, edge) in enumerate(
        ((near_once, near_next, near_edge), (far_once, far_next, far_edge))
    ):
        upper = jnp.logical_not(is_even("gy")) if side else is_even("gy")
        a = jnp.where(upper, 1, 0)
        w_own, _, own_to_side, own_to_other, _, _ = side_weights(layers, table, upper)
        for t in range(TILES):
            spread, gain = gains(w_own, band_ref[pl.ds(128 + 8 * t, 8), :])
            near = spin(sum_near[at(16 * a, 8 * (t % 2)), :], unpack_by - 32 * (t // 2))
            total = jnp.where(near_lanes, near, sum_far[at(64 * a, 8 * t), :])
            k = 64 * side + 8 * t
            edge_ref[pl.ds(k, 8), :] = edge[pl.ds(8 * t, 8), :] + gain * (spread * total)

        def read(c, t):
            return once[pl.ds(64 * c + 8 * t, 8), :] if c < 2 else edge_ref[pl.ds(64 * side + 8 * t, 8), :]

        sides.append((a, w_own, own_to_side, own_to_other, Sources(read), next))
    copies = []
    for c, buffer in enumerate((left_ref, right_ref)):
        for side, (a, w_own, own_to_side, own_to_other, src, next) in enumerate(sides):
            other = sides[1 - side][4]
            total = neighbour_sum(src, src.tile[c], src.turned[c], kinds[c])
            for t in range(TILES):
                k = 64 * c + 8 * t
                spread, gain = gains(w_own, coef_ref[pl.ds(k, 8), :])
                push = spread * total[t] + own_to_side * next[pl.ds(k, 8), :]
                push = push + own_to_other * other.tile[c][t]
                push = push + bulge(w_own, pack_ref[at(128 * a, k), :])
                buffer[side, pl.ds(8 * t, 8), :] = (1.0 - OMEGA) * src.tile[c][t] + gain * push
            target = out_hbm.at[a, :, pl.ds(LANES * c, LANES)]
            copies.append(pltpu.make_async_copy(buffer.at[side], target, sems.at[2 * c + side]))
            copies[-1].start()
    for copy in copies:
        copy.wait()


def swap(block, axis, first):
    route = []
    for i in range(first, lax.axis_size(axis) - 1, 2):
        route += [(i, i + 1), (i + 1, i)]
    return lax.ppermute(block, axis, route)


def call(kernel, shapes, spaces, *operands, scratch=(), out_space=pltpu.VMEM):
    vmem = pltpu.VMEM
    space = {"h": pltpu.HBM, "v": vmem, "s": pltpu.SMEM}
    moved = sum(4 * int(np.prod(o.shape)) for o in operands)
    return pl.pallas_call(
        kernel,
        out_shape=[jax.ShapeDtypeStruct(s, F32) for s in shapes],
        in_specs=[pl.BlockSpec(memory_space=space[s]) for s in spaces],
        out_specs=[pl.BlockSpec(memory_space=out_space) for _ in shapes],
        scratch_shapes=list(scratch),
        compiler_params=pltpu.CompilerParams(vmem_limit_bytes=16 * 2**20),
        cost_estimate=pl.CostEstimate(flops=0, bytes_accessed=moved, transcendentals=0),
    )(*operands)


def local(table, field_old, coef_old, owner, counts, pattern):
    layers = field_old.shape[0]
    stored = [pltpu.with_memory_space_constraint(x, pltpu.HBM) for x in (field_old, coef_old, owner)]
    to_near, field, coef = call(
        near_kernel,
        [(104, LANES), field_old.shape, coef_old.shape],
        "hhhs",
        *stored, counts,
        scratch=[pltpu.VMEM((OLD_SLOTS,), jnp.int32), pltpu.SemaphoreType.DMA((3,))],
    )
    from_near = swap(to_near, "leaf", 0)
    ends_far, gone = call(
        ready_kernel, [(96, LANES), (192, LANES)], "vvv", field, coef, to_near
    )
    to_far, own_part, band_part = call(
        far_kernel,
        [(144, LANES), (256, LANES), (128, LANES)],
        "vvvvvv",
        field, pattern, to_near, ends_far, gone, from_near,
    )
    from_far = swap(to_far, "leaf", 1)
    coef_part, coef_side = call(
        coef_kernel, [(128, LANES), (64, LANES)], "vvvv", coef, to_far, gone, from_near
    )
    pack, pack_far, coef, band = call(
        place_kernel,
        [(288, LANES), (288, LANES), (128, LANES), (192, LANES)],
        "vvvvvv",
        to_far, own_part, band_part, coef_part, coef_side, from_far,
    )
    side_near = swap(pack, "gy", 0)
    side_far = swap(pack_far, "gy", 1)
    (sum_near,) = call(facing_kernel, [(32, LANES)], "vvv", pattern, pack, band)
    sum_near = swap(sum_near, "leaf", 0)
    half, sum_far = call(
        functools.partial(own_kernel, layers, table),
        [(256, LANES), (128, LANES)],
        "vvvvvv",
        pattern, pack, coef, band, to_far, from_far,
    )
    facing = call(
        functools.partial(side_kernel, layers, table, True),
        [(128, LANES), (128, LANES), (64, LANES)],
        "vvvvvv",
        pattern, pack, coef, band, half, side_near,
    )
    (out,) = call(
        functools.partial(final_kernel, layers, table),
        [(layers, 64, BRICKS_DEV)],
        "v" * 11,
        pattern, pack, coef, band, half, side_far, sum_near, sum_far, *facing,
        out_space=pltpu.HBM,
        scratch=[pltpu.VMEM((rows, LANES), F32) for rows in (128, 128, 64, 128)]
        + [pltpu.VMEM((layers, 64, LANES), F32)] * 2
        + [pltpu.SemaphoreType.DMA((4,))],
    )
    return out


def solution(mesh):
    layers = Y // mesh.shape["gy"]
    return jax.shard_map(
        functools.partial(local, weight_table(layers)),
        mesh=mesh,
        in_specs=(P("gy", None, "leaf"), P(None, "leaf"), P("leaf"), P("leaf"), P(None, "leaf")),
        out_specs=P("gy", None, "leaf"),
        check_vma=False,
    )
```
